32 devices in a mesh: row: 4 (over z), col: 8 (over y, x, core).
Axes of the slice: x: 2, y: 2, z: 4, core: 2. Of those that a mesh axis runs over, the one named last changes fastest.
Arguments:
- hamiltonian: float32 [3072, 3072], P('row', 'col'), may hold values from -40 to 40, as said below
- panel: float32 [3072, 256], P('row'), may hold values from -180 to 180
Outputs:
- updated: float32 [3072, 3072], P('row', 'col')
- band_block: float32 [256, 256], replicated
The draws below stay inside these ranges and needn't reach their ends.
Inputs may be any that keep to these rules, and one draw needn't show every extreme that they name: hamiltonian is exactly symmetric.
All inputs are finite; a program needn't handle non-finite values.
Results may differ from the reference program's by a relative error of at most 0.0003.
Values sent between devices are 32-bit elements; how exact they have to be, the bound alone decides.
No kernel may reach another device: no remote copies, remote signals or barrier semaphores. Data moves between devices by JAX's collectives and lax.ppermute only.
A program may use at most 64 MiB of HBM per device.

```python
import jax
import jax.numpy as jnp
from jax import lax

NB = 256
ORDER = 3072


def draw_hamiltonian(key, part):
    key = jax.random.fold_in(key, 11)
    key_vals = jax.random.fold_in(key, 0)
    raw = jnp.clip(jax.random.normal(key_vals, (ORDER, ORDER), jnp.float32), -6.0, 6.0)
    return (raw + raw.T) * 0.7071


def draw_panel(key, part):
    key = jax.random.fold_in(key, 23)
    key_vals = jax.random.fold_in(key, 0)
    key_cols = jax.random.fold_in(key, 1)
    key_common = jax.random.fold_in(key, 3)
    col_scale = jnp.exp(jax.random.uniform(key_cols, (NB,), jnp.float32, 0.0, 2.302))
    raw = jnp.clip(jax.random.normal(key_vals, (ORDER, NB), jnp.float32), -6.0, 6.0)
    common = jnp.clip(jax.random.normal(key_common, (ORDER, 1), jnp.float32), -6.0, 6.0)
    return (common + 0.008 * raw) * col_scale[None, :]


def setup_inputs(seed: int = 0) -> dict:
    arg_keys = jax.random.split(jax.random.key(seed), 3)
    return {
        "hamiltonian": draw_hamiltonian(jax.random.fold_in(arg_keys[2], 71), 0),
        "panel": draw_panel(jax.random.fold_in(arg_keys[2], 71), 0),
    }


def mult(left, right):
    return jnp.dot(left.astype(jnp.float32), right.astype(jnp.float32), precision=lax.Precision.HIGHEST, preferred_element_type=jnp.float32)

def reference(hamiltonian, panel):
    first_low = jnp.linalg.cholesky(mult(panel.T, panel))
    half = jax.scipy.linalg.solve_triangular(first_low, panel.T, lower=True).T
    second_low = jnp.linalg.cholesky(mult(half.T, half))
    ortho = jax.scipy.linalg.solve_triangular(second_low, half.T, lower=True).T
    ident = jnp.eye(NB, dtype=jnp.float32)
    lead = ortho[:NB] + ident
    reflectors = jnp.concatenate([lead, ortho[NB:]], axis=0)
    factor = jnp.linalg.solve(lead.T, ident)
    products = mult(hamiltonian, reflectors)
    images = mult(products, factor)
    coupling = mult(reflectors.T, images)
    correction = images - 0.5 * mult(reflectors, mult(factor.T, coupling))
    updated = hamiltonian - mult(reflectors, correction.T) - mult(correction, reflectors.T)
    band_block = -mult(second_low.T, first_low.T)
    return (updated, band_block)
```

```python
import functools

import jax
import jax.numpy as jnp
from jax import lax
from jax.experimental import pallas as pl
from jax.experimental.pallas import tpu as pltpu
from jax.sharding import PartitionSpec as P

SUB = 8
LANE = 128
BLOCK = 32
HIGHEST = lax.Precision.HIGHEST
HIGH = lax.Precision.HIGH


def mult(left, right, dims=((1,), (0,)), precision=HIGHEST):
    return lax.dot_general(
        left, right, (dims, ((), ())), precision=precision, preferred_element_type=jnp.float32
    )


def chol_kernel(gram_ref, upper_ref, inv_ref, work_ref):
    size = gram_ref.shape[0]
    tiles = size // LANE
    groups = BLOCK // SUB
    lanes = lax.broadcasted_iota(jnp.int32, (SUB, LANE), 1)
    work_ref[...] = gram_ref[...]

    def spread(row):
        return jnp.broadcast_to(row, (SUB, LANE))

    for first in range(0, size, BLOCK):
        rows = [
            [
                work_ref[first + SUB * g : first + SUB * (g + 1), LANE * t : LANE * (t + 1)]
                for t in range(tiles)
            ]
            for g in range(groups)
        ]
        for g in range(groups):
            col = first + SUB * g
            home, low = divmod(col, LANE)
            in_block = (lanes >= low) & (lanes < low + SUB)
            flat = [[spread(rows[g][t][k : k + 1, :]) for t in range(tiles)] for k in range(SUB)]
            diag = [
                [spread(flat[k][home][:, low + i : low + i + 1]) for i in range(k + 1)]
                for k in range(SUB)
            ]
            unit = [jnp.where(lanes == low + k, 1.0, 0.0) for k in range(SUB)]
            later = range(g + 1, groups)
            cols = {
                q: [spread(rows[q][home][:, low + i : low + i + 1]) for i in range(SUB)]
                for q in later
            }
            for q in later:
                rows[q][home] = jnp.where(in_block, 0.0, rows[q][home])
            for i in range(SUB):
                recip = 1.0 / diag[i][i]
                steps = [None] * SUB
                for k in range(i + 1, SUB):
                    steps[k] = diag[k][i] * recip
                for k in range(i + 1, SUB):
                    for j in range(i + 1, k + 1):
                        diag[k][j] = diag[k][j] - steps[k] * diag[j][i]
                for k in range(i + 1, SUB):
                    for t in range(tiles):
                        flat[k][t] = flat[k][t] - steps[k] * flat[i][t]
                    unit[k] = unit[k] - steps[k] * unit[i]
                for q in later:
                    step = cols[q][i] * recip
                    for j in range(i + 1, SUB):
                        cols[q][j] = cols[q][j] - step * diag[j][i]
                    for t in range(tiles):
                        source = flat[i][t]
                        if t == home:
                            source = jnp.where(in_block, unit[i], source)
                        rows[q][t] = rows[q][t] - step * source
            for k in range(SUB):
                scale = lax.rsqrt(diag[k][k])
                for t in range(tiles):
                    scaled = flat[k][t] * scale
                    if t < home:
                        up, inv = jnp.zeros_like(scaled), scaled
                    elif t > home:
                        up, inv = scaled, jnp.zeros_like(scaled)
                    else:
                        up = jnp.where(lanes >= low + k, scaled, 0.0)
                        inv = jnp.where(in_block, unit[k] * scale, scaled)
                        inv = jnp.where(lanes < low + SUB, inv, 0.0)
                    upper_ref[col + k : col + k + 1, LANE * t : LANE * (t + 1)] = up[0:1]
                    inv_ref[col + k : col + k + 1, LANE * t : LANE * (t + 1)] = inv[0:1]
        rest = first + BLOCK
        if rest == size:
            break
        start = rest // LANE * LANE
        left = upper_ref[first:rest, start:size]
        wide = lax.broadcasted_iota(jnp.int32, (BLOCK, size), 1)
        right = jnp.where(wide < rest, inv_ref[first:rest, :], upper_ref[first:rest, :])
        change = mult(left, right, ((0,), (0,)))
        below = lax.broadcasted_iota(jnp.int32, (size - rest, size), 1)
        old = jnp.where((below >= first) & (below < rest), 0.0, work_ref[rest:size, :])
        work_ref[rest:size, :] = old - change[rest - start :, :]


def cholesky(gram):
    size = gram.shape[0]
    shape = jax.ShapeDtypeStruct((size, size), jnp.float32)
    return pl.pallas_call(
        chol_kernel,
        out_shape=(shape, shape),
        scratch_shapes=[pltpu.VMEM((size, size), jnp.float32)],
        compiler_params=pltpu.CompilerParams(vmem_limit_bytes=32 * 2**20),
        name="cholesky_inverse",
    )(gram)


def inverse_kernel(mat_ref, out_ref):
    size = mat_ref.shape[0]
    row = lax.broadcasted_iota(jnp.int32, (size, size), 0)
    col = lax.broadcasted_iota(jnp.int32, (size, size), 1)
    ident = jnp.where(row == col, 1.0, 0.0)
    mat = mat_ref[...]

    def residual(guess):
        return ident - mult(mat, guess)

    def step(state):
        count, guess, rest, _ = state
        guess = guess + mult(guess, rest)
        rest = residual(guess)
        return count + 1, guess, rest, jnp.max(jnp.abs(rest))

    def more(state):
        count, _, _, worst = state
        return (worst > 3e-6) & (count < 40)

    guess = 0.5 * ident
    rest = ident - 0.5 * mat
    for _ in range(4):
        guess = guess + mult(guess, rest)
        rest = mult(rest, rest)
    guess = guess + mult(guess, rest)
    rest = residual(guess)
    state = (jnp.int32(0), guess, rest, jnp.max(jnp.abs(rest)))
    out_ref[...] = lax.while_loop(more, step, state)[1]


def inverse(mat):
    return pl.pallas_call(
        inverse_kernel,
        out_shape=jax.ShapeDtypeStruct(mat.shape, jnp.float32),
        compiler_params=pltpu.CompilerParams(vmem_limit_bytes=32 * 2**20),
        name="wy_inverse",
    )(mat)


def pair_sum(value, axis, size):
    terms = [value]
    for hop in range(1, size):
        terms.append(lax.ppermute(value, axis, [(i, i ^ hop) for i in range(size)]))
    while len(terms) > 1:
        terms = [terms[i] + terms[i + 1] for i in range(0, len(terms), 2)]
    return terms[0]


def scatter_sum(value, axis, size):
    place = lax.axis_index(axis)
    piece = value.shape[0] // size
    terms = []
    for hop in range(size):
        part = lax.dynamic_slice_in_dim(value, (place ^ hop) * piece, piece, 0)
        if hop:
            part = lax.ppermute(part, axis, [(i, i ^ hop) for i in range(size)])
        terms.append(part)
    while len(terms) > 1:
        terms = [terms[i] + terms[i + 1] for i in range(0, len(terms), 2)]
    return terms[0]


def swap_gather(piece, axis, size):
    place = lax.axis_index(axis)
    whole = jnp.zeros((size * piece.shape[0], piece.shape[1]), piece.dtype)
    for hop in range(size):
        part = piece
        if hop:
            part = lax.ppermute(piece, axis, [(i, i ^ hop) for i in range(size)])
        whole = lax.dynamic_update_slice_in_dim(whole, part, (place ^ hop) * piece.shape[0], 0)
    return whole


def gather_cols(piece, size):
    return lax.all_to_all(jnp.concatenate([piece] * size, axis=0), "col", 0, 0, tiled=True)


def spread_rows(value, owners, rows, cols):
    row_place = lax.axis_index("row")
    col_place = lax.axis_index("col")
    owner = jnp.asarray(owners, jnp.int32)[col_place]
    value = jnp.where(row_place == owner, value, 0.0)
    hop = rows // 2
    done = [0]
    while hop:
        pairs = []
        for c in range(cols):
            for d in done:
                source = owners[c] ^ d
                pairs.append((source * cols + c, (source ^ hop) * cols + c))
        value = value + lax.ppermute(value, ("row", "col"), pairs)
        done = done + [d ^ hop for d in done]
        hop //= 2
    return value


def shards(rows, cols, hamiltonian, panel):
    rows_dev, width = panel.shape
    cols_dev = hamiltonian.shape[1]
    row_place = lax.axis_index("row")
    col_place = lax.axis_index("col")
    strip = width // cols

    def sum_strips(strip_value):
        return gather_cols(pair_sum(strip_value, "row", rows), cols)

    def strip_of(array):
        return lax.dynamic_slice_in_dim(array, col_place * strip, strip, 1)

    gram = sum_strips(mult(strip_of(panel), panel, ((0,), (0,))))

    owners = [c * cols_dev // rows_dev for c in range(cols)]
    owner = col_place * cols_dev // rows_dev
    offset = col_place * cols_dev - owner * rows_dev
    slab = lax.dynamic_slice_in_dim(panel, offset, cols_dev, 0)
    top_strip = lax.dynamic_slice_in_dim(panel[:width], col_place * strip, strip, 0)
    gram, slab, top_strip = lax.optimization_barrier((gram, slab, top_strip))
    panel_cols = spread_rows(slab, owners, rows, cols)
    panel_top = gather_cols(spread_rows(top_strip, [0] * cols, rows, cols), cols)

    first_upper, first_inv = cholesky(gram)
    half = mult(panel, first_inv, ((1,), (1,)))
    half_cols = mult(panel_cols, first_inv, ((1,), (1,)))
    half_top = mult(panel_top, first_inv, ((1,), (1,)))

    gram2 = sum_strips(mult(strip_of(half), half, ((0,), (0,))))
    second_upper, _ = cholesky(gram2)
    band_block = -mult(second_upper, first_upper)

    def with_upper(block, first_row):
        lead_rows = block[:width] + jnp.where(first_row == 0, second_upper, 0.0)
        return jnp.concatenate([lead_rows, block[width:]], axis=0)

    left = with_upper(half, row_place)
    right = with_upper(half_cols, col_place)
    factor = inverse(gram2 + mult(half_top, second_upper, ((0,), (0,))))

    part = mult(hamiltonian, right, precision=HIGH)
    part_cols = mult(hamiltonian, left, ((0,), (0,)), precision=HIGH)
    part_coupling = mult(left, part, ((0,), (0,)), precision=HIGH)
    piece = rows_dev // cols
    packed = jnp.concatenate(
        [part.reshape(cols, piece, width), part_coupling.reshape(cols, strip, width)], axis=1
    ).reshape(cols * (piece + strip), width)
    packed = lax.all_to_all(packed, "col", 0, 0, tiled=True)
    packed = packed.reshape(cols, piece + strip, width).sum(axis=0)
    products = gather_cols(packed[:piece], cols)
    coupling = sum_strips_from(packed[piece:], rows, cols)
    products_cols = swap_gather(scatter_sum(part_cols, "row", rows), "row", rows)

    middle = mult(factor, mult(coupling, factor), ((0,), (0,)), precision=HIGH)
    near = mult(products_cols, factor, precision=HIGH) - mult(right, middle, precision=HIGH)
    far = mult(right, factor, ((1,), (1,)), precision=HIGH)
    updated = hamiltonian - mult(
        jnp.concatenate([left, products], axis=1),
        jnp.concatenate([near, far], axis=1),
        ((1,), (1,)),
        precision=HIGH,
    )
    return (updated, band_block)


def sum_strips_from(strip_value, rows, cols):
    return gather_cols(pair_sum(strip_value, "row", rows), cols)


def solution(mesh):
    in_specs = (P("row", "col"), P("row", None))
    out_specs = (P("row", "col"), P())
    body = functools.partial(shards, mesh.shape["row"], mesh.shape["col"])
    return jax.shard_map(body, mesh=mesh, in_specs=in_specs, out_specs=out_specs, check_vma=False)
```

```python
import functools

import jax
import jax.numpy as jnp
from jax import lax
from jax.experimental import pallas as pl
from jax.experimental.pallas import tpu as pltpu
from jax.sharding import PartitionSpec as P

SUB = 8
LANE = 128
BLOCK = 32
HIGHEST = lax.Precision.HIGHEST
PARAMS = pltpu.CompilerParams(vmem_limit_bytes=48 * 2**20)
PLAIN = ((1,), (0,))
TURNED = ((0,), (0,))
ACROSS = ((1,), (1,))


def mult(left, right, dims=PLAIN):
    return lax.dot_general(
        left, right, (dims, ((), ())), precision=HIGHEST, preferred_element_type=jnp.float32
    )


def split(value):
    high = value.astype(jnp.bfloat16)
    return high, (value - high.astype(jnp.float32)).astype(jnp.bfloat16)


def mult3(left, right, dims=PLAIN):
    def one(a, b):
        return lax.dot_general(a, b, (dims, ((), ())), preferred_element_type=jnp.float32)

    return one(left[0], right[0]) + (one(left[0], right[1]) + one(left[1], right[0]))


def chol_kernel(gram_ref, upper_ref, inv_ref, work_ref):
    size = gram_ref.shape[0]
    tiles = size // LANE
    groups = BLOCK // SUB
    lanes = lax.broadcasted_iota(jnp.int32, (SUB, LANE), 1)
    work_ref[...] = gram_ref[...]

    def spread(row):
        return jnp.broadcast_to(row, (SUB, LANE))

    for first in range(0, size, BLOCK):
        rows = [
            [
                work_ref[first + SUB * g : first + SUB * (g + 1), LANE * t : LANE * (t + 1)]
                for t in range(tiles)
            ]
            for g in range(groups)
        ]
        for g in range(groups):
            col = first + SUB * g
            home, low = divmod(col, LANE)
            in_block = (lanes >= low) & (lanes < low + SUB)
            flat = [[spread(rows[g][t][k : k + 1, :]) for t in range(tiles)] for k in range(SUB)]
            diag = [
                [spread(flat[k][home][:, low + i : low + i + 1]) for i in range(k + 1)]
                for k in range(SUB)
            ]
            unit = [jnp.where(lanes == low + k, 1.0, 0.0) for k in range(SUB)]
            later = range(g + 1, groups)
            cols = {
                q: [spread(rows[q][home][:, low + i : low + i + 1]) for i in range(SUB)]
                for q in later
            }
            for q in later:
                rows[q][home] = jnp.where(in_block, 0.0, rows[q][home])
            for i in range(SUB):
                recip = 1.0 / diag[i][i]
                steps = [None] * SUB
                for k in range(i + 1, SUB):
                    steps[k] = diag[k][i] * recip
                for k in range(i + 1, SUB):
                    for j in range(i + 1, k + 1):
                        diag[k][j] = diag[k][j] - steps[k] * diag[j][i]
                for k in range(i + 1, SUB):
                    for t in range(tiles):
                        flat[k][t] = flat[k][t] - steps[k] * flat[i][t]
                    unit[k] = unit[k] - steps[k] * unit[i]
                for q in later:
                    step = cols[q][i] * recip
                    for j in range(i + 1, SUB):
                        cols[q][j] = cols[q][j] - step * diag[j][i]
                    for t in range(tiles):
                        source = flat[i][t]
                        if t == home:
                            source = jnp.where(in_block, unit[i], source)
                        rows[q][t] = rows[q][t] - step * source
            for k in range(SUB):
                scale = lax.rsqrt(diag[k][k])
                for t in range(tiles):
                    scaled = flat[k][t] * scale
                    if t < home:
                        up, inv = jnp.zeros_like(scaled), scaled
                    elif t > home:
                        up, inv = scaled, jnp.zeros_like(scaled)
                    else:
                        up = jnp.where(lanes >= low + k, scaled, 0.0)
                        inv = jnp.where(in_block, unit[k] * scale, scaled)
                        inv = jnp.where(lanes < low + SUB, inv, 0.0)
                    upper_ref[col + k : col + k + 1, LANE * t : LANE * (t + 1)] = up[0:1]
                    inv_ref[col + k : col + k + 1, LANE * t : LANE * (t + 1)] = inv[0:1]
        rest = first + BLOCK
        if rest == size:
            break
        start = rest // LANE * LANE
        left = upper_ref[first:rest, start:size]
        wide = lax.broadcasted_iota(jnp.int32, (BLOCK, size), 1)
        right = jnp.where(wide < rest, inv_ref[first:rest, :], upper_ref[first:rest, :])
        change = mult(left, right, ((0,), (0,)))
        below = lax.broadcasted_iota(jnp.int32, (size - rest, size), 1)
        old = jnp.where((below >= first) & (below < rest), 0.0, work_ref[rest:size, :])
        work_ref[rest:size, :] = old - change[rest - start :, :]


def estimate(micros):
    return pl.CostEstimate(flops=int(micros * 1e9), bytes_accessed=int(micros * 3e6), transcendentals=0)


def square(size):
    return jax.ShapeDtypeStruct((size, size), jnp.float32)


def cholesky(gram):
    size = gram.shape[0]
    return pl.pallas_call(
        chol_kernel,
        out_shape=(square(size), square(size)),
        scratch_shapes=[pltpu.VMEM((size, size), jnp.float32)],
        compiler_params=PARAMS,
        cost_estimate=estimate(10),
        name="cholesky_inverse",
    )(gram)


def grids(size):
    row = lax.broadcasted_iota(jnp.int32, (size, size), 0)
    col = lax.broadcasted_iota(jnp.int32, (size, size), 1)
    return row, col


def near_kernel(gram_ref, first_ref, upper_ref, band_ref, inv_ref, work_ref):
    size = gram_ref.shape[0]
    row, col = grids(size)
    ident = jnp.where(row == col, 1.0, 0.0)
    weight = jnp.where(row > col, 1.0, ident * 0.5)
    gram = gram_ref[...]

    def look(inv):
        upper = mult(inv, gram)
        low = weight * (mult(upper, inv, ACROSS) - ident)
        return upper, low, jnp.max(jnp.abs(low))

    def more(state):
        count, _, _, _, worst = state
        return jnp.logical_not(worst < 1e-4) & (count < 8)

    def step(state):
        count, inv, _, low, _ = state
        turn = mult(low, inv)
        inv = inv - turn + mult(low, turn)
        return (count + 1, inv) + look(inv)

    low = weight * (gram - ident)
    inv = ident - low + mult(low, low)
    state = lax.while_loop(more, step, (jnp.int32(0), inv) + look(inv))
    _, _, upper, low, worst = state
    upper = jnp.where(row <= col, upper + mult(low, upper, TURNED), 0.0)
    upper_ref[...] = upper

    @pl.when(jnp.logical_not(worst < 1e-4))
    def _():
        chol_kernel(gram_ref, upper_ref, inv_ref, work_ref)

    band_ref[...] = -mult(upper_ref[...], first_ref[...])


def near_cholesky(gram, first_upper):
    size = gram.shape[0]
    return pl.pallas_call(
        near_kernel,
        out_shape=(square(size), square(size)),
        scratch_shapes=[pltpu.VMEM((size, size), jnp.float32)] * 2,
        compiler_params=PARAMS,
        cost_estimate=estimate(3),
        name="near_cholesky",
    )(gram, first_upper)


def factor_kernel(gram_ref, top_ref, inv_ref, upper_ref, out_ref):
    size = gram_ref.shape[0]
    row, col = grids(size)
    ident = jnp.where(row == col, 1.0, 0.0)
    half_top = mult(top_ref[...], inv_ref[...], ACROSS)
    mat = gram_ref[...] + mult(half_top, upper_ref[...], TURNED)

    def residual(guess):
        return ident - mult(mat, guess)

    def step(state):
        count, guess, rest, _ = state
        guess = guess + mult(guess, rest)
        rest = residual(guess)
        return count + 1, guess, rest, jnp.max(jnp.abs(rest))

    def more(state):
        count, _, _, worst = state
        return (worst > 3e-6) & (count < 40)

    guess = 0.5 * ident
    rest = ident - 0.5 * mat
    for _ in range(4):
        guess = guess + mult(guess, rest)
        rest = mult(rest, rest)
    guess = guess + mult(guess, rest)
    rest = residual(guess)
    state = (jnp.int32(0), guess, rest, jnp.max(jnp.abs(rest)))
    out_ref[...] = lax.while_loop(more, step, state)[1]


def compact_factor(gram, top, inv, upper):
    return pl.pallas_call(
        factor_kernel,
        out_shape=square(gram.shape[0]),
        compiler_params=PARAMS,
        cost_estimate=estimate(4),
        name="compact_factor",
    )(gram, top, inv, upper)


def products_kernel(
    place_ref, ham_ref, half_ref, near_ref, upper_ref, left_ref, right_ref, packed_ref, cols_ref
):
    width = upper_ref.shape[0]
    cols = packed_ref.shape[0]
    piece = ham_ref.shape[0] // cols
    strip = width // cols
    left_ref[...] = half_ref[...]
    right_ref[...] = near_ref[...]
    for axis, ref in enumerate((left_ref, right_ref)):

        @pl.when(place_ref[axis] == 0)
        def _():
            ref[:width, :] = ref[:width, :] + upper_ref[...]

    ham = split(ham_ref[...])
    left = split(left_ref[...])
    part = mult3(ham, split(right_ref[...]))
    coupling = mult3(left, split(part), TURNED)
    for c in range(cols):
        packed_ref[c, :piece, :] = part[c * piece : (c + 1) * piece]
        packed_ref[c, piece:, :] = coupling[c * strip : (c + 1) * strip]
    cols_ref[...] = mult3(ham, left, TURNED)


def products(place, hamiltonian, half, half_cols, upper, cols):
    rows_dev, cols_dev = hamiltonian.shape
    width = upper.shape[0]
    share = (rows_dev + width) // cols

    def shape(*dims):
        return jax.ShapeDtypeStruct(dims, jnp.float32)

    vmem = pl.BlockSpec(memory_space=pltpu.VMEM)
    return pl.pallas_call(
        products_kernel,
        in_specs=[pl.BlockSpec(memory_space=pltpu.SMEM)] + [vmem] * 4,
        out_shape=(
            shape(rows_dev, width),
            shape(cols_dev, width),
            shape(cols, share, width),
            shape(cols_dev, width),
        ),
        compiler_params=PARAMS,
        cost_estimate=estimate(3),
        name="products",
    )(place, hamiltonian, half, half_cols, upper)


def update_kernel(ham_ref, left_ref, prod_ref, right_ref, near_ref, factor_ref, coupling_ref, out_ref):
    factor = split(factor_ref[...])
    right = split(right_ref[...])
    turn = mult3(split(coupling_ref[...]), factor)
    middle = mult3(factor, split(turn), TURNED)
    near = mult3(split(near_ref[...]), factor) - mult3(right, split(middle))
    far = mult3(right, factor, ACROSS)
    change = mult3(split(left_ref[...]), split(near), ACROSS)
    change = change + mult3(split(prod_ref[...]), split(far), ACROSS)
    out_ref[...] = ham_ref[...] - change


def update(hamiltonian, *operands):
    return pl.pallas_call(
        update_kernel,
        out_shape=jax.ShapeDtypeStruct(hamiltonian.shape, jnp.float32),
        compiler_params=PARAMS,
        cost_estimate=estimate(3),
        name="two_sided_update",
    )(hamiltonian, *operands)


def gather(piece, axis, size):
    copies = jnp.broadcast_to(piece[None], (size,) + piece.shape)
    return lax.all_to_all(copies, axis, 0, 0, tiled=True)


def spread_rows(value, owners, rows, cols):
    row_place = lax.axis_index("row")
    col_place = lax.axis_index("col")
    owner = jnp.asarray(owners, jnp.int32)[col_place]
    value = jnp.where(row_place == owner, value, 0.0)
    hop = rows // 2
    done = [0]
    while hop:
        pairs = []
        for c in range(cols):
            for d in done:
                source = owners[c] ^ d
                pairs.append((source * cols + c, (source ^ hop) * cols + c))
        value = value + lax.ppermute(value, ("row", "col"), pairs)
        done = done + [d ^ hop for d in done]
        hop //= 2
    return value


def shards(rows, cols, hamiltonian, panel):
    rows_dev, width = panel.shape
    cols_dev = hamiltonian.shape[1]
    row_place = lax.axis_index("row")
    col_place = lax.axis_index("col")
    strip = width // cols
    piece = rows_dev // cols

    def strip_of(array):
        return lax.dynamic_slice_in_dim(array, col_place * strip, strip, 1)

    def sum_rows(value):
        return gather(value, "row", rows).sum(axis=0)

    gram_strip = sum_rows(mult(strip_of(panel), panel, TURNED))

    owners = [c * cols_dev // rows_dev for c in range(cols)]
    owner = col_place * cols_dev // rows_dev
    offset = col_place * cols_dev - owner * rows_dev
    slab = lax.dynamic_slice_in_dim(panel, offset, cols_dev, 0)
    top_strip = lax.dynamic_slice_in_dim(panel[:width], col_place * strip, strip, 0)
    gram_strip, slab, top_strip = lax.optimization_barrier((gram_strip, slab, top_strip))
    panel_cols = spread_rows(slab, owners, rows, cols)
    top_strip = spread_rows(top_strip, [0] * cols, rows, cols)

    gram = gather(gram_strip, "col", cols).reshape(width, width)
    first_upper, first_inv = cholesky(gram)
    half = mult(panel, first_inv, ACROSS)
    half_cols = mult(panel_cols, first_inv, ACROSS)

    gram2_strip = sum_rows(mult(strip_of(half), half, TURNED))
    both = gather(jnp.concatenate([gram2_strip, top_strip], axis=0), "col", cols)
    gram2 = both[:, :strip].reshape(width, width)
    panel_top = both[:, strip:].reshape(width, width)
    second_upper, band_block = near_cholesky(gram2, first_upper)

    place = jnp.stack([row_place, col_place]).astype(jnp.int32)
    left, right, packed, part_cols = products(
        place, hamiltonian, half, half_cols, second_upper, cols
    )
    gram2, panel_top, packed = lax.optimization_barrier((gram2, panel_top, packed))
    factor = compact_factor(gram2, panel_top, first_inv, second_upper)
    packed = lax.all_to_all(packed, "col", 0, 0, tiled=True).sum(axis=0)
    part_cols = part_cols.reshape(rows, cols_dev // rows, width)
    cols_piece = lax.all_to_all(part_cols, "row", 0, 0, tiled=True).sum(axis=0)
    product_rows = gather(packed[:piece], "col", cols).reshape(rows_dev, width)
    both = gather(jnp.concatenate([cols_piece, packed[piece:]], axis=0), "row", rows)
    product_cols = both[:, : cols_dev // rows].reshape(cols_dev, width)
    coupling_strip = both[:, cols_dev // rows :].sum(axis=0)
    coupling = gather(coupling_strip, "col", cols).reshape(width, width)
    updated = update(hamiltonian, left, product_rows, right, product_cols, factor, coupling)
    return (updated, band_block)


def solution(mesh):
    in_specs = (P("row", "col"), P("row", None))
    out_specs = (P("row", "col"), P())
    body = functools.partial(shards, mesh.shape["row"], mesh.shape["col"])
    return jax.shard_map(body, mesh=mesh, in_specs=in_specs, out_specs=out_specs, check_vma=False)
```

```python
import functools

import jax
import jax.numpy as jnp
from jax import lax
from jax.experimental import pallas as pl
from jax.experimental.pallas import tpu as pltpu
from jax.sharding import PartitionSpec as P

SUB = 8
LANE = 128
BLOCK = 32
HIGHEST = lax.Precision.HIGHEST
PARAMS = pltpu.CompilerParams(vmem_limit_bytes=48 * 2**20)
PLAIN = ((1,), (0,))
TURNED = ((0,), (0,))
ACROSS = ((1,), (1,))


def mult(left, right, dims=PLAIN):
    return lax.dot_general(
        left, right, (dims, ((), ())), precision=HIGHEST, preferred_element_type=jnp.float32
    )


def split(value):
    high = value.astype(jnp.bfloat16)
    return high, (value - high.astype(jnp.float32)).astype(jnp.bfloat16)


def mult3(left, right, dims=PLAIN):
    def one(a, b):
        return lax.dot_general(a, b, (dims, ((), ())), preferred_element_type=jnp.float32)

    return one(left[0], right[0]) + (one(left[0], right[1]) + one(left[1], right[0]))


def chol_kernel(gram_ref, upper_ref, inv_ref, work_ref):
    size = gram_ref.shape[0]
    tiles = size // LANE
    groups = BLOCK // SUB
    lanes = lax.broadcasted_iota(jnp.int32, (SUB, LANE), 1)
    work_ref[...] = gram_ref[...]

    def spread(row):
        return jnp.broadcast_to(row, (SUB, LANE))

    for first in range(0, size, BLOCK):
        rows = [
            [
                work_ref[first + SUB * g : first + SUB * (g + 1), LANE * t : LANE * (t + 1)]
                for t in range(tiles)
            ]
            for g in range(groups)
        ]
        for g in range(groups):
            col = first + SUB * g
            home, low = divmod(col, LANE)
            in_block = (lanes >= low) & (lanes < low + SUB)
            flat = [[spread(rows[g][t][k : k + 1, :]) for t in range(tiles)] for k in range(SUB)]
            diag = [
                [spread(flat[k][home][:, low + i : low + i + 1]) for i in range(k + 1)]
                for k in range(SUB)
            ]
            unit = [jnp.where(lanes == low + k, 1.0, 0.0) for k in range(SUB)]
            later = range(g + 1, groups)
            cols = {
                q: [spread(rows[q][home][:, low + i : low + i + 1]) for i in range(SUB)]
                for q in later
            }
            for q in later:
                rows[q][home] = jnp.where(in_block, 0.0, rows[q][home])
            for i in range(SUB):
                recip = 1.0 / diag[i][i]
                steps = [None] * SUB
                for k in range(i + 1, SUB):
                    steps[k] = diag[k][i] * recip
                for k in range(i + 1, SUB):
                    for j in range(i + 1, k + 1):
                        diag[k][j] = diag[k][j] - steps[k] * diag[j][i]
                for k in range(i + 1, SUB):
                    for t in range(tiles):
                        flat[k][t] = flat[k][t] - steps[k] * flat[i][t]
                    unit[k] = unit[k] - steps[k] * unit[i]
                for q in later:
                    step = cols[q][i] * recip
                    for j in range(i + 1, SUB):
                        cols[q][j] = cols[q][j] - step * diag[j][i]
                    for t in range(tiles):
                        source = flat[i][t]
                        if t == home:
                            source = jnp.where(in_block, unit[i], source)
                        rows[q][t] = rows[q][t] - step * source
            for k in range(SUB):
                scale = lax.rsqrt(diag[k][k])
                for t in range(tiles):
                    scaled = flat[k][t] * scale
                    if t < home:
                        up, inv = jnp.zeros_like(scaled), scaled
                    elif t > home:
                        up, inv = scaled, jnp.zeros_like(scaled)
                    else:
                        up = jnp.where(lanes >= low + k, scaled, 0.0)
                        inv = jnp.where(in_block, unit[k] * scale, scaled)
                        inv = jnp.where(lanes < low + SUB, inv, 0.0)
                    upper_ref[col + k : col + k + 1, LANE * t : LANE * (t + 1)] = up[0:1]
                    inv_ref[col + k : col + k + 1, LANE * t : LANE * (t + 1)] = inv[0:1]
        rest = first + BLOCK
        if rest == size:
            break
        start = rest // LANE * LANE
        left = upper_ref[first:rest, start:size]
        wide = lax.broadcasted_iota(jnp.int32, (BLOCK, size), 1)
        right = jnp.where(wide < rest, inv_ref[first:rest, :], upper_ref[first:rest, :])
        change = mult(left, right, ((0,), (0,)))
        below = lax.broadcasted_iota(jnp.int32, (size - rest, size), 1)
        old = jnp.where((below >= first) & (below < rest), 0.0, work_ref[rest:size, :])
        work_ref[rest:size, :] = old - change[rest - start :, :]


def estimate(micros):
    return pl.CostEstimate(flops=int(micros * 1e9), bytes_accessed=int(micros * 3e6), transcendentals=0)


def square(size):
    return jax.ShapeDtypeStruct((size, size), jnp.float32)


def cholesky(gram):
    size = gram.shape[0]
    return pl.pallas_call(
        chol_kernel,
        out_shape=(square(size), square(size)),
        scratch_shapes=[pltpu.VMEM((size, size), jnp.float32)],
        compiler_params=PARAMS,
        cost_estimate=estimate(10),
        name="cholesky_inverse",
    )(gram)


def grids(size):
    row = lax.broadcasted_iota(jnp.int32, (size, size), 0)
    col = lax.broadcasted_iota(jnp.int32, (size, size), 1)
    return row, col


def near_kernel(gram_ref, upper_ref, inv_ref, work_ref):
    size = gram_ref.shape[0]
    row, col = grids(size)
    ident = jnp.where(row == col, 1.0, 0.0)
    weight = jnp.where(row > col, 1.0, ident * 0.5)
    gram = split(gram_ref[...])

    def look(inv):
        halves = split(inv)
        upper = mult3(halves, gram)
        low = weight * (mult3(split(upper), halves, ACROSS) - ident)
        return upper, low, jnp.max(jnp.abs(low))

    def more(state):
        count, _, _, _, worst = state
        return jnp.logical_not(worst < 1e-4) & (count < 8)

    def step(state):
        count, inv, _, low, _ = state
        low = split(low)
        turn = mult3(low, split(inv))
        inv = inv - turn + mult3(low, split(turn))
        return (count + 1, inv) + look(inv)

    low = weight * (gram_ref[...] - ident)
    halves = split(low)
    inv = ident - low + mult3(halves, halves)
    state = lax.while_loop(more, step, (jnp.int32(0), inv) + look(inv))
    _, _, upper, low, worst = state
    upper = upper + mult3(split(low), split(upper), TURNED)
    upper_ref[...] = jnp.where(row <= col, upper, 0.0)

    @pl.when(jnp.logical_not(worst < 1e-4))
    def _():
        chol_kernel(gram_ref, upper_ref, inv_ref, work_ref)


def near_cholesky(gram):
    size = gram.shape[0]
    return pl.pallas_call(
        near_kernel,
        out_shape=square(size),
        scratch_shapes=[pltpu.VMEM((size, size), jnp.float32)] * 2,
        compiler_params=PARAMS,
        cost_estimate=estimate(3),
        name="near_cholesky",
    )(gram)


def factor_kernel(gram_ref, top_ref, inv_ref, upper_ref, first_ref, out_ref, band_ref):
    size = gram_ref.shape[0]
    row, col = grids(size)
    ident = jnp.where(row == col, 1.0, 0.0)
    band_ref[...] = -mult(upper_ref[...], first_ref[...])
    half_top = mult(top_ref[...], inv_ref[...], ACROSS)
    mat = gram_ref[...] + mult(half_top, upper_ref[...], TURNED)
    halves = split(mat)

    def residual(guess):
        return ident - mult3(halves, split(guess))

    def step(state):
        count, guess, rest, _ = state
        guess = guess + mult3(split(guess), split(rest))
        rest = residual(guess)
        return count + 1, guess, rest, jnp.max(jnp.abs(rest))

    def more(state):
        count, _, _, worst = state
        return (worst > 2e-5) & (count < 40)

    guess = 0.5 * ident
    rest = ident - 0.5 * mat
    for _ in range(4):
        parts = split(rest)
        guess = guess + mult3(split(guess), parts)
        rest = mult3(parts, parts)
    guess = guess + mult3(split(guess), split(rest))
    rest = residual(guess)
    state = (jnp.int32(0), guess, rest, jnp.max(jnp.abs(rest)))
    out_ref[...] = lax.while_loop(more, step, state)[1]


def compact_factor(gram, top, inv, upper, first):
    return pl.pallas_call(
        factor_kernel,
        out_shape=(square(gram.shape[0]), square(gram.shape[0])),
        compiler_params=PARAMS,
        cost_estimate=estimate(4),
        name="compact_factor",
    )(gram, top, inv, upper, first)


def products_kernel(
    place_ref, ham_ref, wide_ref, half_ref, near_ref, next_ref, upper_ref,
    left_ref, right_ref, packed_ref, *rest_refs
):
    piece_refs, cols_ref = rest_refs[:-1], rest_refs[-1]
    width = upper_ref.shape[0]
    chips = packed_ref.shape[0]
    deep = wide_ref.shape[0]
    piece, strip = deep // chips, width // chips
    share = piece_refs[0].shape[0]
    row_place, col_place = place_ref[0], place_ref[1]
    mine = pl.ds(pl.multiple_of((col_place & 1) * deep, deep), deep)
    row_lead = jnp.where(row_place == 0, 1.0, 0.0)
    left_ref[...] = half_ref[...]
    left_ref[:width, :] = half_ref[:width, :] + row_lead * upper_ref[...]
    col_lead = jnp.where(col_place == 0, 1.0, 0.0)
    right_ref[...] = near_ref[...]
    right_ref[:width, :] = near_ref[:width, :] + col_lead * upper_ref[...]
    next_lead = jnp.where(col_place == 1, 1.0, 0.0)
    beside = jnp.concatenate(
        [next_ref[:width, :] + next_lead * upper_ref[...], next_ref[width:, :]], axis=0
    )
    part = mult3(split(ham_ref[mine, :]), split(right_ref[...]))
    part = part + mult3(split(wide_ref[...]), split(beside))
    coupling = mult3(split(left_ref[mine, :]), split(part), TURNED)
    for c in range(chips):
        packed_ref[c, :piece, :] = part[c * piece : (c + 1) * piece]
        packed_ref[c, piece:, :] = coupling[c * strip : (c + 1) * strip]
    cols_ref[...] = mult3(split(ham_ref[...]), split(left_ref[...]), TURNED)
    for hop, ref in enumerate(piece_refs):
        start = pl.multiple_of((row_place ^ hop) * share, share)
        ref[...] = cols_ref[pl.ds(start, share), :]


def products(place, hamiltonian, wide, half, half_cols, half_next, upper, rows, cols):
    rows_dev, cols_dev = hamiltonian.shape
    width = upper.shape[0]
    chips = cols // 2
    share = (rows_dev // 2 + width) // chips

    def shape(*dims):
        return jax.ShapeDtypeStruct(dims, jnp.float32)

    vmem = pl.BlockSpec(memory_space=pltpu.VMEM)
    out = pl.pallas_call(
        products_kernel,
        in_specs=[pl.BlockSpec(memory_space=pltpu.SMEM)] + [vmem] * 6,
        out_shape=(
            shape(rows_dev, width),
            shape(cols_dev, width),
            shape(chips, share, width),
        )
        + (shape(cols_dev // rows, width),) * rows,
        scratch_shapes=[pltpu.VMEM((cols_dev, width), jnp.float32)],
        compiler_params=PARAMS,
        cost_estimate=estimate(3),
        name="products",
    )(place, hamiltonian, wide, half, half_cols, half_next, upper)
    return out[0], out[1], out[2], out[3:]


def update_kernel(place_ref, ham_ref, left_ref, mine_ref, other_ref, right_ref, factor_ref,
                  coupling_ref, *rest_refs):
    piece_refs, out_ref, near_ref = rest_refs[:-2], rest_refs[-2], rest_refs[-1]
    deep = mine_ref.shape[0]
    share = near_ref.shape[0] // len(piece_refs)
    row_place, core = place_ref[0], place_ref[1] & 1
    for hop, ref in enumerate(piece_refs):
        start = pl.multiple_of((row_place ^ hop) * share, share)
        near_ref[pl.ds(start, share), :] = ref[:share, :]
    factor = split(factor_ref[...])
    right = split(right_ref[...])
    turn = mult3(split(coupling_ref[...]), factor)
    middle = mult3(factor, split(turn), TURNED)
    near = split(mult3(split(near_ref[...]), factor) - mult3(right, split(middle)))
    far = split(mult3(right, factor, ACROSS))
    for place, prod_ref in ((core, mine_ref), (1 - core, other_ref)):
        block = pl.ds(pl.multiple_of(place * deep, deep), deep)
        change = mult3(split(left_ref[block, :]), near, ACROSS)
        change = change + mult3(split(prod_ref[...]), far, ACROSS)
        out_ref[block, :] = ham_ref[block, :] - change


def update(place, hamiltonian, left, mine, other, right, factor, coupling, pieces):
    vmem = pl.BlockSpec(memory_space=pltpu.VMEM)
    return pl.pallas_call(
        update_kernel,
        in_specs=[pl.BlockSpec(memory_space=pltpu.SMEM)] + [vmem] * (7 + len(pieces)),
        out_shape=jax.ShapeDtypeStruct(hamiltonian.shape, jnp.float32),
        scratch_shapes=[pltpu.VMEM(right.shape, jnp.float32)],
        compiler_params=PARAMS,
        cost_estimate=estimate(3),
        name="two_sided_update",
    )(place, hamiltonian, left, mine, other, right, factor, coupling, *pieces)


def gather(piece, axis, size):
    copies = jnp.broadcast_to(piece[None], (size,) + piece.shape)
    return lax.all_to_all(copies, axis, 0, 0, tiled=True)


def hops(values, size):
    got = [values[0]]
    for hop in range(1, size):
        got.append(lax.ppermute(values[hop], "row", [(i, i ^ hop) for i in range(size)]))
    return got


def tree_sum(terms):
    while len(terms) > 1:
        terms = [terms[i] + terms[i + 1] for i in range(0, len(terms), 2)]
    return terms[0]


def spread_rows(value, owners, rows, cols):
    row_place = lax.axis_index("row")
    col_place = lax.axis_index("col")
    owner = jnp.asarray(owners, jnp.int32)[col_place]
    value = jnp.where(row_place == owner, value, 0.0)
    hop = rows // 2
    done = [0]
    while hop:
        pairs = []
        for c in range(cols):
            for d in done:
                source = owners[c] ^ d
                pairs.append((source * cols + c, (source ^ hop) * cols + c))
        value = value + lax.ppermute(value, ("row", "col"), pairs)
        done = done + [d ^ hop for d in done]
        hop //= 2
    return value


def shards(rows, cols, hamiltonian, panel):
    rows_dev, width = panel.shape
    cols_dev = hamiltonian.shape[1]
    row_place = lax.axis_index("row")
    col_place = lax.axis_index("col")
    core = col_place % 2
    chips = cols // 2
    strip = width // cols
    deep = rows_dev // 2
    piece = deep // chips
    share = cols_dev // rows
    pair = [(i, i ^ 1) for i in range(cols)]
    groups = [[2 * k + e for k in range(chips)] for e in range(2)]
    place = jnp.stack([row_place, col_place]).astype(jnp.int32)

    def strip_of(array):
        return lax.dynamic_slice_in_dim(array, col_place * strip, strip, 1)

    wide = lax.dynamic_slice_in_dim(hamiltonian, (1 - core) * deep, deep, 0)
    wide = lax.ppermute(wide, "col", pair)

    gram_strip = mult(strip_of(panel), panel, TURNED)
    top_strip = lax.dynamic_slice_in_dim(panel[:width], col_place * strip, strip, 0)
    top_strip = jnp.where(row_place == 0, top_strip, 0.0)
    strips = gather(jnp.concatenate([gram_strip, top_strip], axis=0), "row", rows).sum(axis=0)

    owners = [c * cols_dev // rows_dev for c in range(cols)]
    owner = col_place * cols_dev // rows_dev
    offset = col_place * cols_dev - owner * rows_dev
    slab = lax.dynamic_slice_in_dim(panel, offset, cols_dev, 0)
    strips, slab = lax.optimization_barrier((strips, slab))
    panel_cols = spread_rows(slab, owners, rows, cols)
    panel_next = lax.ppermute(panel_cols, "col", pair)

    strips = gather(strips, "col", cols)
    gram = strips[:, :strip].reshape(width, width)
    panel_top = strips[:, strip:].reshape(width, width)
    first_upper, first_inv = cholesky(gram)
    half = mult(panel, first_inv, ACROSS)
    half_cols = mult(panel_cols, first_inv, ACROSS)
    half, half_cols = lax.optimization_barrier((half, half_cols))
    half_next = mult(panel_next, first_inv, ACROSS)

    gram2_strip = gather(mult(strip_of(half), half, TURNED), "row", rows).sum(axis=0)
    gram2 = gather(gram2_strip, "col", cols).reshape(width, width)
    second_upper = near_cholesky(gram2)

    left, right, packed, pieces = products(
        place, hamiltonian, wide, half, half_cols, half_next, second_upper, rows, cols
    )
    gram2, panel_top, packed = lax.optimization_barrier((gram2, panel_top, packed))
    factor, band_block = compact_factor(
        gram2, panel_top, first_inv, second_upper, first_upper
    )
    packed = lax.all_to_all(packed, "col", 0, 0, axis_index_groups=groups, tiled=True)
    packed = packed.sum(axis=0)
    near_piece = tree_sum(hops(pieces, rows))
    mine = jnp.broadcast_to(packed[:piece][None], (chips, piece, width))
    mine = lax.all_to_all(mine, "col", 0, 0, axis_index_groups=groups, tiled=True)
    mine = mine.reshape(deep, width)
    other = lax.ppermute(mine, "col", pair)
    both = jnp.concatenate([near_piece, packed[piece:]], axis=0)
    both = hops([both] * rows, rows)
    coupling_strip = tree_sum([value[share:] for value in both])
    coupling = gather(coupling_strip, "col", cols)
    coupling = coupling.reshape(chips, 2, width // chips, width).sum(axis=1)
    coupling = coupling.reshape(width, width)
    updated = update(place, hamiltonian, left, mine, other, right, factor, coupling, both)
    return (updated, band_block)


def solution(mesh):
    in_specs = (P("row", "col"), P("row", None))
    out_specs = (P("row", "col"), P())
    body = functools.partial(shards, mesh.shape["row"], mesh.shape["col"])
    return jax.shard_map(body, mesh=mesh, in_specs=in_specs, out_specs=out_specs, check_vma=False)
```

```python
import functools

import jax
import jax.numpy as jnp
from jax import lax
from jax.experimental import pallas as pl
from jax.experimental.pallas import tpu as pltpu
from jax.sharding import PartitionSpec as P

SUB = 8
LANE = 128
BLOCK = 32
HIGHEST = lax.Precision.HIGHEST
SMALL = pltpu.CompilerParams(vmem_limit_bytes=10 * 2**20)
LARGE = pltpu.CompilerParams(vmem_limit_bytes=24 * 2**20)
VMEM = pl.BlockSpec(memory_space=pltpu.VMEM)
SMEM = pl.BlockSpec(memory_space=pltpu.SMEM)
PLAIN = ((1,), (0,))
TURNED = ((0,), (0,))
ACROSS = ((1,), (1,))


def mult(left, right, dims=PLAIN):
    return lax.dot_general(
        left, right, (dims, ((), ())), precision=HIGHEST, preferred_element_type=jnp.float32
    )


def split(value):
    high = value.astype(jnp.bfloat16)
    return high, (value - high.astype(jnp.float32)).astype(jnp.bfloat16)


def mult3(left, right, dims=PLAIN):
    def one(a, b):
        return lax.dot_general(a, b, (dims, ((), ())), preferred_element_type=jnp.float32)

    return one(left[0], right[0]) + (one(left[0], right[1]) + one(left[1], right[0]))


def chol_kernel(gram_ref, upper_ref, inv_ref, work_ref):
    size = gram_ref.shape[0]
    tiles = size // LANE
    groups = BLOCK // SUB
    lanes = lax.broadcasted_iota(jnp.int32, (SUB, LANE), 1)
    work_ref[...] = gram_ref[...]

    def spread(row):
        return jnp.broadcast_to(row, (SUB, LANE))

    for first in range(0, size, BLOCK):
        rows = [
            [
                work_ref[first + SUB * g : first + SUB * (g + 1), LANE * t : LANE * (t + 1)]
                for t in range(tiles)
            ]
            for g in range(groups)
        ]
        for g in range(groups):
            col = first + SUB * g
            home, low = divmod(col, LANE)
            in_block = (lanes >= low) & (lanes < low + SUB)
            flat = [[spread(rows[g][t][k : k + 1, :]) for t in range(tiles)] for k in range(SUB)]
            diag = [
                [spread(flat[k][home][:, low + i : low + i + 1]) for i in range(k + 1)]
                for k in range(SUB)
            ]
            unit = [jnp.where(lanes == low + k, 1.0, 0.0) for k in range(SUB)]
            later = range(g + 1, groups)
            cols = {
                q: [spread(rows[q][home][:, low + i : low + i + 1]) for i in range(SUB)]
                for q in later
            }
            for q in later:
                rows[q][home] = jnp.where(in_block, 0.0, rows[q][home])
            for i in range(SUB):
                recip = 1.0 / diag[i][i]
                steps = [None] * SUB
                for k in range(i + 1, SUB):
                    steps[k] = diag[k][i] * recip
                for k in range(i + 1, SUB):
                    for j in range(i + 1, k + 1):
                        diag[k][j] = diag[k][j] - steps[k] * diag[j][i]
                for k in range(i + 1, SUB):
                    for t in range(tiles):
                        flat[k][t] = flat[k][t] - steps[k] * flat[i][t]
                    unit[k] = unit[k] - steps[k] * unit[i]
                for q in later:
                    step = cols[q][i] * recip
                    for j in range(i + 1, SUB):
                        cols[q][j] = cols[q][j] - step * diag[j][i]
                    for t in range(tiles):
                        source = flat[i][t]
                        if t == home:
                            source = jnp.where(in_block, unit[i], source)
                        rows[q][t] = rows[q][t] - step * source
            for k in range(SUB):
                scale = lax.rsqrt(diag[k][k])
                for t in range(tiles):
                    scaled = flat[k][t] * scale
                    if t < home:
                        up, inv = jnp.zeros_like(scaled), scaled
                    elif t > home:
                        up, inv = scaled, jnp.zeros_like(scaled)
                    else:
                        up = jnp.where(lanes >= low + k, scaled, 0.0)
                        inv = jnp.where(in_block, unit[k] * scale, scaled)
                        inv = jnp.where(lanes < low + SUB, inv, 0.0)
                    upper_ref[col + k : col + k + 1, LANE * t : LANE * (t + 1)] = up[0:1]
                    inv_ref[col + k : col + k + 1, LANE * t : LANE * (t + 1)] = inv[0:1]
        rest = first + BLOCK
        if rest == size:
            break
        start = rest // LANE * LANE
        left = upper_ref[first:rest, start:size]
        wide = lax.broadcasted_iota(jnp.int32, (BLOCK, size), 1)
        right = jnp.where(wide < rest, inv_ref[first:rest, :], upper_ref[first:rest, :])
        change = mult(left, right, ((0,), (0,)))
        below = lax.broadcasted_iota(jnp.int32, (size - rest, size), 1)
        old = jnp.where((below >= first) & (below < rest), 0.0, work_ref[rest:size, :])
        work_ref[rest:size, :] = old - change[rest - start :, :]


def estimate(micros):
    return pl.CostEstimate(flops=int(micros * 1e9), bytes_accessed=int(micros * 3e6), transcendentals=0)


def square(size):
    return jax.ShapeDtypeStruct((size, size), jnp.float32)


def cholesky(gram):
    size = gram.shape[0]
    return pl.pallas_call(
        chol_kernel,
        out_shape=(square(size), square(size)),
        scratch_shapes=[pltpu.VMEM((size, size), jnp.float32)],
        compiler_params=SMALL,
        cost_estimate=estimate(10),
        name="cholesky_inverse",
    )(gram)


def grids(size):
    row = lax.broadcasted_iota(jnp.int32, (size, size), 0)
    col = lax.broadcasted_iota(jnp.int32, (size, size), 1)
    return row, col


def near_kernel(gram_ref, upper_ref, inv_ref, work_ref):
    size = gram_ref.shape[0]
    row, col = grids(size)
    ident = jnp.where(row == col, 1.0, 0.0)
    weight = jnp.where(row > col, 1.0, ident * 0.5)
    gram = split(gram_ref[...])

    def look(inv):
        halves = split(inv)
        upper = mult3(halves, gram)
        low = weight * (mult3(split(upper), halves, ACROSS) - ident)
        return upper, low, jnp.sum(low * low)

    def more(state):
        count, _, _, _, worst = state
        return jnp.logical_not(worst < 1e-5) & (count < 8)

    def step(state):
        count, inv, _, low, _ = state
        low = split(low)
        turn = mult3(low, split(inv))
        inv = inv - turn + mult3(low, split(turn))
        return (count + 1, inv) + look(inv)

    low = weight * (gram_ref[...] - ident)
    halves = split(low)
    inv = ident - low + mult3(halves, halves)
    state = lax.while_loop(more, step, (jnp.int32(0), inv) + look(inv))
    _, _, upper, low, worst = state
    upper = upper + mult3(split(low), split(upper), TURNED)
    upper_ref[...] = jnp.where(row <= col, upper, 0.0)

    @pl.when(jnp.logical_not(worst < 1e-5))
    def _():
        chol_kernel(gram_ref, upper_ref, inv_ref, work_ref)


def near_cholesky(gram):
    size = gram.shape[0]
    return pl.pallas_call(
        near_kernel,
        out_shape=square(size),
        scratch_shapes=[pltpu.VMEM((size, size), jnp.float32)] * 2,
        compiler_params=SMALL,
        cost_estimate=estimate(3),
        name="near_cholesky",
    )(gram)


def factor_kernel(gram_ref, top_ref, inv_ref, upper_ref, first_ref, out_ref, band_ref):
    size = gram_ref.shape[0]
    row, col = grids(size)
    ident = jnp.where(row == col, 1.0, 0.0)
    band_ref[...] = -mult(upper_ref[...], first_ref[...])
    half_top = mult(top_ref[...], inv_ref[...], ACROSS)
    mat = gram_ref[...] + mult(half_top, upper_ref[...], TURNED)
    halves = split(mat)

    def residual(guess):
        return ident - mult3(halves, split(guess))

    def step(state):
        count, guess, rest, _ = state
        guess = guess + mult3(split(guess), split(rest))
        rest = residual(guess)
        return count + 1, guess, rest, jnp.max(jnp.abs(rest))

    def more(state):
        count, _, _, worst = state
        return (worst > 2e-5) & (count < 40)

    guess = 0.5 * ident
    rest = ident - 0.5 * mat
    for _ in range(4):
        parts = split(rest)
        guess = guess + mult3(split(guess), parts)
        rest = mult3(parts, parts)
    guess = guess + mult3(split(guess), split(rest))
    rest = residual(guess)
    state = (jnp.int32(0), guess, rest, jnp.max(jnp.abs(rest)))
    out_ref[...] = lax.while_loop(more, step, state)[1]


def compact_factor(gram, top, inv, upper, first):
    return pl.pallas_call(
        factor_kernel,
        out_shape=(square(gram.shape[0]), square(gram.shape[0])),
        compiler_params=SMALL,
        cost_estimate=estimate(4),
        name="compact_factor",
    )(gram, top, inv, upper, first)


def products_kernel(
    place_ref, ham_ref, wide_ref, half_ref, near_ref, next_ref, upper_ref,
    left_ref, right_ref, packed_ref, *rest_refs
):
    piece_refs, cols_ref = rest_refs[:-1], rest_refs[-1]
    width = upper_ref.shape[0]
    chips = packed_ref.shape[0]
    deep = wide_ref.shape[0] // 2
    piece, strip = deep // chips, width // chips
    share = piece_refs[0].shape[0]
    row_place, col_place = place_ref[0], place_ref[1]
    mine = pl.ds(pl.multiple_of((col_place & 1) * deep, deep), deep)
    row_lead = jnp.where(row_place == 0, 1.0, 0.0)
    left_ref[...] = half_ref[...]
    left_ref[:width, :] = half_ref[:width, :] + row_lead * upper_ref[...]
    col_lead = jnp.where(col_place == 0, 1.0, 0.0)
    right_ref[...] = near_ref[...]
    right_ref[:width, :] = near_ref[:width, :] + col_lead * upper_ref[...]
    next_lead = jnp.where(col_place == 1, 1.0, 0.0)
    beside = jnp.concatenate(
        [next_ref[:width, :] + next_lead * upper_ref[...], next_ref[width:, :]], axis=0
    )
    part = mult3(split(ham_ref[mine, :]), split(right_ref[...]))
    part = part + mult3(split(wide_ref[mine, :]), split(beside))
    coupling = mult3(split(left_ref[mine, :]), split(part), TURNED)
    for c in range(chips):
        packed_ref[c, :piece, :] = part[c * piece : (c + 1) * piece]
        packed_ref[c, piece:, :] = coupling[c * strip : (c + 1) * strip]
    cols_ref[...] = mult3(split(ham_ref[...]), split(left_ref[...]), TURNED)
    for hop, ref in enumerate(piece_refs):
        start = pl.multiple_of((row_place ^ hop) * share, share)
        ref[...] = cols_ref[pl.ds(start, share), :]


def products(place, hamiltonian, wide, half, half_cols, half_next, upper, rows, cols):
    rows_dev, cols_dev = hamiltonian.shape
    width = upper.shape[0]
    chips = cols // 2
    share = (rows_dev // 2 + width) // chips
    out = pl.pallas_call(
        products_kernel,
        in_specs=[SMEM] + [VMEM] * 6,
        out_shape=(
            array(rows_dev, width),
            array(cols_dev, width),
            array(chips, share, width),
        )
        + (array(cols_dev // rows, width),) * rows,
        scratch_shapes=[pltpu.VMEM((cols_dev, width), jnp.float32)],
        compiler_params=LARGE,
        cost_estimate=estimate(4),
        name="products",
    )(place, hamiltonian, wide, half, half_cols, half_next, upper)
    return out[0], out[1], out[2], out[3:]


def array(*dims):
    return jax.ShapeDtypeStruct(dims, jnp.float32)


def gram_kernel(place_ref, panel_ref, out_ref, gram_ref):
    strip = out_ref.shape[1] // 2
    mine = pl.ds(pl.multiple_of(place_ref[1] * strip, strip), strip)
    gram_ref[...] = mult(panel_ref[...], panel_ref[...], TURNED)
    top = panel_ref[mine, :] * jnp.where(place_ref[0] == 0, 1.0, 0.0)
    for r in range(out_ref.shape[0]):
        out_ref[r, :strip, :] = gram_ref[mine, :]
        out_ref[r, strip:, :] = top


def gram_strips(place, panel, rows, cols):
    width = panel.shape[1]
    return pl.pallas_call(
        gram_kernel,
        in_specs=[SMEM, VMEM],
        out_shape=array(rows, 2 * width // cols, width),
        scratch_shapes=[pltpu.VMEM((width, width), jnp.float32)],
        compiler_params=LARGE,
        cost_estimate=estimate(2),
        name="gram_strips",
    )(place, panel)


def half_kernel(place_ref, panel_ref, slab_ref, got_ref, inv_ref, half_ref, cols_ref, out_ref,
                gram_ref):
    strip = out_ref.shape[1]
    mine = pl.ds(pl.multiple_of(place_ref[1] * strip, strip), strip)
    half = mult(panel_ref[...], inv_ref[...], ACROSS)
    half_ref[...] = half
    cols_ref[...] = mult(slab_ref[...] + got_ref[...], inv_ref[...], ACROSS)
    parts = split(half)
    gram_ref[...] = mult3(parts, parts, TURNED)
    for r in range(out_ref.shape[0]):
        out_ref[r] = gram_ref[mine, :]


def half_stage(place, panel, slab, got, inv, rows, cols):
    width = panel.shape[1]
    return pl.pallas_call(
        half_kernel,
        in_specs=[SMEM] + [VMEM] * 4,
        out_shape=(
            array(*panel.shape),
            array(*slab.shape),
            array(rows, width // cols, width),
        ),
        scratch_shapes=[pltpu.VMEM((width, width), jnp.float32)],
        compiler_params=LARGE,
        cost_estimate=estimate(3),
        name="half_stage",
    )(place, panel, slab, got, inv)


def base_kernel(place_ref, ham_ref, left_ref, mine_ref, other_ref, right_ref, factor_ref,
                *rest_refs):
    piece_refs, out_ref, near_ref = rest_refs[:-2], rest_refs[-2], rest_refs[-1]
    deep = mine_ref.shape[0]
    share = near_ref.shape[0] // len(piece_refs)
    row_place, core = place_ref[0], place_ref[1] & 1
    for hop, ref in enumerate(piece_refs):
        start = pl.multiple_of((row_place ^ hop) * share, share)
        near_ref[pl.ds(start, share), :] = ref[:share, :]
    factor = split(factor_ref[...])
    near = split(mult3(split(near_ref[...]), factor))
    far = split(mult3(split(right_ref[...]), factor, ACROSS))
    for place, prod_ref in ((core, mine_ref), (1 - core, other_ref)):
        block = pl.ds(pl.multiple_of(place * deep, deep), deep)
        change = mult3(split(left_ref[block, :]), near, ACROSS)
        change = change + mult3(split(prod_ref[...]), far, ACROSS)
        out_ref[block, :] = ham_ref[block, :] - change


def base_update(place, hamiltonian, left, mine, other, right, factor, pieces):
    return pl.pallas_call(
        base_kernel,
        in_specs=[SMEM] + [VMEM] * (6 + len(pieces)),
        out_shape=array(*hamiltonian.shape),
        scratch_shapes=[pltpu.VMEM(right.shape, jnp.float32)],
        compiler_params=LARGE,
        cost_estimate=estimate(3),
        name="base_update",
    )(place, hamiltonian, left, mine, other, right, factor, *pieces)


def coupling_kernel(base_ref, left_ref, right_ref, factor_ref, parts_ref, out_ref, sum_ref):
    strip = parts_ref.shape[1]
    for k in range(parts_ref.shape[0] // 2):
        sum_ref[k * strip : (k + 1) * strip, :] = parts_ref[2 * k] + parts_ref[2 * k + 1]
    factor = split(factor_ref[...])
    turn = mult3(split(sum_ref[...]), factor)
    middle = mult3(factor, split(turn), TURNED)
    near = mult3(split(right_ref[...]), split(middle))
    out_ref[...] = base_ref[...] + mult3(split(left_ref[...]), split(near), ACROSS)


def coupling_update(base, left, right, factor, parts):
    return pl.pallas_call(
        coupling_kernel,
        in_specs=[VMEM] * 5,
        out_shape=array(*base.shape),
        scratch_shapes=[pltpu.VMEM(factor.shape, jnp.float32)],
        compiler_params=LARGE,
        cost_estimate=estimate(2),
        name="coupling_update",
    )(base, left, right, factor, parts)


def gather(piece, axis, size):
    copies = jnp.broadcast_to(piece[None], (size,) + piece.shape)
    return lax.all_to_all(copies, axis, 0, 0, tiled=True)


def hops(values, size):
    got = [values[0]]
    for hop in range(1, size):
        got.append(lax.ppermute(values[hop], "row", [(i, i ^ hop) for i in range(size)]))
    return got


def tree_sum(terms):
    while len(terms) > 1:
        terms = [terms[i] + terms[i + 1] for i in range(0, len(terms), 2)]
    return terms[0]


def shards(rows, cols, hamiltonian, panel):
    rows_dev, width = panel.shape
    cols_dev = hamiltonian.shape[1]
    row_place = lax.axis_index("row")
    col_place = lax.axis_index("col")
    chips = cols // 2
    strip = width // cols
    deep = rows_dev // 2
    piece = deep // chips
    share = cols_dev // rows
    pair = [(i, i ^ 1) for i in range(cols)]
    groups = [[2 * k + e for k in range(chips)] for e in range(2)]
    place = jnp.stack([row_place, col_place]).astype(jnp.int32)

    wide = lax.ppermute(hamiltonian, "col", pair)

    owners = [c * cols_dev // rows_dev for c in range(cols)]
    owner = col_place * cols_dev // rows_dev
    offset = col_place * cols_dev - owner * rows_dev
    slab = lax.dynamic_slice_in_dim(panel, offset, cols_dev, 0)
    slab = jnp.where(row_place == owner, slab, 0.0)
    hop, having = rows // 2, [0]
    got = jnp.zeros_like(slab)
    strips = None
    while hop:
        if having != [0]:
            slab = slab + got
        if strips is None and (having != [0] or hop == 1):
            strips = gram_strips(place, panel, rows, cols)
            strips = lax.all_to_all(strips, "row", 0, 0, tiled=True).sum(axis=0)
            strips, slab = lax.optimization_barrier((strips, slab))
        pairs = [
            ((owners[c] ^ d) * cols + c, (owners[c] ^ d ^ hop) * cols + c)
            for c in range(cols)
            for d in having
        ]
        got = lax.ppermute(slab, ("row", "col"), pairs)
        having = having + [d ^ hop for d in having]
        hop //= 2

    strips = gather(strips, "col", cols)
    gram = strips[:, :strip].reshape(width, width)
    panel_top = strips[:, strip:].reshape(width, width)
    first_upper, first_inv = cholesky(gram)
    half, half_cols, gram2_strips = half_stage(place, panel, slab, got, first_inv, rows, cols)
    gram2_strip = lax.all_to_all(gram2_strips, "row", 0, 0, tiled=True).sum(axis=0)
    half_next = lax.ppermute(half_cols, "col", pair)
    gram2 = gather(gram2_strip, "col", cols).reshape(width, width)
    second_upper = near_cholesky(gram2)

    left, right, packed, pieces = products(
        place, hamiltonian, wide, half, half_cols, half_next, second_upper, rows, cols
    )
    gram2, panel_top, packed = lax.optimization_barrier((gram2, panel_top, packed))
    factor, band_block = compact_factor(
        gram2, panel_top, first_inv, second_upper, first_upper
    )
    packed = lax.all_to_all(packed, "col", 0, 0, axis_index_groups=groups, tiled=True)
    packed = packed.sum(axis=0)
    near_piece = tree_sum(hops(pieces, rows))
    mine = jnp.broadcast_to(packed[:piece][None], (chips, piece, width))
    mine = lax.all_to_all(mine, "col", 0, 0, axis_index_groups=groups, tiled=True)
    mine = mine.reshape(deep, width)
    other = lax.ppermute(mine, "col", pair)
    both = jnp.concatenate([near_piece, packed[piece:]], axis=0)
    both = hops([both] * rows, rows)
    coupling_strip = tree_sum([value[share:] for value in both])
    coupling_strip, factor = lax.optimization_barrier((coupling_strip, factor))
    coupling = gather(coupling_strip, "col", cols)
    base = base_update(place, hamiltonian, left, mine, other, right, factor, both)
    updated = coupling_update(base, left, right, factor, coupling)
    return (updated, band_block)


def solution(mesh):
    in_specs = (P("row", "col"), P("row", None))
    out_specs = (P("row", "col"), P())
    body = functools.partial(shards, mesh.shape["row"], mesh.shape["col"])
    return jax.shard_map(body, mesh=mesh, in_specs=in_specs, out_specs=out_specs, check_vma=False)
```

```python
import functools

import jax
import jax.numpy as jnp
from jax import lax
from jax.experimental import pallas as pl
from jax.experimental.pallas import tpu as pltpu
from jax.sharding import PartitionSpec as P

SUB = 8
LANE = 128
BLOCK = 32
HIGHEST = lax.Precision.HIGHEST
SMALL = pltpu.CompilerParams(vmem_limit_bytes=10 * 2**20)
LARGE = pltpu.CompilerParams(vmem_limit_bytes=24 * 2**20)
VMEM = pl.BlockSpec(memory_space=pltpu.VMEM)
SMEM = pl.BlockSpec(memory_space=pltpu.SMEM)
HBM = pl.BlockSpec(memory_space=pltpu.HBM)
PLAIN = ((1,), (0,))
TURNED = ((0,), (0,))
ACROSS = ((1,), (1,))


def mult(left, right, dims=PLAIN):
    return lax.dot_general(
        left, right, (dims, ((), ())), precision=HIGHEST, preferred_element_type=jnp.float32
    )


def move(pairs, sems):
    copies = [pltpu.make_async_copy(src, dst, sems.at[i]) for i, (src, dst) in enumerate(pairs)]
    for copy in copies:
        copy.start()
    return copies


def wait(copies):
    for copy in copies:
        copy.wait()


def split(value):
    high = value.astype(jnp.bfloat16)
    return high, (value - high.astype(jnp.float32)).astype(jnp.bfloat16)


def mult3(left, right, dims=PLAIN):
    def one(a, b):
        return lax.dot_general(a, b, (dims, ((), ())), preferred_element_type=jnp.float32)

    return one(left[0], right[0]) + (one(left[0], right[1]) + one(left[1], right[0]))


def chol_kernel(gram_ref, upper_ref, inv_ref, work_ref):
    size = gram_ref.shape[0]
    tiles = size // LANE
    groups = BLOCK // SUB
    lanes = lax.broadcasted_iota(jnp.int32, (SUB, LANE), 1)
    work_ref[...] = gram_ref[...]

    def spread(row):
        return jnp.broadcast_to(row, (SUB, LANE))

    for first in range(0, size, BLOCK):
        rows = [
            [
                work_ref[first + SUB * g : first + SUB * (g + 1), LANE * t : LANE * (t + 1)]
                for t in range(tiles)
            ]
            for g in range(groups)
        ]
        for g in range(groups):
            col = first + SUB * g
            home, low = divmod(col, LANE)
            in_block = (lanes >= low) & (lanes < low + SUB)
            flat = [[spread(rows[g][t][k : k + 1, :]) for t in range(tiles)] for k in range(SUB)]
            diag = [
                [spread(flat[k][home][:, low + i : low + i + 1]) for i in range(k + 1)]
                for k in range(SUB)
            ]
            unit = [jnp.where(lanes == low + k, 1.0, 0.0) for k in range(SUB)]
            later = range(g + 1, groups)
            cols = {
                q: [spread(rows[q][home][:, low + i : low + i + 1]) for i in range(SUB)]
                for q in later
            }
            for q in later:
                rows[q][home] = jnp.where(in_block, 0.0, rows[q][home])
            for i in range(SUB):
                recip = 1.0 / diag[i][i]
                steps = [None] * SUB
                for k in range(i + 1, SUB):
                    steps[k] = diag[k][i] * recip
                for k in range(i + 1, SUB):
                    for j in range(i + 1, k + 1):
                        diag[k][j] = diag[k][j] - steps[k] * diag[j][i]
                for k in range(i + 1, SUB):
                    for t in range(tiles):
                        flat[k][t] = flat[k][t] - steps[k] * flat[i][t]
                    unit[k] = unit[k] - steps[k] * unit[i]
                for q in later:
                    step = cols[q][i] * recip
                    for j in range(i + 1, SUB):
                        cols[q][j] = cols[q][j] - step * diag[j][i]
                    for t in range(tiles):
                        source = flat[i][t]
                        if t == home:
                            source = jnp.where(in_block, unit[i], source)
                        rows[q][t] = rows[q][t] - step * source
            for k in range(SUB):
                scale = lax.rsqrt(diag[k][k])
                for t in range(tiles):
                    scaled = flat[k][t] * scale
                    if t < home:
                        up, inv = jnp.zeros_like(scaled), scaled
                    elif t > home:
                        up, inv = scaled, jnp.zeros_like(scaled)
                    else:
                        up = jnp.where(lanes >= low + k, scaled, 0.0)
                        inv = jnp.where(in_block, unit[k] * scale, scaled)
                        inv = jnp.where(lanes < low + SUB, inv, 0.0)
                    upper_ref[col + k : col + k + 1, LANE * t : LANE * (t + 1)] = up[0:1]
                    inv_ref[col + k : col + k + 1, LANE * t : LANE * (t + 1)] = inv[0:1]
        rest = first + BLOCK
        if rest == size:
            break
        start = rest // LANE * LANE
        left = upper_ref[first:rest, start:size]
        wide = lax.broadcasted_iota(jnp.int32, (BLOCK, size), 1)
        right = jnp.where(wide < rest, inv_ref[first:rest, :], upper_ref[first:rest, :])
        change = mult(left, right, ((0,), (0,)))
        below = lax.broadcasted_iota(jnp.int32, (size - rest, size), 1)
        old = jnp.where((below >= first) & (below < rest), 0.0, work_ref[rest:size, :])
        work_ref[rest:size, :] = old - change[rest - start :, :]


def estimate(micros):
    return pl.CostEstimate(flops=int(micros * 1e9), bytes_accessed=int(micros * 3e6), transcendentals=0)


def square(size):
    return jax.ShapeDtypeStruct((size, size), jnp.float32)


def first_kernel(parts_ref, upper_out, inv_ref, gram_ref, upper_ref, work_ref, sems):
    strip = parts_ref.shape[1]
    for c in range(parts_ref.shape[0]):
        gram_ref[c * strip : (c + 1) * strip, :] = parts_ref[c]
    chol_kernel(gram_ref, upper_ref, inv_ref, work_ref)
    wait(move([(upper_ref, upper_out)], sems))


def cholesky(parts):
    size = parts.shape[2]
    return pl.pallas_call(
        first_kernel,
        in_specs=[VMEM],
        out_specs=(HBM, VMEM),
        out_shape=(square(size), square(size)),
        scratch_shapes=[pltpu.VMEM((size, size), jnp.float32)] * 3 + [pltpu.SemaphoreType.DMA((1,))],
        compiler_params=SMALL,
        cost_estimate=estimate(10),
        name="cholesky_inverse",
    )(parts)


def grids(size):
    row = lax.broadcasted_iota(jnp.int32, (size, size), 0)
    col = lax.broadcasted_iota(jnp.int32, (size, size), 1)
    return row, col


def near_kernel(gram_ref, upper_ref, inv_ref, work_ref):
    size = gram_ref.shape[0]
    row, col = grids(size)
    ident = jnp.where(row == col, 1.0, 0.0)
    weight = jnp.where(row > col, 1.0, ident * 0.5)
    gram = split(gram_ref[...])

    def look(inv):
        halves = split(inv)
        upper = mult3(halves, gram)
        low = weight * (mult3(split(upper), halves, ACROSS) - ident)
        return upper, low, jnp.sum(low * low)

    def more(state):
        count, _, _, _, worst = state
        return jnp.logical_not(worst < 1e-5) & (count < 8)

    def step(state):
        count, inv, _, low, _ = state
        low = split(low)
        turn = mult3(low, split(inv))
        inv = inv - turn + mult3(low, split(turn))
        return (count + 1, inv) + look(inv)

    low = weight * (gram_ref[...] - ident)
    halves = split(low)
    inv = ident - low + mult3(halves, halves)
    state = lax.while_loop(more, step, (jnp.int32(0), inv) + look(inv))
    _, _, upper, low, worst = state
    upper = upper + mult3(split(low), split(upper), TURNED)
    upper_ref[...] = jnp.where(row <= col, upper, 0.0)

    @pl.when(jnp.logical_not(worst < 1e-5))
    def _():
        chol_kernel(gram_ref, upper_ref, inv_ref, work_ref)


def near_cholesky(gram):
    size = gram.shape[0]
    return pl.pallas_call(
        near_kernel,
        out_shape=square(size),
        scratch_shapes=[pltpu.VMEM((size, size), jnp.float32)] * 2,
        compiler_params=SMALL,
        cost_estimate=estimate(3),
        name="near_cholesky",
    )(gram)


def factor_kernel(parts_ref, inv_ref, upper_ref, first_ref, out_ref, band_ref,
                  first, out, band, sems):
    fetch = move([(first_ref, first)], sems)
    size = inv_ref.shape[0]
    strip = size // parts_ref.shape[0]
    row, col = grids(size)
    ident = jnp.where(row == col, 1.0, 0.0)
    pieces = range(parts_ref.shape[0])
    gram = jnp.concatenate([parts_ref[c, :strip, :] for c in pieces], axis=0)
    top = jnp.concatenate([parts_ref[c, strip:, :] for c in pieces], axis=0)
    half_top = mult(top, inv_ref[...], ACROSS)
    mat = gram + mult(half_top, upper_ref[...], TURNED)
    halves = split(mat)
    wait(fetch)
    band[...] = -mult(upper_ref[...], first[...])
    store = move([(band, band_ref)], sems)

    def residual(guess):
        return ident - mult3(halves, split(guess))

    def step(state):
        count, guess, rest, _ = state
        guess = guess + mult3(split(guess), split(rest))
        rest = residual(guess)
        return count + 1, guess, rest, jnp.max(jnp.abs(rest))

    def more(state):
        count, _, _, worst = state
        return (worst > 2e-5) & (count < 40)

    guess = 0.5 * ident
    rest = ident - 0.5 * mat
    for _ in range(4):
        parts = split(rest)
        guess = guess + mult3(split(guess), parts)
        rest = mult3(parts, parts)
    guess = guess + mult3(split(guess), split(rest))
    rest = residual(guess)
    state = (jnp.int32(0), guess, rest, jnp.max(jnp.abs(rest)))
    out[...] = lax.while_loop(more, step, state)[1]
    wait(store + move([(out, out_ref)], sems.at[pl.ds(1, 1)]))


def compact_factor(parts, inv, upper, first):
    size = inv.shape[0]
    return pl.pallas_call(
        factor_kernel,
        in_specs=[VMEM] * 3 + [HBM],
        out_specs=(HBM, HBM),
        out_shape=(square(size), square(size)),
        scratch_shapes=[pltpu.VMEM((size, size), jnp.float32)] * 3 + [pltpu.SemaphoreType.DMA((2,))],
        compiler_params=SMALL,
        cost_estimate=estimate(4),
        name="compact_factor",
    )(parts, inv, upper, first)


def array(*dims):
    return jax.ShapeDtypeStruct(dims, jnp.float32)


def scratch(*dims):
    return pltpu.VMEM(dims, jnp.float32)


def gram_kernel(place_ref, panel_ref, out_ref, gram_ref):
    strip = out_ref.shape[0] // 2
    mine = pl.ds(pl.multiple_of(place_ref[1] * strip, strip), strip)
    gram_ref[...] = mult(panel_ref[...], panel_ref[...], TURNED)
    out_ref[:strip, :] = gram_ref[mine, :]
    out_ref[strip:, :] = panel_ref[mine, :] * jnp.where(place_ref[0] == 0, 1.0, 0.0)


def gram_strips(place, panel, cols):
    width = panel.shape[1]
    return pl.pallas_call(
        gram_kernel,
        in_specs=[SMEM, VMEM],
        out_shape=array(2 * width // cols, width),
        scratch_shapes=[scratch(width, width)],
        compiler_params=LARGE,
        cost_estimate=estimate(2),
        name="gram_strips",
    )(place, panel)


def half_kernel(place_ref, panel_ref, slab_ref, got_ref, inv_ref, half_out, cols_out, out_ref,
                half_ref, cols_ref, gram_ref, sems):
    strip = out_ref.shape[0]
    mine = pl.ds(pl.multiple_of(place_ref[1] * strip, strip), strip)
    half = mult(panel_ref[...], inv_ref[...], ACROSS)
    half_ref[...] = half
    cols_ref[...] = mult(slab_ref[...] + got_ref[...], inv_ref[...], ACROSS)
    store = move([(half_ref, half_out), (cols_ref, cols_out)], sems)
    parts = split(half)
    gram_ref[...] = mult3(parts, parts, TURNED)
    out_ref[...] = gram_ref[mine, :]
    wait(store)


def half_stage(place, panel, slab, got, inv, cols):
    width = panel.shape[1]
    return pl.pallas_call(
        half_kernel,
        in_specs=[SMEM] + [VMEM] * 4,
        out_specs=(HBM, HBM, VMEM),
        out_shape=(array(*panel.shape), array(*slab.shape), array(width // cols, width)),
        scratch_shapes=[
            scratch(*panel.shape),
            scratch(*slab.shape),
            scratch(width, width),
            pltpu.SemaphoreType.DMA((2,)),
        ],
        compiler_params=LARGE,
        cost_estimate=estimate(3),
        name="half_stage",
    )(place, panel, slab, got, inv)


def products_kernel(place_ref, ham_ref, half_in, cols_in, upper_ref,
                    left_out, right_out, keep_ref, send_ref, *rest_refs):
    piece_refs = rest_refs[:-6]
    left_ref, right_ref, part_ref, coupling_ref, near_ref, sems = rest_refs[-6:]
    fetch = move([(cols_in, right_ref), (half_in, left_ref)], sems)
    width = upper_ref.shape[0]
    chips = keep_ref.shape[0]
    rows_dev = ham_ref.shape[0]
    piece, strip = rows_dev // 2 // chips, width // 2 // chips
    share = piece_refs[0].shape[0]
    row_place, col_place = place_ref[0], place_ref[1]
    core, chip = col_place & 1, col_place // 2
    ham = split(ham_ref[...])
    fetch[0].wait()
    lead = jnp.where(col_place == 0, 1.0, 0.0)
    right_ref[:width, :] = right_ref[:width, :] + lead * upper_ref[...]
    part = mult3(ham, split(right_ref[...]))
    part_ref[...] = part
    fetch[1].wait()
    lead = jnp.where(row_place == 0, 1.0, 0.0)
    left_ref[:width, :] = left_ref[:width, :] + lead * upper_ref[...]
    store = move([(right_ref, right_out), (left_ref, left_out)], sems)
    left = split(left_ref[...])
    coupling_ref[...] = mult3(left, split(part), TURNED)
    for ref, half in ((send_ref, 1 - core), (keep_ref, core)):
        for hop in range(chips):
            start = (half * chips + (chip ^ hop)) * piece
            ref[hop, :piece, :] = part_ref[pl.ds(pl.multiple_of(start, piece), piece), :]
            start = (half * chips + (chip ^ hop)) * strip
            ref[hop, piece:, :] = coupling_ref[pl.ds(pl.multiple_of(start, strip), strip), :]
    near_ref[...] = mult3(ham, left, TURNED)
    for hop, ref in enumerate(piece_refs):
        start = pl.multiple_of((row_place ^ hop) * share, share)
        ref[...] = near_ref[pl.ds(start, share), :]
    wait(store)


def products(place, hamiltonian, half, half_cols, upper, rows, cols):
    rows_dev, cols_dev = hamiltonian.shape
    width = upper.shape[0]
    chips = cols // 2
    share = (rows_dev + width) // cols
    out = pl.pallas_call(
        products_kernel,
        in_specs=[SMEM, VMEM, HBM, HBM, VMEM],
        out_specs=(HBM, HBM) + (VMEM,) * (2 + rows),
        out_shape=(
            array(rows_dev, width),
            array(cols_dev, width),
            array(chips, share, width),
            array(chips, share, width),
        )
        + (array(cols_dev // rows, width),) * rows,
        scratch_shapes=[
            scratch(rows_dev, width),
            scratch(cols_dev, width),
            scratch(rows_dev, width),
            scratch(width, width),
            scratch(cols_dev, width),
            pltpu.SemaphoreType.DMA((2,)),
        ],
        compiler_params=LARGE,
        cost_estimate=estimate(4),
        name="products",
    )(place, hamiltonian, half, half_cols, upper)
    return out[0], out[1], out[2], out[3], out[4:]


def pair_kernel(keep_ref, got_ref, *out_refs):
    for hop, ref in enumerate(out_refs):
        ref[...] = keep_ref[hop] + got_ref[hop]


def pair_add(keep, got):
    return pl.pallas_call(
        pair_kernel,
        in_specs=[VMEM] * 2,
        out_shape=(array(*keep.shape[1:]),) * keep.shape[0],
        compiler_params=LARGE,
        cost_estimate=estimate(0.5),
        name="pair_add",
    )(keep, got)


def tree_sum(terms):
    while len(terms) > 1:
        terms = [terms[i] + terms[i + 1] for i in range(0, len(terms), 2)]
    return terms[0]


def sums_kernel(count, *refs):
    total_refs, piece_refs = refs[:count], refs[count:-2]
    mine_ref, both_ref = refs[-2:]
    piece, share = mine_ref.shape[0], piece_refs[0].shape[0]
    total = tree_sum([ref[...] for ref in total_refs])
    mine_ref[...] = total[:piece]
    both_ref[:share, :] = tree_sum([ref[...] for ref in piece_refs])
    both_ref[share:, :] = total[piece:]


def sum_pieces(totals, pieces, piece):
    share, width = pieces[0].shape
    strip = totals[0].shape[0] - piece
    return pl.pallas_call(
        functools.partial(sums_kernel, len(totals)),
        in_specs=[VMEM] * (len(totals) + len(pieces)),
        out_shape=(array(piece, width), array(share + strip, width)),
        compiler_params=LARGE,
        cost_estimate=estimate(0.5),
        name="sum_pieces",
    )(*totals, *pieces)


def spread_kernel(groups, *refs):
    out_ref = refs[-1]
    start = 0
    for count, first, last in groups:
        total = tree_sum([ref[first:last, :] for ref in refs[:count]])
        refs = refs[count:]
        for c in range(out_ref.shape[0]):
            out_ref[c, start : start + last - first, :] = total
        start += last - first


def sum_gather(cols, *groups):
    terms = [term for group in groups for term in group[0]]
    bounds = [(len(group[0]), group[1], group[2]) for group in groups]
    height = sum(last - first for _, first, last in bounds)
    copies = pl.pallas_call(
        functools.partial(spread_kernel, bounds),
        in_specs=[VMEM] * len(terms),
        out_shape=array(cols, height, terms[0].shape[1]),
        compiler_params=LARGE,
        cost_estimate=estimate(0.5),
        name="sum_copies",
    )(*terms)
    return lax.all_to_all(copies, "col", 0, 0, tiled=True)


def merge_kernel(place_ref, *refs):
    out_ref = refs[-1]
    piece = refs[0].shape[0]
    chip = place_ref[1] // 2
    for hop, ref in enumerate(refs[:-1]):
        out_ref[pl.ds(pl.multiple_of((chip ^ hop) * piece, piece), piece), :] = ref[...]


def merge(place, pieces):
    piece, width = pieces[0].shape
    return pl.pallas_call(
        merge_kernel,
        in_specs=[SMEM] + [VMEM] * len(pieces),
        out_shape=array(len(pieces) * piece, width),
        compiler_params=LARGE,
        cost_estimate=estimate(0.5),
        name="merge_pieces",
    )(place, *pieces)


def base_kernel(place_ref, ham_ref, left_in, mine_ref, other_ref, right_in, factor_in, *rest_refs):
    piece_refs, out_hbm = rest_refs[:-7], rest_refs[-7]
    left_ref, right_ref, factor_ref, near_ref, out_ref, sems = rest_refs[-6:]
    fetch = move([(factor_in, factor_ref), (right_in, right_ref), (left_in, left_ref)], sems)
    deep = mine_ref.shape[0]
    share = near_ref.shape[0] // len(piece_refs)
    row_place, core = place_ref[0], place_ref[1] & 1
    for hop, ref in enumerate(piece_refs):
        start = pl.multiple_of((row_place ^ hop) * share, share)
        near_ref[pl.ds(start, share), :] = ref[:share, :]
    fetch[0].wait()
    factor = split(factor_ref[...])
    near = split(mult3(split(near_ref[...]), factor))
    fetch[1].wait()
    far = split(mult3(split(right_ref[...]), factor, ACROSS))
    fetch[2].wait()
    for place, prod_ref in ((core, mine_ref), (1 - core, other_ref)):
        block = pl.ds(pl.multiple_of(place * deep, deep), deep)
        change = mult3(split(left_ref[block, :]), near, ACROSS)
        change = change + mult3(split(prod_ref[...]), far, ACROSS)
        out_ref[block, :] = ham_ref[block, :] - change
    wait(move([(out_ref, out_hbm)], sems))


def base_update(place, hamiltonian, left, mine, other, right, factor, pieces):
    return pl.pallas_call(
        base_kernel,
        in_specs=[SMEM, VMEM, HBM, VMEM, VMEM, HBM, HBM] + [VMEM] * len(pieces),
        out_specs=HBM,
        out_shape=array(*hamiltonian.shape),
        scratch_shapes=[
            scratch(*left.shape),
            scratch(*right.shape),
            scratch(*factor.shape),
            scratch(*right.shape),
            scratch(*hamiltonian.shape),
            pltpu.SemaphoreType.DMA((3,)),
        ],
        compiler_params=LARGE,
        cost_estimate=estimate(4),
        name="base_update",
    )(place, hamiltonian, left, mine, other, right, factor, *pieces)


def coupling_kernel(base_in, left_in, right_in, factor_in, parts_ref, out_hbm,
                    base_ref, left_ref, right_ref, factor_ref, sum_ref, sems):
    fetch = move(
        [(factor_in, factor_ref), (right_in, right_ref), (left_in, left_ref), (base_in, base_ref)],
        sems,
    )
    strip = parts_ref.shape[1]
    chips = parts_ref.shape[0] // 2
    for c in range(parts_ref.shape[0]):
        start = ((c % 2) * chips + c // 2) * strip
        sum_ref[start : start + strip, :] = parts_ref[c]
    fetch[0].wait()
    factor = split(factor_ref[...])
    turn = mult3(split(sum_ref[...]), factor)
    middle = mult3(factor, split(turn), TURNED)
    fetch[1].wait()
    near = split(mult3(split(right_ref[...]), split(middle)))
    fetch[2].wait()
    fetch[3].wait()
    deep = base_ref.shape[0] // 2
    stores = []
    for half in range(2):
        block = pl.ds(half * deep, deep)
        base_ref[block, :] += mult3(split(left_ref[block, :]), near, ACROSS)
        copy = pltpu.make_async_copy(base_ref.at[block], out_hbm.at[block], sems.at[half])
        copy.start()
        stores.append(copy)
    wait(stores)


def coupling_update(base, left, right, factor, parts):
    return pl.pallas_call(
        coupling_kernel,
        in_specs=[HBM] * 4 + [VMEM],
        out_specs=HBM,
        out_shape=array(*base.shape),
        scratch_shapes=[
            scratch(*base.shape),
            scratch(*left.shape),
            scratch(*right.shape),
            scratch(*factor.shape),
            scratch(*factor.shape),
            pltpu.SemaphoreType.DMA((4,)),
        ],
        compiler_params=LARGE,
        cost_estimate=estimate(3),
        name="coupling_update",
    )(base, left, right, factor, parts)


def hops(values, axis, size, scale=1):
    got = [values[0]]
    for hop in range(1, len(values)):
        pairs = [(i, i ^ (hop * scale)) for i in range(size)]
        got.append(lax.ppermute(values[hop], axis, pairs))
    return got


def shards(rows, cols, hamiltonian, panel):
    rows_dev, width = panel.shape
    cols_dev = hamiltonian.shape[1]
    row_place = lax.axis_index("row")
    col_place = lax.axis_index("col")
    chips = cols // 2
    strip = width // cols
    piece = rows_dev // cols
    share = cols_dev // rows
    pair = [(i, i ^ 1) for i in range(cols)]
    place = jnp.stack([row_place, col_place]).astype(jnp.int32)

    strips = hops([gram_strips(place, panel, cols)] * rows, "row", rows)

    owners = [c * cols_dev // rows_dev for c in range(cols)]
    owner = col_place * cols_dev // rows_dev
    offset = col_place * cols_dev - owner * rows_dev
    slab = lax.dynamic_slice_in_dim(panel, offset, cols_dev, 0)
    slab = jnp.where(row_place == owner, slab, 0.0)
    strips, slab = lax.optimization_barrier((strips, slab))
    hop, having = rows // 2, [0]
    got = jnp.zeros_like(slab)
    while hop:
        if having != [0]:
            slab = slab + got
        pairs = [
            ((owners[c] ^ d) * cols + c, (owners[c] ^ d ^ hop) * cols + c)
            for c in range(cols)
            for d in having
        ]
        got = lax.ppermute(slab, ("row", "col"), pairs)
        having = having + [d ^ hop for d in having]
        hop //= 2

    gram = sum_gather(cols, (strips, 0, strip))
    first_upper, first_inv = cholesky(gram)
    half, half_cols, gram2_strip = half_stage(place, panel, slab, got, first_inv, cols)
    gram2_strips = hops([gram2_strip] * rows, "row", rows)
    parts = sum_gather(cols, (gram2_strips, 0, strip), (strips, strip, 2 * strip))
    gram2 = parts[:, :strip].reshape(width, width)
    second_upper = near_cholesky(gram2)

    left, right, keep, send, pieces = products(
        place, hamiltonian, half, half_cols, second_upper, rows, cols
    )
    parts, send = lax.optimization_barrier((parts, send))
    factor, band_block = compact_factor(parts, first_inv, second_upper, first_upper)
    totals = pair_add(keep, lax.ppermute(send, "col", pair))
    totals = hops(totals, "col", cols, 2)
    pieces = hops(pieces, "row", rows)
    mine, both = sum_pieces(totals, pieces, piece)
    both = hops([both] * rows, "row", rows)
    mine = merge(place, hops([mine] * chips, "col", cols, 2))
    other = lax.ppermute(mine, "col", pair)
    both, factor = lax.optimization_barrier((both, factor))
    coupling = sum_gather(cols, (both, share, share + strip))
    base = base_update(place, hamiltonian, left, mine, other, right, factor, both)
    updated = coupling_update(base, left, right, factor, coupling)
    return (updated, band_block)


def solution(mesh):
    in_specs = (P("row", "col"), P("row", None))
    out_specs = (P("row", "col"), P())
    body = functools.partial(shards, mesh.shape["row"], mesh.shape["col"])
    return jax.shard_map(body, mesh=mesh, in_specs=in_specs, out_specs=out_specs, check_vma=False)
```

```python
import functools

import jax
import jax.numpy as jnp
from jax import lax
from jax.experimental import pallas as pl
from jax.experimental.pallas import tpu as pltpu
from jax.sharding import PartitionSpec as P

SUB = 8
LANE = 128
BLOCK = 32
HIGHEST = lax.Precision.HIGHEST
SMALL = pltpu.CompilerParams(vmem_limit_bytes=10 * 2**20)
LARGE = pltpu.CompilerParams(vmem_limit_bytes=24 * 2**20)
VMEM = pl.BlockSpec(memory_space=pltpu.VMEM)
SMEM = pl.BlockSpec(memory_space=pltpu.SMEM)
PLAIN = ((1,), (0,))
TURNED = ((0,), (0,))
ACROSS = ((1,), (1,))


def mult(left, right, dims=PLAIN):
    return lax.dot_general(
        left, right, (dims, ((), ())), precision=HIGHEST, preferred_element_type=jnp.float32
    )


def split(value):
    high = value.astype(jnp.bfloat16)
    return high, (value - high.astype(jnp.float32)).astype(jnp.bfloat16)


def mult3(left, right, dims=PLAIN):
    def one(a, b):
        return lax.dot_general(a, b, (dims, ((), ())), preferred_element_type=jnp.float32)

    return one(left[0], right[0]) + (one(left[0], right[1]) + one(left[1], right[0]))


def chol_kernel(gram_ref, upper_ref, inv_ref, work_ref):
    size = gram_ref.shape[0]
    tiles = size // LANE
    groups = BLOCK // SUB
    lanes = lax.broadcasted_iota(jnp.int32, (SUB, LANE), 1)
    work_ref[...] = gram_ref[...]

    def spread(row):
        return jnp.broadcast_to(row, (SUB, LANE))

    for first in range(0, size, BLOCK):
        rows = [
            [
                work_ref[first + SUB * g : first + SUB * (g + 1), LANE * t : LANE * (t + 1)]
                for t in range(tiles)
            ]
            for g in range(groups)
        ]
        for g in range(groups):
            col = first + SUB * g
            home, low = divmod(col, LANE)
            in_block = (lanes >= low) & (lanes < low + SUB)
            flat = [[spread(rows[g][t][k : k + 1, :]) for t in range(tiles)] for k in range(SUB)]
            diag = [
                [spread(flat[k][home][:, low + i : low + i + 1]) for i in range(k + 1)]
                for k in range(SUB)
            ]
            unit = [jnp.where(lanes == low + k, 1.0, 0.0) for k in range(SUB)]
            later = range(g + 1, groups)
            cols = {
                q: [spread(rows[q][home][:, low + i : low + i + 1]) for i in range(SUB)]
                for q in later
            }
            for q in later:
                rows[q][home] = jnp.where(in_block, 0.0, rows[q][home])
            for i in range(SUB):
                recip = 1.0 / diag[i][i]
                steps = [None] * SUB
                for k in range(i + 1, SUB):
                    steps[k] = diag[k][i] * recip
                for k in range(i + 1, SUB):
                    for j in range(i + 1, k + 1):
                        diag[k][j] = diag[k][j] - steps[k] * diag[j][i]
                for k in range(i + 1, SUB):
                    for t in range(tiles):
                        flat[k][t] = flat[k][t] - steps[k] * flat[i][t]
                    unit[k] = unit[k] - steps[k] * unit[i]
                for q in later:
                    step = cols[q][i] * recip
                    for j in range(i + 1, SUB):
                        cols[q][j] = cols[q][j] - step * diag[j][i]
                    for t in range(tiles):
                        source = flat[i][t]
                        if t == home:
                            source = jnp.where(in_block, unit[i], source)
                        rows[q][t] = rows[q][t] - step * source
            for k in range(SUB):
                scale = lax.rsqrt(diag[k][k])
                for t in range(tiles):
                    scaled = flat[k][t] * scale
                    if t < home:
                        up, inv = jnp.zeros_like(scaled), scaled
                    elif t > home:
                        up, inv = scaled, jnp.zeros_like(scaled)
                    else:
                        up = jnp.where(lanes >= low + k, scaled, 0.0)
                        inv = jnp.where(in_block, unit[k] * scale, scaled)
                        inv = jnp.where(lanes < low + SUB, inv, 0.0)
                    upper_ref[col + k : col + k + 1, LANE * t : LANE * (t + 1)] = up[0:1]
                    inv_ref[col + k : col + k + 1, LANE * t : LANE * (t + 1)] = inv[0:1]
        rest = first + BLOCK
        if rest == size:
            break
        start = rest // LANE * LANE
        left = upper_ref[first:rest, start:size]
        wide = lax.broadcasted_iota(jnp.int32, (BLOCK, size), 1)
        right = jnp.where(wide < rest, inv_ref[first:rest, :], upper_ref[first:rest, :])
        change = mult(left, right, ((0,), (0,)))
        below = lax.broadcasted_iota(jnp.int32, (size - rest, size), 1)
        old = jnp.where((below >= first) & (below < rest), 0.0, work_ref[rest:size, :])
        work_ref[rest:size, :] = old - change[rest - start :, :]


def estimate(micros):
    return pl.CostEstimate(flops=int(micros * 1e7), bytes_accessed=int(micros * 3e4), transcendentals=0)


def square(size):
    return jax.ShapeDtypeStruct((size, size), jnp.float32)


def first_kernel(parts_ref, upper_ref, inv_ref, gram_ref, work_ref):
    strip = parts_ref.shape[1]
    for c in range(parts_ref.shape[0]):
        gram_ref[c * strip : (c + 1) * strip, :] = parts_ref[c]
    chol_kernel(gram_ref, upper_ref, inv_ref, work_ref)


def cholesky(parts):
    size = parts.shape[2]
    return pl.pallas_call(
        first_kernel,
        in_specs=[VMEM],
        out_shape=(square(size), square(size)),
        scratch_shapes=[pltpu.VMEM((size, size), jnp.float32)] * 2,
        compiler_params=SMALL,
        cost_estimate=estimate(10),
        name="cholesky_inverse",
    )(parts)


def grids(size):
    row = lax.broadcasted_iota(jnp.int32, (size, size), 0)
    col = lax.broadcasted_iota(jnp.int32, (size, size), 1)
    return row, col


def near_kernel(gram_ref, upper_ref, inv_ref, work_ref):
    size = gram_ref.shape[0]
    row, col = grids(size)
    ident = jnp.where(row == col, 1.0, 0.0)
    weight = jnp.where(row > col, 1.0, ident * 0.5)
    gram = split(gram_ref[...])

    def look(inv):
        halves = split(inv)
        upper = mult3(halves, gram)
        low = weight * (mult3(split(upper), halves, ACROSS) - ident)
        return upper, low, jnp.sum(low * low)

    def more(state):
        count, _, _, _, worst = state
        return jnp.logical_not(worst < 1e-5) & (count < 8)

    def step(state):
        count, inv, _, low, _ = state
        low = split(low)
        turn = mult3(low, split(inv))
        inv = inv - turn + mult3(low, split(turn))
        return (count + 1, inv) + look(inv)

    low = weight * (gram_ref[...] - ident)
    halves = split(low)
    inv = ident - low + mult3(halves, halves)
    state = lax.while_loop(more, step, (jnp.int32(0), inv) + look(inv))
    _, _, upper, low, worst = state
    upper = upper + mult3(split(low), split(upper), TURNED)
    upper_ref[...] = jnp.where(row <= col, upper, 0.0)

    @pl.when(jnp.logical_not(worst < 1e-5))
    def _():
        chol_kernel(gram_ref, upper_ref, inv_ref, work_ref)


def near_cholesky(gram):
    size = gram.shape[0]
    return pl.pallas_call(
        near_kernel,
        out_shape=square(size),
        scratch_shapes=[pltpu.VMEM((size, size), jnp.float32)] * 2,
        compiler_params=SMALL,
        cost_estimate=estimate(3),
        name="near_cholesky",
    )(gram)


def factor_kernel(gram_ref, top_ref, inv_ref, upper_ref, first_ref, out_ref, band_ref):
    size = inv_ref.shape[0]
    row, col = grids(size)
    ident = jnp.where(row == col, 1.0, 0.0)
    band_ref[...] = -mult(upper_ref[...], first_ref[...])
    top = top_ref[...].reshape(size, size)
    half_top = mult(top, inv_ref[...], ACROSS)
    mat = gram_ref[...].reshape(size, size) + mult3(split(half_top), split(upper_ref[...]), TURNED)
    halves = split(mat)

    def rough(left, right):
        return jnp.dot(
            left.astype(jnp.bfloat16),
            right.astype(jnp.bfloat16),
            preferred_element_type=jnp.float32,
        )

    def residual(guess):
        return ident - mult3(halves, split(guess))

    def step(state):
        count, guess, rest, _ = state
        guess = guess + mult3(split(guess), split(rest))
        rest = residual(guess)
        return count + 1, guess, rest, jnp.max(jnp.abs(rest))

    def more(state):
        count, _, _, worst = state
        return (worst > 2e-5) & (count < 40)

    guess = 0.5 * ident
    rest = ident - 0.5 * mat
    for _ in range(4):
        guess = guess + rough(guess, rest)
        rest = rough(rest, rest)
    guess = guess + rough(guess, rest)
    rest = residual(guess)
    state = (jnp.int32(0), guess, rest, jnp.max(jnp.abs(rest)))
    out_ref[...] = lax.while_loop(more, step, state)[1]


def compact_factor(gram, top, inv, upper, first):
    return pl.pallas_call(
        factor_kernel,
        out_shape=(square(inv.shape[0]), square(inv.shape[0])),
        compiler_params=SMALL,
        cost_estimate=estimate(4),
        name="compact_factor",
    )(gram, top, inv, upper, first)


def array(*dims):
    return jax.ShapeDtypeStruct(dims, jnp.float32)


def scratch(*dims):
    return pltpu.VMEM(dims, jnp.float32)


def gram_kernel(place_ref, panel_ref, out_ref, gram_ref):
    strip = out_ref.shape[0] // 2
    mine = pl.ds(pl.multiple_of(place_ref[1] * strip, strip), strip)
    gram_ref[...] = mult(panel_ref[...], panel_ref[...], TURNED)
    out_ref[:strip, :] = gram_ref[mine, :]
    out_ref[strip:, :] = panel_ref[mine, :] * jnp.where(place_ref[0] == 0, 1.0, 0.0)


def gram_strips(place, panel, cols):
    width = panel.shape[1]
    return pl.pallas_call(
        gram_kernel,
        in_specs=[SMEM, VMEM],
        out_shape=array(2 * width // cols, width),
        scratch_shapes=[scratch(width, width)],
        compiler_params=LARGE,
        cost_estimate=estimate(2),
        name="gram_strips",
    )(place, panel)


def half_kernel(place_ref, panel_ref, slab_ref, got_ref, inv_ref, half_ref, cols_ref, out_ref, gram_ref):
    strip = out_ref.shape[0]
    mine = pl.ds(pl.multiple_of(place_ref[1] * strip, strip), strip)
    half = mult(panel_ref[...], inv_ref[...], ACROSS)
    half_ref[...] = half
    parts = split(half)
    gram_ref[...] = mult3(parts, parts, TURNED)
    out_ref[...] = gram_ref[mine, :]
    cols_ref[...] = mult(slab_ref[...] + got_ref[...], inv_ref[...], ACROSS)


def half_stage(place, panel, slab, got, inv, cols):
    width = panel.shape[1]
    return pl.pallas_call(
        half_kernel,
        in_specs=[SMEM] + [VMEM] * 4,
        out_shape=(array(*panel.shape), array(*slab.shape), array(width // cols, width)),
        scratch_shapes=[scratch(width, width)],
        compiler_params=LARGE,
        cost_estimate=estimate(3),
        name="half_stage",
    )(place, panel, slab, got, inv)


def near_rows_kernel(place_ref, ham_ref, half_ref, top_ref, *rest_refs):
    piece_refs, near_ref = rest_refs[:-1], rest_refs[-1]
    share = piece_refs[0].shape[0]
    row_place = place_ref[0]
    near_ref[...] = mult3(split(ham_ref[...]), split(half_ref[...]), TURNED)
    for hop, ref in enumerate(piece_refs):
        start = pl.multiple_of((row_place ^ hop) * share, share)
        ref[...] = near_ref[pl.ds(start, share), :]
    top_ref[...] = ham_ref[: top_ref.shape[0], :] * jnp.where(row_place == 0, 1.0, 0.0)


def near_rows(place, hamiltonian, half, rows):
    cols_dev, width = hamiltonian.shape[1], half.shape[1]
    out = pl.pallas_call(
        near_rows_kernel,
        in_specs=[SMEM, VMEM, VMEM],
        out_shape=(array(width, cols_dev),) + (array(cols_dev // rows, width),) * rows,
        scratch_shapes=[scratch(cols_dev, width)],
        compiler_params=LARGE,
        cost_estimate=estimate(3),
        name="near_rows",
    )(place, hamiltonian, half)
    return out[0], out[1:]


def products_kernel(place_ref, ham_ref, half_ref, cols_ref, upper_ref,
                    left_ref, right_ref, keep_ref, send_ref, part_ref, coupling_ref):
    width = upper_ref.shape[0]
    chips = keep_ref.shape[0]
    rows_dev = ham_ref.shape[0]
    piece, strip = rows_dev // 2 // chips, width // 2 // chips
    row_place, col_place = place_ref[0], place_ref[1]
    core, chip = col_place & 1, col_place // 2
    lead = jnp.where(col_place == 0, 1.0, 0.0)
    right_ref[...] = cols_ref[...]
    right_ref[:width, :] = cols_ref[:width, :] + lead * upper_ref[...]
    part = mult3(split(ham_ref[...]), split(right_ref[...]))
    part_ref[...] = part
    lead = jnp.where(row_place == 0, 1.0, 0.0)
    left_ref[...] = half_ref[...]
    left_ref[:width, :] = half_ref[:width, :] + lead * upper_ref[...]
    coupling_ref[...] = mult3(split(left_ref[...]), split(part), TURNED)
    for ref, half in ((send_ref, 1 - core), (keep_ref, core)):
        for hop in range(chips):
            start = (half * chips + (chip ^ hop)) * piece
            ref[hop, :piece, :] = part_ref[pl.ds(pl.multiple_of(start, piece), piece), :]
            start = (half * chips + (chip ^ hop)) * strip
            ref[hop, piece:, :] = coupling_ref[pl.ds(pl.multiple_of(start, strip), strip), :]


def products(place, hamiltonian, half, half_cols, upper, cols):
    rows_dev, cols_dev = hamiltonian.shape
    width = upper.shape[0]
    chips = cols // 2
    share = (rows_dev + width) // cols
    return pl.pallas_call(
        products_kernel,
        in_specs=[SMEM] + [VMEM] * 4,
        out_shape=(
            array(rows_dev, width),
            array(cols_dev, width),
            array(chips, share, width),
            array(chips, share, width),
        ),
        scratch_shapes=[scratch(rows_dev, width), scratch(width, width)],
        compiler_params=LARGE,
        cost_estimate=estimate(4),
        name="products",
    )(place, hamiltonian, half, half_cols, upper)


def pair_kernel(keep_ref, got_ref, *out_refs):
    for hop, ref in enumerate(out_refs):
        ref[...] = keep_ref[hop] + got_ref[hop]


def pair_add(keep, got):
    return pl.pallas_call(
        pair_kernel,
        in_specs=[VMEM] * 2,
        out_shape=(array(*keep.shape[1:]),) * keep.shape[0],
        compiler_params=LARGE,
        cost_estimate=estimate(0.5),
        name="pair_add",
    )(keep, got)


def tree_sum(terms):
    while len(terms) > 1:
        terms = [terms[i] + terms[i + 1] for i in range(0, len(terms), 2)]
    return terms[0]


def sums_kernel(*refs):
    mine_ref, strip_ref = refs[-2:]
    piece = mine_ref.shape[0]
    total = tree_sum([ref[...] for ref in refs[:-2]])
    mine_ref[...] = total[:piece]
    strip_ref[...] = total[piece:]


def sum_pieces(totals, piece):
    height, width = totals[0].shape
    return pl.pallas_call(
        sums_kernel,
        out_shape=(array(piece, width), array(height - piece, width)),
        compiler_params=LARGE,
        cost_estimate=estimate(0.5),
        name="sum_pieces",
    )(*totals)


def spread_kernel(first, last, *refs):
    out_ref = refs[-1]
    total = tree_sum([ref[first:last, :] for ref in refs[:-1]])
    for c in range(out_ref.shape[0]):
        out_ref[c] = total


def sum_copies(cols, terms, first, last):
    return pl.pallas_call(
        functools.partial(spread_kernel, first, last),
        in_specs=[VMEM] * len(terms),
        out_shape=array(cols, last - first, terms[0].shape[1]),
        compiler_params=LARGE,
        cost_estimate=estimate(0.5),
        name="sum_copies",
    )(*terms)


def trade(copies):
    return lax.all_to_all(copies, "col", 0, 0, tiled=True)


def merge_kernel(place_ref, *refs):
    out_ref = refs[-1]
    piece = refs[0].shape[0]
    chip = place_ref[1] // 2
    for hop, ref in enumerate(refs[:-1]):
        out_ref[pl.ds(pl.multiple_of((chip ^ hop) * piece, piece), piece), :] = ref[...]


def merge(place, pieces):
    piece, width = pieces[0].shape
    return pl.pallas_call(
        merge_kernel,
        in_specs=[SMEM] + [VMEM] * len(pieces),
        out_shape=array(len(pieces) * piece, width),
        compiler_params=LARGE,
        cost_estimate=estimate(0.5),
        name="merge_pieces",
    )(place, *pieces)


def base_kernel(
    place_ref, ham_ref, left_ref, mine_ref, other_ref, right_ref, factor_ref,
    upper_ref, top_ref, got_ref, *rest_refs
):
    piece_refs, out_ref, near_ref = rest_refs[:-2], rest_refs[-2], rest_refs[-1]
    deep = mine_ref.shape[0]
    share = piece_refs[0].shape[0]
    row_place, core = place_ref[0], place_ref[1] & 1
    for hop, ref in enumerate(piece_refs):
        start = pl.multiple_of((row_place ^ hop) * share, share)
        near_ref[pl.ds(start, share), :] = ref[...]
    factor = split(factor_ref[...])
    top = split(top_ref[...] + got_ref[...])
    near = near_ref[...] + mult3(top, split(upper_ref[...]), TURNED)
    near = split(mult3(split(near), factor))
    far = split(mult3(split(right_ref[...]), factor, ACROSS))
    for place, prod_ref in ((core, mine_ref), (1 - core, other_ref)):
        block = pl.ds(pl.multiple_of(place * deep, deep), deep)
        change = mult3(split(left_ref[block, :]), near, ACROSS)
        change = change + mult3(split(prod_ref[...]), far, ACROSS)
        out_ref[block, :] = ham_ref[block, :] - change


def base_update(place, hamiltonian, left, mine, other, right, factor, upper, top, got, pieces):
    return pl.pallas_call(
        base_kernel,
        in_specs=[SMEM] + [VMEM] * (9 + len(pieces)),
        out_shape=array(*hamiltonian.shape),
        scratch_shapes=[scratch(*right.shape)],
        compiler_params=LARGE,
        cost_estimate=estimate(4),
        name="base_update",
    )(place, hamiltonian, left, mine, other, right, factor, upper, top, got, *pieces)


def coupling_kernel(base_ref, left_ref, right_ref, factor_ref, parts_ref, out_ref, sum_ref):
    strip = parts_ref.shape[1]
    chips = parts_ref.shape[0] // 2
    for c in range(parts_ref.shape[0]):
        start = ((c % 2) * chips + c // 2) * strip
        sum_ref[start : start + strip, :] = parts_ref[c]
    factor = split(factor_ref[...])
    turn = mult3(split(sum_ref[...]), factor)
    middle = mult3(factor, split(turn), TURNED)
    near = split(mult3(split(right_ref[...]), split(middle)))
    out_ref[...] = base_ref[...] + mult3(split(left_ref[...]), near, ACROSS)


def coupling_update(base, left, right, factor, parts):
    return pl.pallas_call(
        coupling_kernel,
        in_specs=[VMEM] * 5,
        out_shape=array(*base.shape),
        scratch_shapes=[scratch(*factor.shape)],
        compiler_params=LARGE,
        cost_estimate=estimate(3),
        name="coupling_update",
    )(base, left, right, factor, parts)


def hops(values, axis, size, scale=1):
    got = [values[0]]
    for hop in range(1, len(values)):
        pairs = [(i, i ^ (hop * scale)) for i in range(size)]
        got.append(lax.ppermute(values[hop], axis, pairs))
    return got


def pass_on(value, owners, rows, cols):
    hop, having = rows // 2, [0]
    got = jnp.zeros_like(value)
    while hop:
        if having != [0]:
            value = value + got
        pairs = [
            ((owners[c] ^ d) * cols + c, (owners[c] ^ d ^ hop) * cols + c)
            for c in range(cols)
            for d in having
        ]
        got = lax.ppermute(value, ("row", "col"), pairs)
        having = having + [d ^ hop for d in having]
        hop //= 2
    return value, got


def shards(rows, cols, hamiltonian, panel):
    rows_dev, width = panel.shape
    cols_dev = hamiltonian.shape[1]
    row_place = lax.axis_index("row")
    col_place = lax.axis_index("col")
    chips = cols // 2
    strip = width // cols
    piece = rows_dev // cols
    share = cols_dev // rows
    pair = [(i, i ^ 1) for i in range(cols)]
    place = jnp.stack([row_place, col_place]).astype(jnp.int32)

    strips = hops([gram_strips(place, panel, cols)] * rows, "row", rows)

    owners = [c * cols_dev // rows_dev for c in range(cols)]
    owner = col_place * cols_dev // rows_dev
    offset = col_place * cols_dev - owner * rows_dev
    slab = lax.dynamic_slice_in_dim(panel, offset, cols_dev, 0)
    slab = jnp.where(row_place == owner, slab, 0.0)
    strips, slab = lax.optimization_barrier((strips, slab))
    slab, got = pass_on(slab, owners, rows, cols)

    gram = trade(sum_copies(cols, strips, 0, strip))
    first_upper, first_inv = cholesky(gram)
    half, half_cols, gram2_strip = half_stage(place, panel, slab, got, first_inv, cols)
    gram2_strips = hops([gram2_strip] * rows, "row", rows)
    gram2 = trade(sum_copies(cols, gram2_strips, 0, strip))

    half, _ = lax.optimization_barrier((half, gram2_strips[-1]))
    ham_top, near_pieces = near_rows(place, hamiltonian, half, rows)
    gram2, near_pieces = lax.optimization_barrier((gram2, near_pieces))
    near_pieces = hops(near_pieces, "row", rows)
    second_upper = near_cholesky(gram2.reshape(width, width))
    second_upper, near_pieces = lax.optimization_barrier((second_upper, near_pieces))

    left, right, keep, send = products(place, hamiltonian, half, half_cols, second_upper, cols)
    got = lax.ppermute(send, "col", pair)
    near_pieces, _ = lax.optimization_barrier((near_pieces, left))
    near_piece = tree_sum(near_pieces)
    got, near_piece = lax.optimization_barrier((got, near_piece))
    near_pieces = hops([near_piece] * rows, "row", rows)
    totals = pair_add(keep, got)
    ham_top, _ = lax.optimization_barrier((ham_top, totals[0]))
    ham_top, top_got = pass_on(ham_top, [0] * cols, rows, cols)
    totals = hops(totals, "col", cols, 2)
    late = lax.optimization_barrier(tuple(strips) + (totals[0],))
    top = sum_copies(cols, late[:-1], strip, 2 * strip)
    totals, top, near_pieces = lax.optimization_barrier((totals, top, near_pieces))
    top = trade(top)
    mine, coupling_strip = sum_pieces(totals, piece)
    coupling_strips = hops([coupling_strip] * rows, "row", rows)
    mine = merge(place, hops([mine] * chips, "col", cols, 2))
    other = lax.ppermute(mine, "col", pair)
    factor, band_block = compact_factor(gram2, top, first_inv, second_upper, first_upper)
    coupling = trade(sum_copies(cols, coupling_strips, 0, strip))
    base = base_update(place, hamiltonian, left, mine, other, right, factor, second_upper,
                       ham_top, top_got, near_pieces)
    updated = coupling_update(base, left, right, factor, coupling)
    return (updated, band_block)


def solution(mesh):
    in_specs = (P("row", "col"), P("row", None))
    out_specs = (P("row", "col"), P())
    body = functools.partial(shards, mesh.shape["row"], mesh.shape["col"])
    return jax.shard_map(body, mesh=mesh, in_specs=in_specs, out_specs=out_specs, check_vma=False)
```

```python
import functools

import jax
import jax.numpy as jnp
from jax import lax
from jax.experimental import pallas as pl
from jax.experimental.pallas import tpu as pltpu
from jax.sharding import PartitionSpec as P

SUB = 8
LANE = 128
BLOCK = 32
HIGHEST = lax.Precision.HIGHEST
SMALL = pltpu.CompilerParams(vmem_limit_bytes=10 * 2**20)
LARGE = pltpu.CompilerParams(vmem_limit_bytes=24 * 2**20)
VMEM = pl.BlockSpec(memory_space=pltpu.VMEM)
SMEM = pl.BlockSpec(memory_space=pltpu.SMEM)
PLAIN = ((1,), (0,))
TURNED = ((0,), (0,))
ACROSS = ((1,), (1,))


def mult(left, right, dims=PLAIN):
    return lax.dot_general(
        left, right, (dims, ((), ())), precision=HIGHEST, preferred_element_type=jnp.float32
    )


def split(value):
    high = value.astype(jnp.bfloat16)
    return high, (value - high.astype(jnp.float32)).astype(jnp.bfloat16)


def mult3(left, right, dims=PLAIN):
    def one(a, b):
        return lax.dot_general(a, b, (dims, ((), ())), preferred_element_type=jnp.float32)

    return one(left[0], right[0]) + (one(left[0], right[1]) + one(left[1], right[0]))


def chol_kernel(gram_ref, upper_ref, inv_ref, work_ref):
    size = gram_ref.shape[0]
    tiles = size // LANE
    groups = BLOCK // SUB
    lanes = lax.broadcasted_iota(jnp.int32, (SUB, LANE), 1)
    work_ref[...] = gram_ref[...]

    def spread(row):
        return jnp.broadcast_to(row, (SUB, LANE))

    for first in range(0, size, BLOCK):
        rows = [
            [
                work_ref[first + SUB * g : first + SUB * (g + 1), LANE * t : LANE * (t + 1)]
                for t in range(tiles)
            ]
            for g in range(groups)
        ]
        for g in range(groups):
            col = first + SUB * g
            home, low = divmod(col, LANE)
            in_block = (lanes >= low) & (lanes < low + SUB)
            flat = [[spread(rows[g][t][k : k + 1, :]) for t in range(tiles)] for k in range(SUB)]
            diag = [
                [spread(flat[k][home][:, low + i : low + i + 1]) for i in range(k + 1)]
                for k in range(SUB)
            ]
            unit = [jnp.where(lanes == low + k, 1.0, 0.0) for k in range(SUB)]
            later = range(g + 1, groups)
            cols = {
                q: [spread(rows[q][home][:, low + i : low + i + 1]) for i in range(SUB)]
                for q in later
            }
            for q in later:
                rows[q][home] = jnp.where(in_block, 0.0, rows[q][home])
            for i in range(SUB):
                recip = 1.0 / diag[i][i]
                steps = [None] * SUB
                for k in range(i + 1, SUB):
                    steps[k] = diag[k][i] * recip
                for k in range(i + 1, SUB):
                    for j in range(i + 1, k + 1):
                        diag[k][j] = diag[k][j] - steps[k] * diag[j][i]
                for k in range(i + 1, SUB):
                    for t in range(tiles):
                        flat[k][t] = flat[k][t] - steps[k] * flat[i][t]
                    unit[k] = unit[k] - steps[k] * unit[i]
                for q in later:
                    step = cols[q][i] * recip
                    for j in range(i + 1, SUB):
                        cols[q][j] = cols[q][j] - step * diag[j][i]
                    for t in range(tiles):
                        source = flat[i][t]
                        if t == home:
                            source = jnp.where(in_block, unit[i], source)
                        rows[q][t] = rows[q][t] - step * source
            for k in range(SUB):
                scale = lax.rsqrt(diag[k][k])
                for t in range(tiles):
                    scaled = flat[k][t] * scale
                    if t < home:
                        up, inv = jnp.zeros_like(scaled), scaled
                    elif t > home:
                        up, inv = scaled, jnp.zeros_like(scaled)
                    else:
                        up = jnp.where(lanes >= low + k, scaled, 0.0)
                        inv = jnp.where(in_block, unit[k] * scale, scaled)
                        inv = jnp.where(lanes < low + SUB, inv, 0.0)
                    upper_ref[col + k : col + k + 1, LANE * t : LANE * (t + 1)] = up[0:1]
                    inv_ref[col + k : col + k + 1, LANE * t : LANE * (t + 1)] = inv[0:1]
        rest = first + BLOCK
        if rest == size:
            break
        start = rest // LANE * LANE
        left = upper_ref[first:rest, start:size]
        wide = lax.broadcasted_iota(jnp.int32, (BLOCK, size), 1)
        right = jnp.where(wide < rest, inv_ref[first:rest, :], upper_ref[first:rest, :])
        change = mult(left, right, ((0,), (0,)))
        below = lax.broadcasted_iota(jnp.int32, (size - rest, size), 1)
        old = jnp.where((below >= first) & (below < rest), 0.0, work_ref[rest:size, :])
        work_ref[rest:size, :] = old - change[rest - start :, :]


def estimate(micros):
    return pl.CostEstimate(flops=int(micros * 1e9), bytes_accessed=int(micros * 3e6), transcendentals=0)


def square(size):
    return jax.ShapeDtypeStruct((size, size), jnp.float32)


def first_kernel(parts_ref, upper_ref, inv_ref, gram_ref, work_ref):
    strip = parts_ref.shape[1]
    for c in range(parts_ref.shape[0]):
        gram_ref[c * strip : (c + 1) * strip, :] = parts_ref[c]
    chol_kernel(gram_ref, upper_ref, inv_ref, work_ref)


def cholesky(parts):
    size = parts.shape[2]
    return pl.pallas_call(
        first_kernel,
        in_specs=[VMEM],
        out_shape=(square(size), square(size)),
        scratch_shapes=[pltpu.VMEM((size, size), jnp.float32)] * 2,
        compiler_params=SMALL,
        cost_estimate=estimate(10),
        name="cholesky_inverse",
    )(parts)


def grids(size):
    row = lax.broadcasted_iota(jnp.int32, (size, size), 0)
    col = lax.broadcasted_iota(jnp.int32, (size, size), 1)
    return row, col


def near_kernel(gram_ref, upper_ref, inv_ref, work_ref):
    size = gram_ref.shape[0]
    row, col = grids(size)
    ident = jnp.where(row == col, 1.0, 0.0)
    weight = jnp.where(row > col, 1.0, ident * 0.5)
    gram = split(gram_ref[...])

    def look(inv):
        halves = split(inv)
        upper = mult3(halves, gram)
        low = weight * (mult3(split(upper), halves, ACROSS) - ident)
        return upper, low, jnp.sum(low * low)

    def more(state):
        count, _, _, _, worst = state
        return jnp.logical_not(worst < 1e-8) & (count < 10)

    def step(state):
        count, inv, _, low, _ = state
        low = split(low)
        turn = mult3(low, split(inv))
        inv = inv - turn + mult3(low, split(turn))
        return (count + 1, inv) + look(inv)

    low = weight * (gram_ref[...] - ident)
    halves = split(low)
    inv = ident - low + mult3(halves, halves)
    state = lax.while_loop(more, step, (jnp.int32(0), inv) + look(inv))
    _, _, upper, low, worst = state
    upper = upper + mult3(split(low), split(upper), TURNED)
    upper_ref[...] = jnp.where(row <= col, upper, 0.0)

    @pl.when(jnp.logical_not(worst < 1e-8))
    def _():
        chol_kernel(gram_ref, upper_ref, inv_ref, work_ref)


def near_cholesky(gram):
    size = gram.shape[0]
    return pl.pallas_call(
        near_kernel,
        out_shape=square(size),
        scratch_shapes=[pltpu.VMEM((size, size), jnp.float32)] * 2,
        compiler_params=SMALL,
        cost_estimate=estimate(3),
        name="near_cholesky",
    )(gram)


def factor_kernel(gram_ref, top_ref, inv_ref, upper_ref, first_ref, out_ref, band_ref):
    size = inv_ref.shape[0]
    row, col = grids(size)
    ident = jnp.where(row == col, 1.0, 0.0)
    band_ref[...] = -mult(upper_ref[...], first_ref[...])
    top = top_ref[...].reshape(size, size)
    half_top = mult(top, inv_ref[...], ACROSS)
    mat = gram_ref[...].reshape(size, size) + mult3(split(half_top), split(upper_ref[...]), TURNED)
    halves = split(mat)

    def residual(guess):
        return ident - mult3(halves, split(guess))

    def step(state):
        count, guess, rest, _ = state
        guess = guess + mult3(split(guess), split(rest))
        rest = residual(guess)
        return count + 1, guess, rest, jnp.max(jnp.abs(rest))

    def more(state):
        count, _, _, worst = state
        return (worst > 2e-5) & (count < 40)

    guess = 0.5 * ident
    rest = ident - 0.5 * mat
    for _ in range(4):
        parts = split(rest)
        guess = guess + mult3(split(guess), parts)
        rest = mult3(parts, parts)
    guess = guess + mult3(split(guess), split(rest))
    rest = residual(guess)
    state = (jnp.int32(0), guess, rest, jnp.max(jnp.abs(rest)))
    out_ref[...] = lax.while_loop(more, step, state)[1]


def compact_factor(gram, top, inv, upper, first):
    return pl.pallas_call(
        factor_kernel,
        out_shape=(square(inv.shape[0]), square(inv.shape[0])),
        compiler_params=SMALL,
        cost_estimate=estimate(4),
        name="compact_factor",
    )(gram, top, inv, upper, first)


def array(*dims):
    return jax.ShapeDtypeStruct(dims, jnp.float32)


def scratch(*dims):
    return pltpu.VMEM(dims, jnp.float32)


def gram_kernel(place_ref, panel_ref, out_ref, gram_ref):
    strip = out_ref.shape[0] // 2
    mine = pl.ds(pl.multiple_of(place_ref[1] * strip, strip), strip)
    gram_ref[...] = mult(panel_ref[...], panel_ref[...], TURNED)
    out_ref[:strip, :] = gram_ref[mine, :]
    out_ref[strip:, :] = panel_ref[mine, :] * jnp.where(place_ref[0] == 0, 1.0, 0.0)


def gram_strips(place, panel, cols):
    width = panel.shape[1]
    return pl.pallas_call(
        gram_kernel,
        in_specs=[SMEM, VMEM],
        out_shape=array(2 * width // cols, width),
        scratch_shapes=[scratch(width, width)],
        compiler_params=LARGE,
        cost_estimate=estimate(2),
        name="gram_strips",
    )(place, panel)


def half_kernel(place_ref, panel_ref, slab_ref, got_ref, inv_ref, half_ref, cols_ref, out_ref, gram_ref):
    strip = out_ref.shape[0]
    mine = pl.ds(pl.multiple_of(place_ref[1] * strip, strip), strip)
    half = mult(panel_ref[...], inv_ref[...], ACROSS)
    half_ref[...] = half
    parts = split(half)
    gram_ref[...] = mult3(parts, parts, TURNED)
    out_ref[...] = gram_ref[mine, :]
    cols_ref[...] = mult(slab_ref[...] + got_ref[...], inv_ref[...], ACROSS)


def half_stage(place, panel, slab, got, inv, cols):
    width = panel.shape[1]
    return pl.pallas_call(
        half_kernel,
        in_specs=[SMEM] + [VMEM] * 4,
        out_shape=(array(*panel.shape), array(*slab.shape), array(width // cols, width)),
        scratch_shapes=[scratch(width, width)],
        compiler_params=LARGE,
        cost_estimate=estimate(3),
        name="half_stage",
    )(place, panel, slab, got, inv)


def store_pieces(place_ref, whole_ref, piece_refs):
    share = piece_refs[0].shape[0]
    for hop, ref in enumerate(piece_refs):
        start = pl.multiple_of((place_ref[0] ^ hop) * share, share)
        ref[...] = whole_ref[pl.ds(start, share), :]


def top_rows_kernel(place_ref, ham_ref, *rest_refs):
    top_ref = rest_refs[-1]
    lead = jnp.where(place_ref[0] == 0, 1.0, 0.0)
    top_ref[...] = ham_ref[: top_ref.shape[1], :].T * lead
    store_pieces(place_ref, top_ref, rest_refs[:-1])


def near_rows_kernel(place_ref, ham_ref, half_ref, *rest_refs):
    near_ref = rest_refs[-1]
    near_ref[...] = mult3(split(ham_ref[...]), split(half_ref[...]), TURNED)
    store_pieces(place_ref, near_ref, rest_refs[:-1])


def row_pieces(kernel, name, cols_dev, width, rows, place, *operands):
    return pl.pallas_call(
        kernel,
        in_specs=[SMEM] + [VMEM] * len(operands),
        out_shape=(array(cols_dev // rows, width),) * rows,
        scratch_shapes=[scratch(cols_dev, width)],
        compiler_params=LARGE,
        cost_estimate=estimate(1 if len(operands) == 1 else 2),
        name=name,
    )(place, *operands)


def near_sum_kernel(upper_ref, *refs):
    terms, out_ref = refs[:-1], refs[-1]
    count = len(terms) // 2
    total = tree_sum([ref[...] for ref in terms[:count]])
    top = tree_sum([ref[...] for ref in terms[count:]])
    out_ref[...] = total + mult3(split(top), split(upper_ref[...]))


def near_sum(upper, terms, tops):
    return pl.pallas_call(
        near_sum_kernel,
        out_shape=array(*terms[0].shape),
        compiler_params=LARGE,
        cost_estimate=estimate(1),
        name="near_sum",
    )(upper, *terms, *tops)


def products_kernel(place_ref, ham_ref, half_ref, cols_ref, upper_ref,
                    left_ref, right_ref, keep_ref, send_ref, part_ref, coupling_ref):
    width = upper_ref.shape[0]
    chips = keep_ref.shape[0]
    rows_dev = ham_ref.shape[0]
    piece, strip = rows_dev // 2 // chips, width // 2 // chips
    row_place, col_place = place_ref[0], place_ref[1]
    core, chip = col_place & 1, col_place // 2
    lead = jnp.where(col_place == 0, 1.0, 0.0)
    right_ref[...] = cols_ref[...]
    right_ref[:width, :] = cols_ref[:width, :] + lead * upper_ref[...]
    part = mult3(split(ham_ref[...]), split(right_ref[...]))
    part_ref[...] = part
    lead = jnp.where(row_place == 0, 1.0, 0.0)
    left_ref[...] = half_ref[...]
    left_ref[:width, :] = half_ref[:width, :] + lead * upper_ref[...]
    coupling_ref[...] = mult3(split(left_ref[...]), split(part), TURNED)
    for ref, half in ((send_ref, 1 - core), (keep_ref, core)):
        for hop in range(chips):
            start = (half * chips + (chip ^ hop)) * piece
            ref[hop, :piece, :] = part_ref[pl.ds(pl.multiple_of(start, piece), piece), :]
            start = (half * chips + (chip ^ hop)) * strip
            ref[hop, piece:, :] = coupling_ref[pl.ds(pl.multiple_of(start, strip), strip), :]


def products(place, hamiltonian, half, half_cols, upper, cols):
    rows_dev, cols_dev = hamiltonian.shape
    width = upper.shape[0]
    chips = cols // 2
    share = (rows_dev + width) // cols
    return pl.pallas_call(
        products_kernel,
        in_specs=[SMEM] + [VMEM] * 4,
        out_shape=(
            array(rows_dev, width),
            array(cols_dev, width),
            array(chips, share, width),
            array(chips, share, width),
        ),
        scratch_shapes=[scratch(rows_dev, width), scratch(width, width)],
        compiler_params=LARGE,
        cost_estimate=estimate(4),
        name="products",
    )(place, hamiltonian, half, half_cols, upper)


def pair_kernel(keep_ref, got_ref, *out_refs):
    for hop, ref in enumerate(out_refs):
        ref[...] = keep_ref[hop] + got_ref[hop]


def pair_add(keep, got):
    return pl.pallas_call(
        pair_kernel,
        in_specs=[VMEM] * 2,
        out_shape=(array(*keep.shape[1:]),) * keep.shape[0],
        compiler_params=LARGE,
        cost_estimate=estimate(0.5),
        name="pair_add",
    )(keep, got)


def tree_sum(terms):
    while len(terms) > 1:
        terms = [terms[i] + terms[i + 1] for i in range(0, len(terms), 2)]
    return terms[0]


def sums_kernel(*refs):
    mine_ref, strip_ref = refs[-2:]
    piece = mine_ref.shape[0]
    total = tree_sum([ref[...] for ref in refs[:-2]])
    mine_ref[...] = total[:piece]
    strip_ref[...] = total[piece:]


def sum_pieces(totals, piece):
    height, width = totals[0].shape
    return pl.pallas_call(
        sums_kernel,
        out_shape=(array(piece, width), array(height - piece, width)),
        compiler_params=LARGE,
        cost_estimate=estimate(0.5),
        name="sum_pieces",
    )(*totals)


def spread_kernel(first, last, *refs):
    out_ref = refs[-1]
    total = tree_sum([ref[first:last, :] for ref in refs[:-1]])
    for c in range(out_ref.shape[0]):
        out_ref[c] = total


def sum_copies(cols, terms, first, last):
    return pl.pallas_call(
        functools.partial(spread_kernel, first, last),
        in_specs=[VMEM] * len(terms),
        out_shape=array(cols, last - first, terms[0].shape[1]),
        compiler_params=LARGE,
        cost_estimate=estimate(0.5),
        name="sum_copies",
    )(*terms)


def trade(copies):
    return lax.all_to_all(copies, "col", 0, 0, tiled=True)


def merge_kernel(place_ref, *refs):
    out_ref = refs[-1]
    piece = refs[0].shape[0]
    chip = place_ref[1] // 2
    for hop, ref in enumerate(refs[:-1]):
        out_ref[pl.ds(pl.multiple_of((chip ^ hop) * piece, piece), piece), :] = ref[...]


def merge(place, pieces):
    piece, width = pieces[0].shape
    return pl.pallas_call(
        merge_kernel,
        in_specs=[SMEM] + [VMEM] * len(pieces),
        out_shape=array(len(pieces) * piece, width),
        compiler_params=LARGE,
        cost_estimate=estimate(0.5),
        name="merge_pieces",
    )(place, *pieces)


def update_kernel(
    place_ref, ham_ref, left_ref, mine_ref, other_ref, right_ref, factor_ref,
    parts_ref, *rest_refs
):
    piece_refs, (out_ref, near_ref, sum_ref) = rest_refs[:-3], rest_refs[-3:]
    deep = mine_ref.shape[0]
    share = piece_refs[0].shape[0]
    row_place, core = place_ref[0], place_ref[1] & 1
    for hop, ref in enumerate(piece_refs):
        start = pl.multiple_of((row_place ^ hop) * share, share)
        near_ref[pl.ds(start, share), :] = ref[...]
    strip = parts_ref.shape[1]
    chips = parts_ref.shape[0] // 2
    for c in range(parts_ref.shape[0]):
        start = ((c % 2) * chips + c // 2) * strip
        sum_ref[start : start + strip, :] = parts_ref[c]
    factor = split(factor_ref[...])
    right = split(right_ref[...])
    turn = mult3(split(sum_ref[...]), factor)
    middle = mult3(factor, split(turn), TURNED)
    near = split(mult3(split(near_ref[...]), factor) - mult3(right, split(middle)))
    far = split(mult3(right, factor, ACROSS))
    for place, prod_ref in ((core, mine_ref), (1 - core, other_ref)):
        block = pl.ds(pl.multiple_of(place * deep, deep), deep)
        change = mult3(split(left_ref[block, :]), near, ACROSS)
        change = change + mult3(split(prod_ref[...]), far, ACROSS)
        out_ref[block, :] = ham_ref[block, :] - change


def update(place, hamiltonian, left, mine, other, right, factor, parts, pieces):
    return pl.pallas_call(
        update_kernel,
        in_specs=[SMEM] + [VMEM] * (7 + len(pieces)),
        out_shape=array(*hamiltonian.shape),
        scratch_shapes=[scratch(*right.shape), scratch(*factor.shape)],
        compiler_params=LARGE,
        cost_estimate=estimate(4),
        name="two_sided_update",
    )(place, hamiltonian, left, mine, other, right, factor, parts, *pieces)


def hops(values, axis, size, scale=1):
    got = [values[0]]
    for hop in range(1, len(values)):
        pairs = [(i, i ^ (hop * scale)) for i in range(size)]
        got.append(lax.ppermute(values[hop], axis, pairs))
    return got


def pass_on(value, owners, rows, cols):
    hop, having = rows // 2, [0]
    got = jnp.zeros_like(value)
    while hop:
        if having != [0]:
            value = value + got
        pairs = [
            ((owners[c] ^ d) * cols + c, (owners[c] ^ d ^ hop) * cols + c)
            for c in range(cols)
            for d in having
        ]
        got = lax.ppermute(value, ("row", "col"), pairs)
        having = having + [d ^ hop for d in having]
        hop //= 2
    return value, got


def shards(rows, cols, hamiltonian, panel):
    rows_dev, width = panel.shape
    cols_dev = hamiltonian.shape[1]
    row_place = lax.axis_index("row")
    col_place = lax.axis_index("col")
    chips = cols // 2
    strip = width // cols
    piece = rows_dev // cols
    share = cols_dev // rows
    pair = [(i, i ^ 1) for i in range(cols)]
    place = jnp.stack([row_place, col_place]).astype(jnp.int32)

    strips = hops([gram_strips(place, panel, cols)] * rows, "row", rows)

    owners = [c * cols_dev // rows_dev for c in range(cols)]
    owner = col_place * cols_dev // rows_dev
    offset = col_place * cols_dev - owner * rows_dev
    slab = lax.dynamic_slice_in_dim(panel, offset, cols_dev, 0)
    slab = jnp.where(row_place == owner, slab, 0.0)
    strips, slab = lax.optimization_barrier((strips, slab))
    slab, got = pass_on(slab, owners, rows, cols)

    block, _ = lax.optimization_barrier((hamiltonian, slab))
    near_tops = row_pieces(
        top_rows_kernel, "top_rows", cols_dev, width, rows, place, block
    )
    near_tops = hops(near_tops, "row", rows)

    gram = trade(sum_copies(cols, strips, 0, strip))
    first_upper, first_inv = cholesky(gram)
    first_inv, near_tops = lax.optimization_barrier((first_inv, near_tops))
    half, half_cols, gram2_strip = half_stage(place, panel, slab, got, first_inv, cols)
    gram2_strips = hops([gram2_strip] * rows, "row", rows)
    gram2 = trade(sum_copies(cols, gram2_strips, 0, strip))

    half, _ = lax.optimization_barrier((half, gram2_strips[-1]))
    near_pieces = row_pieces(
        near_rows_kernel, "near_rows", cols_dev, width, rows, place, hamiltonian, half
    )
    gram2, _ = lax.optimization_barrier((gram2, near_pieces[0]))
    near_pieces = hops(near_pieces, "row", rows)
    second_upper = near_cholesky(gram2.reshape(width, width))
    second_upper, near_pieces = lax.optimization_barrier((second_upper, near_pieces))

    left, right, keep, send = products(place, hamiltonian, half, half_cols, second_upper, cols)
    got = lax.ppermute(send, "col", pair)
    near_pieces, _ = lax.optimization_barrier((near_pieces, left))
    near_piece = near_sum(second_upper, near_pieces, near_tops)
    got, near_piece = lax.optimization_barrier((got, near_piece))
    near_pieces = hops([near_piece] * rows, "row", rows)
    totals = pair_add(keep, got)
    totals = hops(totals, "col", cols, 2)
    late = lax.optimization_barrier(tuple(strips) + (totals[0],))
    top = sum_copies(cols, late[:-1], strip, 2 * strip)
    totals, top, near_pieces = lax.optimization_barrier((totals, top, near_pieces))
    top = trade(top)
    mine, coupling_strip = sum_pieces(totals, piece)
    coupling_strips = hops([coupling_strip] * rows, "row", rows)
    mine = hops([mine] * chips, "col", cols, 2)
    coupling = sum_copies(cols, coupling_strips, 0, strip)
    mine, _ = lax.optimization_barrier((mine, coupling))
    coupling = trade(coupling)
    mine = merge(place, mine)
    top, mine = lax.optimization_barrier((top, mine))
    other = lax.ppermute(mine, "col", pair)
    factor, band_block = compact_factor(gram2, top, first_inv, second_upper, first_upper)
    updated = update(place, hamiltonian, left, mine, other, right, factor, coupling,
                     near_pieces)
    return (updated, band_block)


def solution(mesh):
    in_specs = (P("row", "col"), P("row", None))
    out_specs = (P("row", "col"), P())
    body = functools.partial(shards, mesh.shape["row"], mesh.shape["col"])
    return jax.shard_map(body, mesh=mesh, in_specs=in_specs, out_specs=out_specs, check_vma=False)
```

```python
import functools

import jax
import jax.numpy as jnp
from jax import lax
from jax.experimental import pallas as pl
from jax.experimental.pallas import tpu as pltpu
from jax.sharding import PartitionSpec as P

SUB = 8
LANE = 128
BLOCK = 32
HIGHEST = lax.Precision.HIGHEST
SMALL = pltpu.CompilerParams(vmem_limit_bytes=10 * 2**20)
LARGE = pltpu.CompilerParams(vmem_limit_bytes=24 * 2**20)
VMEM = pl.BlockSpec(memory_space=pltpu.VMEM)
SMEM = pl.BlockSpec(memory_space=pltpu.SMEM)
HBM = pl.BlockSpec(memory_space=pltpu.HBM)
PLAIN = ((1,), (0,))
TURNED = ((0,), (0,))
ACROSS = ((1,), (1,))


def mult(left, right, dims=PLAIN):
    return lax.dot_general(
        left, right, (dims, ((), ())), precision=HIGHEST, preferred_element_type=jnp.float32
    )


def move(pairs, sems):
    copies = [pltpu.make_async_copy(src, dst, sems.at[i]) for i, (src, dst) in enumerate(pairs)]
    for copy in copies:
        copy.start()
    return copies


def wait(copies):
    for copy in copies:
        copy.wait()


def split(value):
    high = value.astype(jnp.bfloat16)
    return high, (value - high.astype(jnp.float32)).astype(jnp.bfloat16)


def mult3(left, right, dims=PLAIN):
    def one(a, b):
        return lax.dot_general(a, b, (dims, ((), ())), preferred_element_type=jnp.float32)

    return one(left[0], right[0]) + (one(left[0], right[1]) + one(left[1], right[0]))


def chol_kernel(gram_ref, upper_ref, inv_ref, work_ref):
    size = gram_ref.shape[0]
    tiles = size // LANE
    groups = BLOCK // SUB
    lanes = lax.broadcasted_iota(jnp.int32, (SUB, LANE), 1)
    work_ref[...] = gram_ref[...]

    def spread(row):
        return jnp.broadcast_to(row, (SUB, LANE))

    for first in range(0, size, BLOCK):
        rows = [
            [
                work_ref[first + SUB * g : first + SUB * (g + 1), LANE * t : LANE * (t + 1)]
                for t in range(tiles)
            ]
            for g in range(groups)
        ]
        for g in range(groups):
            col = first + SUB * g
            home, low = divmod(col, LANE)
            in_block = (lanes >= low) & (lanes < low + SUB)
            flat = [[spread(rows[g][t][k : k + 1, :]) for t in range(tiles)] for k in range(SUB)]
            diag = [
                [spread(flat[k][home][:, low + i : low + i + 1]) for i in range(k + 1)]
                for k in range(SUB)
            ]
            unit = [jnp.where(lanes == low + k, 1.0, 0.0) for k in range(SUB)]
            later = range(g + 1, groups)
            cols = {
                q: [spread(rows[q][home][:, low + i : low + i + 1]) for i in range(SUB)]
                for q in later
            }
            for q in later:
                rows[q][home] = jnp.where(in_block, 0.0, rows[q][home])
            for i in range(SUB):
                recip = 1.0 / diag[i][i]
                steps = [None] * SUB
                for k in range(i + 1, SUB):
                    steps[k] = diag[k][i] * recip
                for k in range(i + 1, SUB):
                    for j in range(i + 1, k + 1):
                        diag[k][j] = diag[k][j] - steps[k] * diag[j][i]
                for k in range(i + 1, SUB):
                    for t in range(tiles):
                        flat[k][t] = flat[k][t] - steps[k] * flat[i][t]
                    unit[k] = unit[k] - steps[k] * unit[i]
                for q in later:
                    step = cols[q][i] * recip
                    for j in range(i + 1, SUB):
                        cols[q][j] = cols[q][j] - step * diag[j][i]
                    for t in range(tiles):
                        source = flat[i][t]
                        if t == home:
                            source = jnp.where(in_block, unit[i], source)
                        rows[q][t] = rows[q][t] - step * source
            for k in range(SUB):
                scale = lax.rsqrt(diag[k][k])
                for t in range(tiles):
                    scaled = flat[k][t] * scale
                    if t < home:
                        up, inv = jnp.zeros_like(scaled), scaled
                    elif t > home:
                        up, inv = scaled, jnp.zeros_like(scaled)
                    else:
                        up = jnp.where(lanes >= low + k, scaled, 0.0)
                        inv = jnp.where(in_block, unit[k] * scale, scaled)
                        inv = jnp.where(lanes < low + SUB, inv, 0.0)
                    upper_ref[col + k : col + k + 1, LANE * t : LANE * (t + 1)] = up[0:1]
                    inv_ref[col + k : col + k + 1, LANE * t : LANE * (t + 1)] = inv[0:1]
        rest = first + BLOCK
        if rest == size:
            break
        start = rest // LANE * LANE
        left = upper_ref[first:rest, start:size]
        wide = lax.broadcasted_iota(jnp.int32, (BLOCK, size), 1)
        right = jnp.where(wide < rest, inv_ref[first:rest, :], upper_ref[first:rest, :])
        change = mult(left, right, ((0,), (0,)))
        below = lax.broadcasted_iota(jnp.int32, (size - rest, size), 1)
        old = jnp.where((below >= first) & (below < rest), 0.0, work_ref[rest:size, :])
        work_ref[rest:size, :] = old - change[rest - start :, :]


def estimate(micros):
    return pl.CostEstimate(flops=int(micros * 1e9), bytes_accessed=int(micros * 3e6), transcendentals=0)


def square(size):
    return jax.ShapeDtypeStruct((size, size), jnp.float32)


def first_kernel(parts_ref, upper_ref, inv_ref, gram_ref, work_ref):
    strip = parts_ref.shape[1]
    for c in range(parts_ref.shape[0]):
        gram_ref[c * strip : (c + 1) * strip, :] = parts_ref[c]
    chol_kernel(gram_ref, upper_ref, inv_ref, work_ref)


def cholesky(parts):
    size = parts.shape[2]
    return pl.pallas_call(
        first_kernel,
        in_specs=[VMEM],
        out_shape=(square(size), square(size)),
        scratch_shapes=[pltpu.VMEM((size, size), jnp.float32)] * 2,
        compiler_params=SMALL,
        cost_estimate=estimate(10),
        name="cholesky_inverse",
    )(parts)


def grids(size):
    row = lax.broadcasted_iota(jnp.int32, (size, size), 0)
    col = lax.broadcasted_iota(jnp.int32, (size, size), 1)
    return row, col


def near_kernel(gram_ref, upper_ref, inv_ref, work_ref):
    size = gram_ref.shape[0]
    row, col = grids(size)
    ident = jnp.where(row == col, 1.0, 0.0)
    weight = jnp.where(row > col, 1.0, ident * 0.5)
    gram = split(gram_ref[...])

    def look(inv):
        halves = split(inv)
        upper = mult3(halves, gram)
        low = weight * (mult3(split(upper), halves, ACROSS) - ident)
        return upper, low, jnp.sum(low * low)

    def more(state):
        count, _, _, _, worst = state
        return jnp.logical_not(worst < 1e-8) & (count < 10)

    def step(state):
        count, inv, _, low, _ = state
        low = split(low)
        turn = mult3(low, split(inv))
        inv = inv - turn + mult3(low, split(turn))
        return (count + 1, inv) + look(inv)

    low = weight * (gram_ref[...] - ident)
    halves = split(low)
    inv = ident - low + mult3(halves, halves)
    state = lax.while_loop(more, step, (jnp.int32(0), inv) + look(inv))
    _, _, upper, low, worst = state
    upper = upper + mult3(split(low), split(upper), TURNED)
    upper_ref[...] = jnp.where(row <= col, upper, 0.0)

    @pl.when(jnp.logical_not(worst < 1e-8))
    def _():
        chol_kernel(gram_ref, upper_ref, inv_ref, work_ref)


def near_cholesky(gram):
    size = gram.shape[0]
    return pl.pallas_call(
        near_kernel,
        out_shape=square(size),
        scratch_shapes=[pltpu.VMEM((size, size), jnp.float32)] * 2,
        compiler_params=SMALL,
        cost_estimate=estimate(3),
        name="near_cholesky",
    )(gram)


def factor_kernel(gram_ref, top_ref, inv_ref, upper_ref, first_ref, out_ref, band_ref):
    size = inv_ref.shape[0]
    row, col = grids(size)
    ident = jnp.where(row == col, 1.0, 0.0)
    band_ref[...] = -mult(upper_ref[...], first_ref[...])
    top = top_ref[...].reshape(size, size)
    half_top = mult(top, inv_ref[...], ACROSS)
    mat = gram_ref[...].reshape(size, size) + mult3(split(half_top), split(upper_ref[...]), TURNED)
    halves = split(mat)

    def residual(guess):
        return ident - mult3(halves, split(guess))

    def step(state):
        count, guess, rest, _ = state
        guess = guess + mult3(split(guess), split(rest))
        rest = residual(guess)
        return count + 1, guess, rest, jnp.max(jnp.abs(rest))

    def more(state):
        count, _, _, worst = state
        return (worst > 2e-5) & (count < 40)

    guess = 0.5 * ident
    rest = ident - 0.5 * mat
    for _ in range(4):
        parts = split(rest)
        guess = guess + mult3(split(guess), parts)
        rest = mult3(parts, parts)
    guess = guess + mult3(split(guess), split(rest))
    rest = residual(guess)
    state = (jnp.int32(0), guess, rest, jnp.max(jnp.abs(rest)))
    out_ref[...] = lax.while_loop(more, step, state)[1]


def compact_factor(gram, top, inv, upper, first):
    return pl.pallas_call(
        factor_kernel,
        out_shape=(square(inv.shape[0]), square(inv.shape[0])),
        compiler_params=SMALL,
        cost_estimate=estimate(4),
        name="compact_factor",
    )(gram, top, inv, upper, first)


def array(*dims):
    return jax.ShapeDtypeStruct(dims, jnp.float32)


def scratch(*dims):
    return pltpu.VMEM(dims, jnp.float32)


def gram_kernel(place_ref, panel_ref, out_ref, gram_ref):
    strip = out_ref.shape[0] // 2
    mine = pl.ds(pl.multiple_of(place_ref[1] * strip, strip), strip)
    gram_ref[...] = mult(panel_ref[...], panel_ref[...], TURNED)
    out_ref[:strip, :] = gram_ref[mine, :]
    out_ref[strip:, :] = panel_ref[mine, :] * jnp.where(place_ref[0] == 0, 1.0, 0.0)


def gram_strips(place, panel, cols):
    width = panel.shape[1]
    return pl.pallas_call(
        gram_kernel,
        in_specs=[SMEM, VMEM],
        out_shape=array(2 * width // cols, width),
        scratch_shapes=[scratch(width, width)],
        compiler_params=LARGE,
        cost_estimate=estimate(2),
        name="gram_strips",
    )(place, panel)


def half_kernel(place_ref, panel_ref, slab_ref, got_ref, inv_ref, half_out, cols_out, out_ref,
                half_ref, cols_ref, gram_ref, sems):
    strip = out_ref.shape[0]
    mine = pl.ds(pl.multiple_of(place_ref[1] * strip, strip), strip)
    half = mult(panel_ref[...], inv_ref[...], ACROSS)
    half_ref[...] = half
    cols_ref[...] = mult(slab_ref[...] + got_ref[...], inv_ref[...], ACROSS)
    store = move([(half_ref, half_out), (cols_ref, cols_out)], sems)
    parts = split(half)
    gram_ref[...] = mult3(parts, parts, TURNED)
    out_ref[...] = gram_ref[mine, :]
    wait(store)


def half_stage(place, panel, slab, got, inv, cols):
    width = panel.shape[1]
    return pl.pallas_call(
        half_kernel,
        in_specs=[SMEM] + [VMEM] * 4,
        out_specs=(HBM, HBM, VMEM),
        out_shape=(array(*panel.shape), array(*slab.shape), array(width // cols, width)),
        scratch_shapes=[
            scratch(*panel.shape),
            scratch(*slab.shape),
            scratch(width, width),
            pltpu.SemaphoreType.DMA((2,)),
        ],
        compiler_params=LARGE,
        cost_estimate=estimate(3),
        name="half_stage",
    )(place, panel, slab, got, inv)


def products_kernel(place_ref, ham_ref, half_in, cols_in, upper_ref,
                    left_out, right_out, keep_ref, send_ref, *rest_refs):
    piece_refs = rest_refs[:-6]
    left_ref, right_ref, part_ref, coupling_ref, near_ref, sems = rest_refs[-6:]
    fetch = move([(cols_in, right_ref), (half_in, left_ref)], sems)
    width = upper_ref.shape[0]
    chips = keep_ref.shape[0]
    rows_dev = ham_ref.shape[0]
    piece, strip = rows_dev // 2 // chips, width // 2 // chips
    share = piece_refs[0].shape[0]
    row_place, col_place = place_ref[0], place_ref[1]
    core, chip = col_place & 1, col_place // 2
    ham = split(ham_ref[...])
    fetch[0].wait()
    lead = jnp.where(col_place == 0, 1.0, 0.0)
    right_ref[:width, :] = right_ref[:width, :] + lead * upper_ref[...]
    part = mult3(ham, split(right_ref[...]))
    part_ref[...] = part
    fetch[1].wait()
    lead = jnp.where(row_place == 0, 1.0, 0.0)
    left_ref[:width, :] = left_ref[:width, :] + lead * upper_ref[...]
    store = move([(right_ref, right_out), (left_ref, left_out)], sems)
    left = split(left_ref[...])
    coupling_ref[...] = mult3(left, split(part), TURNED)
    for ref, half in ((send_ref, 1 - core), (keep_ref, core)):
        for hop in range(chips):
            start = (half * chips + (chip ^ hop)) * piece
            ref[hop, :piece, :] = part_ref[pl.ds(pl.multiple_of(start, piece), piece), :]
            start = (half * chips + (chip ^ hop)) * strip
            ref[hop, piece:, :] = coupling_ref[pl.ds(pl.multiple_of(start, strip), strip), :]
    near_ref[...] = mult3(ham, left, TURNED)
    for hop, ref in enumerate(piece_refs):
        start = pl.multiple_of((row_place ^ hop) * share, share)
        ref[...] = near_ref[pl.ds(start, share), :]
    wait(store)


def products(place, hamiltonian, half, half_cols, upper, rows, cols):
    rows_dev, cols_dev = hamiltonian.shape
    width = upper.shape[0]
    chips = cols // 2
    share = (rows_dev + width) // cols
    out = pl.pallas_call(
        products_kernel,
        in_specs=[SMEM, VMEM, HBM, HBM, VMEM],
        out_specs=(HBM, HBM) + (VMEM,) * (2 + rows),
        out_shape=(
            array(rows_dev, width),
            array(cols_dev, width),
            array(chips, share, width),
            array(chips, share, width),
        )
        + (array(cols_dev // rows, width),) * rows,
        scratch_shapes=[
            scratch(rows_dev, width),
            scratch(cols_dev, width),
            scratch(rows_dev, width),
            scratch(width, width),
            scratch(cols_dev, width),
            pltpu.SemaphoreType.DMA((2,)),
        ],
        compiler_params=LARGE,
        cost_estimate=estimate(4),
        name="products",
    )(place, hamiltonian, half, half_cols, upper)
    return out[0], out[1], out[2], out[3], out[4:]


def pair_kernel(keep_ref, got_ref, *out_refs):
    for hop, ref in enumerate(out_refs):
        ref[...] = keep_ref[hop] + got_ref[hop]


def pair_add(keep, got):
    return pl.pallas_call(
        pair_kernel,
        in_specs=[VMEM] * 2,
        out_shape=(array(*keep.shape[1:]),) * keep.shape[0],
        compiler_params=LARGE,
        cost_estimate=estimate(0.5),
        name="pair_add",
    )(keep, got)


def tree_sum(terms):
    while len(terms) > 1:
        terms = [terms[i] + terms[i + 1] for i in range(0, len(terms), 2)]
    return terms[0]


def sums_kernel(count, *refs):
    total_refs, piece_refs = refs[:count], refs[count:-2]
    mine_ref, both_ref = refs[-2:]
    piece, share = mine_ref.shape[0], piece_refs[0].shape[0]
    total = tree_sum([ref[...] for ref in total_refs])
    mine_ref[...] = total[:piece]
    both_ref[:share, :] = tree_sum([ref[...] for ref in piece_refs])
    both_ref[share:, :] = total[piece:]


def sum_pieces(totals, pieces, piece):
    share, width = pieces[0].shape
    strip = totals[0].shape[0] - piece
    return pl.pallas_call(
        functools.partial(sums_kernel, len(totals)),
        in_specs=[VMEM] * (len(totals) + len(pieces)),
        out_shape=(array(piece, width), array(share + strip, width)),
        compiler_params=LARGE,
        cost_estimate=estimate(0.5),
        name="sum_pieces",
    )(*totals, *pieces)


def spread_kernel(first, last, *refs):
    out_ref = refs[-1]
    total = tree_sum([ref[first:last, :] for ref in refs[:-1]])
    for c in range(out_ref.shape[0]):
        out_ref[c] = total


def sum_copies(cols, terms, first, last):
    return pl.pallas_call(
        functools.partial(spread_kernel, first, last),
        in_specs=[VMEM] * len(terms),
        out_shape=array(cols, last - first, terms[0].shape[1]),
        compiler_params=LARGE,
        cost_estimate=estimate(0.5),
        name="sum_copies",
    )(*terms)


def trade(copies):
    return lax.all_to_all(copies, "col", 0, 0, tiled=True)


def merge_kernel(place_ref, *refs):
    out_ref = refs[-1]
    piece = refs[0].shape[0]
    chip = place_ref[1] // 2
    for hop, ref in enumerate(refs[:-1]):
        out_ref[pl.ds(pl.multiple_of((chip ^ hop) * piece, piece), piece), :] = ref[...]


def merge(place, pieces):
    piece, width = pieces[0].shape
    return pl.pallas_call(
        merge_kernel,
        in_specs=[SMEM] + [VMEM] * len(pieces),
        out_shape=array(len(pieces) * piece, width),
        compiler_params=LARGE,
        cost_estimate=estimate(0.5),
        name="merge_pieces",
    )(place, *pieces)


def update_kernel(
    place_ref, ham_ref, left_ref, mine_ref, other_ref, right_ref, factor_ref,
    parts_ref, *rest_refs
):
    piece_refs, (out_ref, near_ref, sum_ref) = rest_refs[:-3], rest_refs[-3:]
    deep = mine_ref.shape[0]
    share = near_ref.shape[0] // len(piece_refs)
    row_place, core = place_ref[0], place_ref[1] & 1
    for hop, ref in enumerate(piece_refs):
        start = pl.multiple_of((row_place ^ hop) * share, share)
        near_ref[pl.ds(start, share), :] = ref[:share, :]
    strip = parts_ref.shape[1]
    chips = parts_ref.shape[0] // 2
    for c in range(parts_ref.shape[0]):
        start = ((c % 2) * chips + c // 2) * strip
        sum_ref[start : start + strip, :] = parts_ref[c]
    factor = split(factor_ref[...])
    right = split(right_ref[...])
    turn = mult3(split(sum_ref[...]), factor)
    middle = mult3(factor, split(turn), TURNED)
    near = split(mult3(split(near_ref[...]), factor) - mult3(right, split(middle)))
    far = split(mult3(right, factor, ACROSS))
    for place, prod_ref in ((core, mine_ref), (1 - core, other_ref)):
        block = pl.ds(pl.multiple_of(place * deep, deep), deep)
        change = mult3(split(left_ref[block, :]), near, ACROSS)
        change = change + mult3(split(prod_ref[...]), far, ACROSS)
        out_ref[block, :] = ham_ref[block, :] - change


def update(place, hamiltonian, left, mine, other, right, factor, parts, pieces):
    return pl.pallas_call(
        update_kernel,
        in_specs=[SMEM] + [VMEM] * (7 + len(pieces)),
        out_shape=array(*hamiltonian.shape),
        scratch_shapes=[scratch(*right.shape), scratch(*factor.shape)],
        compiler_params=LARGE,
        cost_estimate=estimate(4),
        name="two_sided_update",
    )(place, hamiltonian, left, mine, other, right, factor, parts, *pieces)


def hops(values, axis, size, scale=1):
    got = [values[0]]
    for hop in range(1, len(values)):
        pairs = [(i, i ^ (hop * scale)) for i in range(size)]
        got.append(lax.ppermute(values[hop], axis, pairs))
    return got


def shards(rows, cols, hamiltonian, panel):
    rows_dev, width = panel.shape
    cols_dev = hamiltonian.shape[1]
    row_place = lax.axis_index("row")
    col_place = lax.axis_index("col")
    chips = cols // 2
    strip = width // cols
    piece = rows_dev // cols
    share = cols_dev // rows
    pair = [(i, i ^ 1) for i in range(cols)]
    place = jnp.stack([row_place, col_place]).astype(jnp.int32)

    strips = hops([gram_strips(place, panel, cols)] * rows, "row", rows)

    owners = [c * cols_dev // rows_dev for c in range(cols)]
    owner = col_place * cols_dev // rows_dev
    offset = col_place * cols_dev - owner * rows_dev
    slab = lax.dynamic_slice_in_dim(panel, offset, cols_dev, 0)
    slab = jnp.where(row_place == owner, slab, 0.0)
    strips, slab = lax.optimization_barrier((strips, slab))
    hop, having = rows // 2, [0]
    got = jnp.zeros_like(slab)
    while hop:
        if having != [0]:
            slab = slab + got
        pairs = [
            ((owners[c] ^ d) * cols + c, (owners[c] ^ d ^ hop) * cols + c)
            for c in range(cols)
            for d in having
        ]
        got = lax.ppermute(slab, ("row", "col"), pairs)
        having = having + [d ^ hop for d in having]
        hop //= 2

    gram = trade(sum_copies(cols, strips, 0, strip))
    first_upper, first_inv = cholesky(gram)
    half, half_cols, gram2_strip = half_stage(place, panel, slab, got, first_inv, cols)
    gram2_strips = hops([gram2_strip] * rows, "row", rows)
    gram2 = trade(sum_copies(cols, gram2_strips, 0, strip))
    second_upper = near_cholesky(gram2.reshape(width, width))

    left, right, keep, send, pieces = products(
        place, hamiltonian, half, half_cols, second_upper, rows, cols
    )
    got = lax.ppermute(send, "col", pair)
    pieces = hops(pieces, "row", rows)
    got, pieces[:3] = lax.optimization_barrier((got, pieces[:3]))
    totals = hops(pair_add(keep, got), "col", cols, 2)

    late = lax.optimization_barrier(tuple(strips) + (totals[0],))
    top = sum_copies(cols, late[:-1], strip, 2 * strip)
    totals, top = lax.optimization_barrier((totals, top))
    top = trade(top)
    mine, both = sum_pieces(totals, pieces, piece)
    both = hops([both] * rows, "row", rows)
    mine, both[1] = lax.optimization_barrier((mine, both[1]))
    factor, band_block = compact_factor(gram2, top, first_inv, second_upper, first_upper)
    both, factor = lax.optimization_barrier((both, factor))
    coupling = sum_copies(cols, both, share, share + strip)
    mine = hops([mine] * chips, "col", cols, 2)
    mine, _ = lax.optimization_barrier((mine, coupling))
    coupling = trade(coupling)
    mine = merge(place, mine)
    other = lax.ppermute(mine, "col", pair)
    updated = update(place, hamiltonian, left, mine, other, right, factor, coupling, both)
    return (updated, band_block)


def solution(mesh):
    in_specs = (P("row", "col"), P("row", None))
    out_specs = (P("row", "col"), P())
    body = functools.partial(shards, mesh.shape["row"], mesh.shape["col"])
    return jax.shard_map(body, mesh=mesh, in_specs=in_specs, out_specs=out_specs, check_vma=False)
```

```python
import functools

import jax
import jax.numpy as jnp
from jax import lax
from jax.experimental import pallas as pl
from jax.experimental.pallas import tpu as pltpu
from jax.sharding import PartitionSpec as P

SUB = 8
LANE = 128
BLOCK = 32
HIGHEST = lax.Precision.HIGHEST
SMALL = pltpu.CompilerParams(vmem_limit_bytes=10 * 2**20)
LARGE = pltpu.CompilerParams(vmem_limit_bytes=24 * 2**20)
VMEM = pl.BlockSpec(memory_space=pltpu.VMEM)
SMEM = pl.BlockSpec(memory_space=pltpu.SMEM)
HBM = pl.BlockSpec(memory_space=pltpu.HBM)
PLAIN = ((1,), (0,))
TURNED = ((0,), (0,))
ACROSS = ((1,), (1,))


def mult(left, right, dims=PLAIN):
    return lax.dot_general(
        left, right, (dims, ((), ())), precision=HIGHEST, preferred_element_type=jnp.float32
    )


def move(pairs, sems):
    copies = [pltpu.make_async_copy(src, dst, sems.at[i]) for i, (src, dst) in enumerate(pairs)]
    for copy in copies:
        copy.start()
    return copies


def wait(copies):
    for copy in copies:
        copy.wait()


def split(value):
    high = value.astype(jnp.bfloat16)
    return high, (value - high.astype(jnp.float32)).astype(jnp.bfloat16)


def mult3(left, right, dims=PLAIN):
    def one(a, b):
        return lax.dot_general(a, b, (dims, ((), ())), preferred_element_type=jnp.float32)

    return one(left[0], right[0]) + (one(left[0], right[1]) + one(left[1], right[0]))


def chol_kernel(gram_ref, upper_ref, inv_ref, work_ref):
    size = gram_ref.shape[0]
    tiles = size // LANE
    groups = BLOCK // SUB
    lanes = lax.broadcasted_iota(jnp.int32, (SUB, LANE), 1)
    work_ref[...] = gram_ref[...]

    def spread(row):
        return jnp.broadcast_to(row, (SUB, LANE))

    for first in range(0, size, BLOCK):
        rows = [
            [
                work_ref[first + SUB * g : first + SUB * (g + 1), LANE * t : LANE * (t + 1)]
                for t in range(tiles)
            ]
            for g in range(groups)
        ]
        for g in range(groups):
            col = first + SUB * g
            home, low = divmod(col, LANE)
            in_block = (lanes >= low) & (lanes < low + SUB)
            flat = [[spread(rows[g][t][k : k + 1, :]) for t in range(tiles)] for k in range(SUB)]
            diag = [
                [spread(flat[k][home][:, low + i : low + i + 1]) for i in range(k + 1)]
                for k in range(SUB)
            ]
            unit = [jnp.where(lanes == low + k, 1.0, 0.0) for k in range(SUB)]
            later = range(g + 1, groups)
            cols = {
                q: [spread(rows[q][home][:, low + i : low + i + 1]) for i in range(SUB)]
                for q in later
            }
            for q in later:
                rows[q][home] = jnp.where(in_block, 0.0, rows[q][home])
            for i in range(SUB):
                recip = 1.0 / diag[i][i]
                steps = [None] * SUB
                for k in range(i + 1, SUB):
                    steps[k] = diag[k][i] * recip
                for k in range(i + 1, SUB):
                    for j in range(i + 1, k + 1):
                        diag[k][j] = diag[k][j] - steps[k] * diag[j][i]
                for k in range(i + 1, SUB):
                    for t in range(tiles):
                        flat[k][t] = flat[k][t] - steps[k] * flat[i][t]
                    unit[k] = unit[k] - steps[k] * unit[i]
                for q in later:
                    step = cols[q][i] * recip
                    for j in range(i + 1, SUB):
                        cols[q][j] = cols[q][j] - step * diag[j][i]
                    for t in range(tiles):
                        source = flat[i][t]
                        if t == home:
                            source = jnp.where(in_block, unit[i], source)
                        rows[q][t] = rows[q][t] - step * source
            for k in range(SUB):
                scale = lax.rsqrt(diag[k][k])
                for t in range(tiles):
                    scaled = flat[k][t] * scale
                    if t < home:
                        up, inv = jnp.zeros_like(scaled), scaled
                    elif t > home:
                        up, inv = scaled, jnp.zeros_like(scaled)
                    else:
                        up = jnp.where(lanes >= low + k, scaled, 0.0)
                        inv = jnp.where(in_block, unit[k] * scale, scaled)
                        inv = jnp.where(lanes < low + SUB, inv, 0.0)
                    upper_ref[col + k : col + k + 1, LANE * t : LANE * (t + 1)] = up[0:1]
                    inv_ref[col + k : col + k + 1, LANE * t : LANE * (t + 1)] = inv[0:1]
        rest = first + BLOCK
        if rest == size:
            break
        start = rest // LANE * LANE
        left = upper_ref[first:rest, start:size]
        wide = lax.broadcasted_iota(jnp.int32, (BLOCK, size), 1)
        right = jnp.where(wide < rest, inv_ref[first:rest, :], upper_ref[first:rest, :])
        change = mult(left, right, ((0,), (0,)))
        below = lax.broadcasted_iota(jnp.int32, (size - rest, size), 1)
        old = jnp.where((below >= first) & (below < rest), 0.0, work_ref[rest:size, :])
        work_ref[rest:size, :] = old - change[rest - start :, :]


def estimate(micros):
    return pl.CostEstimate(flops=int(micros * 1e9), bytes_accessed=int(micros * 3e6), transcendentals=0)


def square(size):
    return jax.ShapeDtypeStruct((size, size), jnp.float32)


def first_kernel(parts_ref, upper_out, inv_ref, gram_ref, upper_ref, work_ref, sems):
    strip = parts_ref.shape[1]
    for c in range(parts_ref.shape[0]):
        gram_ref[c * strip : (c + 1) * strip, :] = parts_ref[c]
    chol_kernel(gram_ref, upper_ref, inv_ref, work_ref)
    wait(move([(upper_ref, upper_out)], sems))


def cholesky(parts):
    size = parts.shape[2]
    return pl.pallas_call(
        first_kernel,
        in_specs=[VMEM],
        out_specs=(HBM, VMEM),
        out_shape=(square(size), square(size)),
        scratch_shapes=[pltpu.VMEM((size, size), jnp.float32)] * 3 + [pltpu.SemaphoreType.DMA((1,))],
        compiler_params=SMALL,
        cost_estimate=estimate(10),
        name="cholesky_inverse",
    )(parts)


def grids(size):
    row = lax.broadcasted_iota(jnp.int32, (size, size), 0)
    col = lax.broadcasted_iota(jnp.int32, (size, size), 1)
    return row, col


def near_kernel(gram_ref, upper_ref, inv_ref, work_ref):
    size = gram_ref.shape[0]
    row, col = grids(size)
    ident = jnp.where(row == col, 1.0, 0.0)
    weight = jnp.where(row > col, 1.0, ident * 0.5)
    gram = split(gram_ref[...])

    def look(inv):
        halves = split(inv)
        upper = mult3(halves, gram)
        low = weight * (mult3(split(upper), halves, ACROSS) - ident)
        return upper, low, jnp.sum(low * low)

    def more(state):
        count, _, _, _, worst = state
        return jnp.logical_not(worst < 1e-8) & (count < 10)

    def step(state):
        count, inv, _, low, _ = state
        low = split(low)
        turn = mult3(low, split(inv))
        inv = inv - turn + mult3(low, split(turn))
        return (count + 1, inv) + look(inv)

    low = weight * (gram_ref[...] - ident)
    halves = split(low)
    inv = ident - low + mult3(halves, halves)
    state = lax.while_loop(more, step, (jnp.int32(0), inv) + look(inv))
    _, _, upper, low, worst = state
    upper = upper + mult3(split(low), split(upper), TURNED)
    upper_ref[...] = jnp.where(row <= col, upper, 0.0)

    @pl.when(jnp.logical_not(worst < 1e-8))
    def _():
        chol_kernel(gram_ref, upper_ref, inv_ref, work_ref)


def near_cholesky(gram):
    size = gram.shape[0]
    return pl.pallas_call(
        near_kernel,
        out_shape=square(size),
        scratch_shapes=[pltpu.VMEM((size, size), jnp.float32)] * 2,
        compiler_params=SMALL,
        cost_estimate=estimate(3),
        name="near_cholesky",
    )(gram)


def factor_kernel(parts_ref, inv_ref, upper_ref, first_ref, out_ref, band_ref,
                  first, out, band, sems):
    fetch = move([(first_ref, first)], sems)
    size = inv_ref.shape[0]
    strip = size // parts_ref.shape[0]
    row, col = grids(size)
    ident = jnp.where(row == col, 1.0, 0.0)
    pieces = range(parts_ref.shape[0])
    gram = jnp.concatenate([parts_ref[c, :strip, :] for c in pieces], axis=0)
    top = jnp.concatenate([parts_ref[c, strip:, :] for c in pieces], axis=0)
    half_top = mult(top, inv_ref[...], ACROSS)
    mat = gram + mult(half_top, upper_ref[...], TURNED)
    halves = split(mat)
    wait(fetch)
    band[...] = -mult(upper_ref[...], first[...])
    store = move([(band, band_ref)], sems)

    def residual(guess):
        return ident - mult3(halves, split(guess))

    def step(state):
        count, guess, rest, _ = state
        guess = guess + mult3(split(guess), split(rest))
        rest = residual(guess)
        return count + 1, guess, rest, jnp.max(jnp.abs(rest))

    def more(state):
        count, _, _, worst = state
        return (worst > 2e-5) & (count < 40)

    guess = 0.5 * ident
    rest = ident - 0.5 * mat
    for _ in range(4):
        parts = split(rest)
        guess = guess + mult3(split(guess), parts)
        rest = mult3(parts, parts)
    guess = guess + mult3(split(guess), split(rest))
    rest = residual(guess)
    state = (jnp.int32(0), guess, rest, jnp.max(jnp.abs(rest)))
    out[...] = lax.while_loop(more, step, state)[1]
    wait(store + move([(out, out_ref)], sems.at[pl.ds(1, 1)]))


def compact_factor(parts, inv, upper, first):
    size = inv.shape[0]
    return pl.pallas_call(
        factor_kernel,
        in_specs=[VMEM] * 3 + [HBM],
        out_specs=(HBM, HBM),
        out_shape=(square(size), square(size)),
        scratch_shapes=[pltpu.VMEM((size, size), jnp.float32)] * 3 + [pltpu.SemaphoreType.DMA((2,))],
        compiler_params=SMALL,
        cost_estimate=estimate(4),
        name="compact_factor",
    )(parts, inv, upper, first)


def array(*dims):
    return jax.ShapeDtypeStruct(dims, jnp.float32)


def scratch(*dims):
    return pltpu.VMEM(dims, jnp.float32)


def gram_kernel(place_ref, panel_ref, out_ref, gram_ref):
    strip = out_ref.shape[0] // 2
    mine = pl.ds(pl.multiple_of(place_ref[1] * strip, strip), strip)
    gram_ref[...] = mult(panel_ref[...], panel_ref[...], TURNED)
    out_ref[:strip, :] = gram_ref[mine, :]
    out_ref[strip:, :] = panel_ref[mine, :] * jnp.where(place_ref[0] == 0, 1.0, 0.0)


def gram_strips(place, panel, cols):
    width = panel.shape[1]
    return pl.pallas_call(
        gram_kernel,
        in_specs=[SMEM, VMEM],
        out_shape=array(2 * width // cols, width),
        scratch_shapes=[scratch(width, width)],
        compiler_params=LARGE,
        cost_estimate=estimate(2),
        name="gram_strips",
    )(place, panel)


def half_kernel(place_ref, panel_ref, slab_ref, got_ref, inv_ref, half_out, cols_out, out_ref,
                half_ref, cols_ref, gram_ref, sems):
    strip = out_ref.shape[0]
    mine = pl.ds(pl.multiple_of(place_ref[1] * strip, strip), strip)
    half = mult(panel_ref[...], inv_ref[...], ACROSS)
    half_ref[...] = half
    cols_ref[...] = mult(slab_ref[...] + got_ref[...], inv_ref[...], ACROSS)
    store = move([(half_ref, half_out), (cols_ref, cols_out)], sems)
    parts = split(half)
    gram_ref[...] = mult3(parts, parts, TURNED)
    out_ref[...] = gram_ref[mine, :]
    wait(store)


def half_stage(place, panel, slab, got, inv, cols):
    width = panel.shape[1]
    return pl.pallas_call(
        half_kernel,
        in_specs=[SMEM] + [VMEM] * 4,
        out_specs=(HBM, HBM, VMEM),
        out_shape=(array(*panel.shape), array(*slab.shape), array(width // cols, width)),
        scratch_shapes=[
            scratch(*panel.shape),
            scratch(*slab.shape),
            scratch(width, width),
            pltpu.SemaphoreType.DMA((2,)),
        ],
        compiler_params=LARGE,
        cost_estimate=estimate(3),
        name="half_stage",
    )(place, panel, slab, got, inv)


def products_kernel(place_ref, ham_ref, half_in, cols_in, upper_ref,
                    left_out, right_out, keep_ref, send_ref, *rest_refs):
    piece_refs = rest_refs[:-6]
    left_ref, right_ref, part_ref, coupling_ref, near_ref, sems = rest_refs[-6:]
    fetch = move([(cols_in, right_ref), (half_in, left_ref)], sems)
    width = upper_ref.shape[0]
    chips = keep_ref.shape[0]
    rows_dev = ham_ref.shape[0]
    piece, strip = rows_dev // 2 // chips, width // 2 // chips
    share = piece_refs[0].shape[0]
    row_place, col_place = place_ref[0], place_ref[1]
    core, chip = col_place & 1, col_place // 2
    ham = split(ham_ref[...])
    fetch[0].wait()
    lead = jnp.where(col_place == 0, 1.0, 0.0)
    right_ref[:width, :] = right_ref[:width, :] + lead * upper_ref[...]
    part = mult3(ham, split(right_ref[...]))
    part_ref[...] = part
    fetch[1].wait()
    lead = jnp.where(row_place == 0, 1.0, 0.0)
    left_ref[:width, :] = left_ref[:width, :] + lead * upper_ref[...]
    store = move([(right_ref, right_out), (left_ref, left_out)], sems)
    left = split(left_ref[...])
    coupling_ref[...] = mult3(left, split(part), TURNED)
    for ref, half in ((send_ref, 1 - core), (keep_ref, core)):
        for hop in range(chips):
            start = (half * chips + (chip ^ hop)) * piece
            ref[hop, :piece, :] = part_ref[pl.ds(pl.multiple_of(start, piece), piece), :]
            start = (half * chips + (chip ^ hop)) * strip
            ref[hop, piece:, :] = coupling_ref[pl.ds(pl.multiple_of(start, strip), strip), :]
    near_ref[...] = mult3(ham, left, TURNED)
    for hop, ref in enumerate(piece_refs):
        start = pl.multiple_of((row_place ^ hop) * share, share)
        ref[...] = near_ref[pl.ds(start, share), :]
    wait(store)


def products(place, hamiltonian, half, half_cols, upper, rows, cols):
    rows_dev, cols_dev = hamiltonian.shape
    width = upper.shape[0]
    chips = cols // 2
    share = (rows_dev + width) // cols
    out = pl.pallas_call(
        products_kernel,
        in_specs=[SMEM, VMEM, HBM, HBM, VMEM],
        out_specs=(HBM, HBM) + (VMEM,) * (2 + rows),
        out_shape=(
            array(rows_dev, width),
            array(cols_dev, width),
            array(chips, share, width),
            array(chips, share, width),
        )
        + (array(cols_dev // rows, width),) * rows,
        scratch_shapes=[
            scratch(rows_dev, width),
            scratch(cols_dev, width),
            scratch(rows_dev, width),
            scratch(width, width),
            scratch(cols_dev, width),
            pltpu.SemaphoreType.DMA((2,)),
        ],
        compiler_params=LARGE,
        cost_estimate=estimate(4),
        name="products",
    )(place, hamiltonian, half, half_cols, upper)
    return out[0], out[1], out[2], out[3], out[4:]


def pair_kernel(keep_ref, got_ref, *out_refs):
    for hop, ref in enumerate(out_refs):
        ref[...] = keep_ref[hop] + got_ref[hop]


def pair_add(keep, got):
    return pl.pallas_call(
        pair_kernel,
        in_specs=[VMEM] * 2,
        out_shape=(array(*keep.shape[1:]),) * keep.shape[0],
        compiler_params=LARGE,
        cost_estimate=estimate(0.5),
        name="pair_add",
    )(keep, got)


def tree_sum(terms):
    while len(terms) > 1:
        terms = [terms[i] + terms[i + 1] for i in range(0, len(terms), 2)]
    return terms[0]


def sums_kernel(count, *refs):
    total_refs, piece_refs = refs[:count], refs[count:-2]
    mine_ref, both_ref = refs[-2:]
    piece, share = mine_ref.shape[0], piece_refs[0].shape[0]
    total = tree_sum([ref[...] for ref in total_refs])
    mine_ref[...] = total[:piece]
    both_ref[:share, :] = tree_sum([ref[...] for ref in piece_refs])
    both_ref[share:, :] = total[piece:]


def sum_pieces(totals, pieces, piece):
    share, width = pieces[0].shape
    strip = totals[0].shape[0] - piece
    return pl.pallas_call(
        functools.partial(sums_kernel, len(totals)),
        in_specs=[VMEM] * (len(totals) + len(pieces)),
        out_shape=(array(piece, width), array(share + strip, width)),
        compiler_params=LARGE,
        cost_estimate=estimate(0.5),
        name="sum_pieces",
    )(*totals, *pieces)


def spread_kernel(groups, *refs):
    out_ref = refs[-1]
    start = 0
    for count, first, last in groups:
        total = tree_sum([ref[first:last, :] for ref in refs[:count]])
        refs = refs[count:]
        for c in range(out_ref.shape[0]):
            out_ref[c, start : start + last - first, :] = total
        start += last - first


def sum_gather(cols, *groups):
    terms = [term for group in groups for term in group[0]]
    bounds = [(len(group[0]), group[1], group[2]) for group in groups]
    height = sum(last - first for _, first, last in bounds)
    copies = pl.pallas_call(
        functools.partial(spread_kernel, bounds),
        in_specs=[VMEM] * len(terms),
        out_shape=array(cols, height, terms[0].shape[1]),
        compiler_params=LARGE,
        cost_estimate=estimate(0.5),
        name="sum_copies",
    )(*terms)
    return lax.all_to_all(copies, "col", 0, 0, tiled=True)


def merge_kernel(place_ref, *refs):
    out_ref = refs[-1]
    piece = refs[0].shape[0]
    chip = place_ref[1] // 2
    for hop, ref in enumerate(refs[:-1]):
        out_ref[pl.ds(pl.multiple_of((chip ^ hop) * piece, piece), piece), :] = ref[...]


def merge(place, pieces):
    piece, width = pieces[0].shape
    return pl.pallas_call(
        merge_kernel,
        in_specs=[SMEM] + [VMEM] * len(pieces),
        out_shape=array(len(pieces) * piece, width),
        compiler_params=LARGE,
        cost_estimate=estimate(0.5),
        name="merge_pieces",
    )(place, *pieces)


def update_kernel(
    place_ref, ham_ref, left_ref, mine_ref, other_ref, right_ref, factor_ref,
    parts_ref, *rest_refs
):
    piece_refs, (out_ref, near_ref, sum_ref) = rest_refs[:-3], rest_refs[-3:]
    deep = mine_ref.shape[0]
    share = near_ref.shape[0] // len(piece_refs)
    row_place, core = place_ref[0], place_ref[1] & 1
    for hop, ref in enumerate(piece_refs):
        start = pl.multiple_of((row_place ^ hop) * share, share)
        near_ref[pl.ds(start, share), :] = ref[:share, :]
    strip = parts_ref.shape[1]
    chips = parts_ref.shape[0] // 2
    for c in range(parts_ref.shape[0]):
        start = ((c % 2) * chips + c // 2) * strip
        sum_ref[start : start + strip, :] = parts_ref[c]
    factor = split(factor_ref[...])
    right = split(right_ref[...])
    turn = mult3(split(sum_ref[...]), factor)
    middle = mult3(factor, split(turn), TURNED)
    near = split(mult3(split(near_ref[...]), factor) - mult3(right, split(middle)))
    far = split(mult3(right, factor, ACROSS))
    for place, prod_ref in ((core, mine_ref), (1 - core, other_ref)):
        block = pl.ds(pl.multiple_of(place * deep, deep), deep)
        change = mult3(split(left_ref[block, :]), near, ACROSS)
        change = change + mult3(split(prod_ref[...]), far, ACROSS)
        out_ref[block, :] = ham_ref[block, :] - change


def update(place, hamiltonian, left, mine, other, right, factor, parts, pieces):
    return pl.pallas_call(
        update_kernel,
        in_specs=[SMEM] + [VMEM] * (7 + len(pieces)),
        out_shape=array(*hamiltonian.shape),
        scratch_shapes=[scratch(*right.shape), scratch(*factor.shape)],
        compiler_params=LARGE,
        cost_estimate=estimate(4),
        name="two_sided_update",
    )(place, hamiltonian, left, mine, other, right, factor, parts, *pieces)


def hops(values, axis, size, scale=1):
    got = [values[0]]
    for hop in range(1, len(values)):
        pairs = [(i, i ^ (hop * scale)) for i in range(size)]
        got.append(lax.ppermute(values[hop], axis, pairs))
    return got


def shards(rows, cols, hamiltonian, panel):
    rows_dev, width = panel.shape
    cols_dev = hamiltonian.shape[1]
    row_place = lax.axis_index("row")
    col_place = lax.axis_index("col")
    chips = cols // 2
    strip = width // cols
    piece = rows_dev // cols
    share = cols_dev // rows
    pair = [(i, i ^ 1) for i in range(cols)]
    place = jnp.stack([row_place, col_place]).astype(jnp.int32)

    strips = hops([gram_strips(place, panel, cols)] * rows, "row", rows)

    owners = [c * cols_dev // rows_dev for c in range(cols)]
    owner = col_place * cols_dev // rows_dev
    offset = col_place * cols_dev - owner * rows_dev
    slab = lax.dynamic_slice_in_dim(panel, offset, cols_dev, 0)
    slab = jnp.where(row_place == owner, slab, 0.0)
    strips, slab = lax.optimization_barrier((strips, slab))
    hop, having = rows // 2, [0]
    got = jnp.zeros_like(slab)
    while hop:
        if having != [0]:
            slab = slab + got
        pairs = [
            ((owners[c] ^ d) * cols + c, (owners[c] ^ d ^ hop) * cols + c)
            for c in range(cols)
            for d in having
        ]
        got = lax.ppermute(slab, ("row", "col"), pairs)
        having = having + [d ^ hop for d in having]
        hop //= 2

    gram = sum_gather(cols, (strips, 0, strip))
    first_upper, first_inv = cholesky(gram)
    half, half_cols, gram2_strip = half_stage(place, panel, slab, got, first_inv, cols)
    gram2_strips = hops([gram2_strip] * rows, "row", rows)
    parts = sum_gather(cols, (gram2_strips, 0, strip), (strips, strip, 2 * strip))
    gram2 = parts[:, :strip].reshape(width, width)
    second_upper = near_cholesky(gram2)

    left, right, keep, send, pieces = products(
        place, hamiltonian, half, half_cols, second_upper, rows, cols
    )
    parts, send = lax.optimization_barrier((parts, send))
    factor, band_block = compact_factor(parts, first_inv, second_upper, first_upper)
    totals = pair_add(keep, lax.ppermute(send, "col", pair))
    totals = hops(totals, "col", cols, 2)
    pieces = hops(pieces, "row", rows)
    mine, both = sum_pieces(totals, pieces, piece)
    both = hops([both] * rows, "row", rows)
    mine, both[1] = lax.optimization_barrier((mine, both[1]))
    mine = merge(place, hops([mine] * chips, "col", cols, 2))
    other = lax.ppermute(mine, "col", pair)
    both, factor = lax.optimization_barrier((both, factor))
    coupling = sum_gather(cols, (both, share, share + strip))
    updated = update(place, hamiltonian, left, mine, other, right, factor, coupling, both)
    return (updated, band_block)


def solution(mesh):
    in_specs = (P("row", "col"), P("row", None))
    out_specs = (P("row", "col"), P())
    body = functools.partial(shards, mesh.shape["row"], mesh.shape["col"])
    return jax.shard_map(body, mesh=mesh, in_specs=in_specs, out_specs=out_specs, check_vma=False)
```

```python
import functools

import jax
import jax.numpy as jnp
from jax import lax
from jax.experimental import pallas as pl
from jax.experimental.pallas import tpu as pltpu
from jax.sharding import PartitionSpec as P

SUB = 8
LANE = 128
BLOCK = 32
HIGHEST = lax.Precision.HIGHEST
SMALL = pltpu.CompilerParams(vmem_limit_bytes=10 * 2**20)
LARGE = pltpu.CompilerParams(vmem_limit_bytes=24 * 2**20)
VMEM = pl.BlockSpec(memory_space=pltpu.VMEM)
SMEM = pl.BlockSpec(memory_space=pltpu.SMEM)
HBM = pl.BlockSpec(memory_space=pltpu.HBM)
PLAIN = ((1,), (0,))
TURNED = ((0,), (0,))
ACROSS = ((1,), (1,))


def mult(left, right, dims=PLAIN):
    return lax.dot_general(
        left, right, (dims, ((), ())), precision=HIGHEST, preferred_element_type=jnp.float32
    )


def move(pairs, sems):
    copies = [pltpu.make_async_copy(src, dst, sems.at[i]) for i, (src, dst) in enumerate(pairs)]
    for copy in copies:
        copy.start()
    return copies


def wait(copies):
    for copy in copies:
        copy.wait()


def split(value):
    high = value.astype(jnp.bfloat16)
    return high, (value - high.astype(jnp.float32)).astype(jnp.bfloat16)


def mult3(left, right, dims=PLAIN):
    def one(a, b):
        return lax.dot_general(a, b, (dims, ((), ())), preferred_element_type=jnp.float32)

    return one(left[0], right[0]) + (one(left[0], right[1]) + one(left[1], right[0]))


def chol_kernel(gram_ref, upper_ref, inv_ref, work_ref):
    size = gram_ref.shape[0]
    tiles = size // LANE
    groups = BLOCK // SUB
    lanes = lax.broadcasted_iota(jnp.int32, (SUB, LANE), 1)
    work_ref[...] = gram_ref[...]

    def spread(row):
        return jnp.broadcast_to(row, (SUB, LANE))

    for first in range(0, size, BLOCK):
        rows = [
            [
                work_ref[first + SUB * g : first + SUB * (g + 1), LANE * t : LANE * (t + 1)]
                for t in range(tiles)
            ]
            for g in range(groups)
        ]
        for g in range(groups):
            col = first + SUB * g
            home, low = divmod(col, LANE)
            in_block = (lanes >= low) & (lanes < low + SUB)
            flat = [[spread(rows[g][t][k : k + 1, :]) for t in range(tiles)] for k in range(SUB)]
            diag = [
                [spread(flat[k][home][:, low + i : low + i + 1]) for i in range(k + 1)]
                for k in range(SUB)
            ]
            unit = [jnp.where(lanes == low + k, 1.0, 0.0) for k in range(SUB)]
            later = range(g + 1, groups)
            cols = {
                q: [spread(rows[q][home][:, low + i : low + i + 1]) for i in range(SUB)]
                for q in later
            }
            for q in later:
                rows[q][home] = jnp.where(in_block, 0.0, rows[q][home])
            for i in range(SUB):
                recip = 1.0 / diag[i][i]
                steps = [None] * SUB
                for k in range(i + 1, SUB):
                    steps[k] = diag[k][i] * recip
                for k in range(i + 1, SUB):
                    for j in range(i + 1, k + 1):
                        diag[k][j] = diag[k][j] - steps[k] * diag[j][i]
                for k in range(i + 1, SUB):
                    for t in range(tiles):
                        flat[k][t] = flat[k][t] - steps[k] * flat[i][t]
                    unit[k] = unit[k] - steps[k] * unit[i]
                for q in later:
                    step = cols[q][i] * recip
                    for j in range(i + 1, SUB):
                        cols[q][j] = cols[q][j] - step * diag[j][i]
                    for t in range(tiles):
                        source = flat[i][t]
                        if t == home:
                            source = jnp.where(in_block, unit[i], source)
                        rows[q][t] = rows[q][t] - step * source
            for k in range(SUB):
                scale = lax.rsqrt(diag[k][k])
                for t in range(tiles):
                    scaled = flat[k][t] * scale
                    if t < home:
                        up, inv = jnp.zeros_like(scaled), scaled
                    elif t > home:
                        up, inv = scaled, jnp.zeros_like(scaled)
                    else:
                        up = jnp.where(lanes >= low + k, scaled, 0.0)
                        inv = jnp.where(in_block, unit[k] * scale, scaled)
                        inv = jnp.where(lanes < low + SUB, inv, 0.0)
                    upper_ref[col + k : col + k + 1, LANE * t : LANE * (t + 1)] = up[0:1]
                    inv_ref[col + k : col + k + 1, LANE * t : LANE * (t + 1)] = inv[0:1]
        rest = first + BLOCK
        if rest == size:
            break
        start = rest // LANE * LANE
        left = upper_ref[first:rest, start:size]
        wide = lax.broadcasted_iota(jnp.int32, (BLOCK, size), 1)
        right = jnp.where(wide < rest, inv_ref[first:rest, :], upper_ref[first:rest, :])
        change = mult(left, right, ((0,), (0,)))
        below = lax.broadcasted_iota(jnp.int32, (size - rest, size), 1)
        old = jnp.where((below >= first) & (below < rest), 0.0, work_ref[rest:size, :])
        work_ref[rest:size, :] = old - change[rest - start :, :]


def estimate(micros):
    return pl.CostEstimate(flops=int(micros * 1e9), bytes_accessed=int(micros * 3e6), transcendentals=0)


def square(size):
    return jax.ShapeDtypeStruct((size, size), jnp.float32)


def first_kernel(parts_ref, upper_out, inv_ref, gram_ref, upper_ref, work_ref, sems):
    strip = parts_ref.shape[1]
    for c in range(parts_ref.shape[0]):
        gram_ref[c * strip : (c + 1) * strip, :] = parts_ref[c]
    chol_kernel(gram_ref, upper_ref, inv_ref, work_ref)
    wait(move([(upper_ref, upper_out)], sems))


def cholesky(parts):
    size = parts.shape[2]
    return pl.pallas_call(
        first_kernel,
        in_specs=[VMEM],
        out_specs=(HBM, VMEM),
        out_shape=(square(size), square(size)),
        scratch_shapes=[pltpu.VMEM((size, size), jnp.float32)] * 3 + [pltpu.SemaphoreType.DMA((1,))],
        compiler_params=SMALL,
        cost_estimate=estimate(10),
        name="cholesky_inverse",
    )(parts)


def grids(size):
    row = lax.broadcasted_iota(jnp.int32, (size, size), 0)
    col = lax.broadcasted_iota(jnp.int32, (size, size), 1)
    return row, col


def near_kernel(gram_ref, upper_ref, inv_ref, work_ref):
    size = gram_ref.shape[0]
    row, col = grids(size)
    ident = jnp.where(row == col, 1.0, 0.0)
    weight = jnp.where(row > col, 1.0, ident * 0.5)
    gram = split(gram_ref[...])

    def look(inv):
        halves = split(inv)
        upper = mult3(halves, gram)
        low = weight * (mult3(split(upper), halves, ACROSS) - ident)
        return upper, low, jnp.sum(low * low)

    def more(state):
        count, _, _, _, worst = state
        return jnp.logical_not(worst < 1e-8) & (count < 10)

    def step(state):
        count, inv, _, low, _ = state
        low = split(low)
        turn = mult3(low, split(inv))
        inv = inv - turn + mult3(low, split(turn))
        return (count + 1, inv) + look(inv)

    low = weight * (gram_ref[...] - ident)
    halves = split(low)
    inv = ident - low + mult3(halves, halves)
    state = lax.while_loop(more, step, (jnp.int32(0), inv) + look(inv))
    _, _, upper, low, worst = state
    upper = upper + mult3(split(low), split(upper), TURNED)
    upper_ref[...] = jnp.where(row <= col, upper, 0.0)

    @pl.when(jnp.logical_not(worst < 1e-8))
    def _():
        chol_kernel(gram_ref, upper_ref, inv_ref, work_ref)


def near_cholesky(gram):
    size = gram.shape[0]
    return pl.pallas_call(
        near_kernel,
        out_shape=square(size),
        scratch_shapes=[pltpu.VMEM((size, size), jnp.float32)] * 2,
        compiler_params=SMALL,
        cost_estimate=estimate(3),
        name="near_cholesky",
    )(gram)


def factor_kernel(parts_ref, inv_ref, upper_ref, first_ref, out_ref, band_ref,
                  first, out, band, sems):
    fetch = move([(first_ref, first)], sems)
    size = inv_ref.shape[0]
    strip = size // parts_ref.shape[0]
    row, col = grids(size)
    ident = jnp.where(row == col, 1.0, 0.0)
    pieces = range(parts_ref.shape[0])
    gram = jnp.concatenate([parts_ref[c, :strip, :] for c in pieces], axis=0)
    top = jnp.concatenate([parts_ref[c, strip:, :] for c in pieces], axis=0)
    half_top = mult(top, inv_ref[...], ACROSS)
    mat = gram + mult(half_top, upper_ref[...], TURNED)
    halves = split(mat)
    wait(fetch)
    band[...] = -mult(upper_ref[...], first[...])
    store = move([(band, band_ref)], sems)

    def residual(guess):
        return ident - mult3(halves, split(guess))

    def step(state):
        count, guess, rest, _ = state
        guess = guess + mult3(split(guess), split(rest))
        rest = residual(guess)
        return count + 1, guess, rest, jnp.max(jnp.abs(rest))

    def more(state):
        count, _, _, worst = state
        return (worst > 2e-5) & (count < 40)

    guess = 0.5 * ident
    rest = ident - 0.5 * mat
    for _ in range(4):
        parts = split(rest)
        guess = guess + mult3(split(guess), parts)
        rest = mult3(parts, parts)
    guess = guess + mult3(split(guess), split(rest))
    rest = residual(guess)
    state = (jnp.int32(0), guess, rest, jnp.max(jnp.abs(rest)))
    out[...] = lax.while_loop(more, step, state)[1]
    wait(store + move([(out, out_ref)], sems.at[pl.ds(1, 1)]))


def compact_factor(parts, inv, upper, first):
    size = inv.shape[0]
    return pl.pallas_call(
        factor_kernel,
        in_specs=[VMEM] * 3 + [HBM],
        out_specs=(HBM, HBM),
        out_shape=(square(size), square(size)),
        scratch_shapes=[pltpu.VMEM((size, size), jnp.float32)] * 3 + [pltpu.SemaphoreType.DMA((2,))],
        compiler_params=SMALL,
        cost_estimate=estimate(4),
        name="compact_factor",
    )(parts, inv, upper, first)


def array(*dims):
    return jax.ShapeDtypeStruct(dims, jnp.float32)


def scratch(*dims):
    return pltpu.VMEM(dims, jnp.float32)


def gram_kernel(place_ref, panel_ref, out_ref, gram_ref):
    strip = out_ref.shape[0] // 2
    mine = pl.ds(pl.multiple_of(place_ref[1] * strip, strip), strip)
    gram_ref[...] = mult(panel_ref[...], panel_ref[...], TURNED)
    out_ref[:strip, :] = gram_ref[mine, :]
    out_ref[strip:, :] = panel_ref[mine, :] * jnp.where(place_ref[0] == 0, 1.0, 0.0)


def gram_strips(place, panel, cols):
    width = panel.shape[1]
    return pl.pallas_call(
        gram_kernel,
        in_specs=[SMEM, VMEM],
        out_shape=array(2 * width // cols, width),
        scratch_shapes=[scratch(width, width)],
        compiler_params=LARGE,
        cost_estimate=estimate(2),
        name="gram_strips",
    )(place, panel)


def half_kernel(place_ref, panel_ref, slab_ref, got_ref, inv_ref, half_out, cols_out, out_ref,
                half_ref, cols_ref, gram_ref, sems):
    strip = out_ref.shape[0]
    mine = pl.ds(pl.multiple_of(place_ref[1] * strip, strip), strip)
    half = mult(panel_ref[...], inv_ref[...], ACROSS)
    half_ref[...] = half
    cols_ref[...] = mult(slab_ref[...] + got_ref[...], inv_ref[...], ACROSS)
    store = move([(half_ref, half_out), (cols_ref, cols_out)], sems)
    parts = split(half)
    gram_ref[...] = mult3(parts, parts, TURNED)
    out_ref[...] = gram_ref[mine, :]
    wait(store)


def half_stage(place, panel, slab, got, inv, cols):
    width = panel.shape[1]
    return pl.pallas_call(
        half_kernel,
        in_specs=[SMEM] + [VMEM] * 4,
        out_specs=(HBM, HBM, VMEM),
        out_shape=(array(*panel.shape), array(*slab.shape), array(width // cols, width)),
        scratch_shapes=[
            scratch(*panel.shape),
            scratch(*slab.shape),
            scratch(width, width),
            pltpu.SemaphoreType.DMA((2,)),
        ],
        compiler_params=LARGE,
        cost_estimate=estimate(3),
        name="half_stage",
    )(place, panel, slab, got, inv)


def products_kernel(place_ref, ham_ref, half_in, cols_in, upper_ref,
                    left_out, right_out, keep_ref, send_ref, *rest_refs):
    piece_refs = rest_refs[:-6]
    left_ref, right_ref, part_ref, coupling_ref, near_ref, sems = rest_refs[-6:]
    fetch = move([(cols_in, right_ref), (half_in, left_ref)], sems)
    width = upper_ref.shape[0]
    chips = keep_ref.shape[0]
    rows_dev = ham_ref.shape[0]
    piece, strip = rows_dev // 2 // chips, width // 2 // chips
    share = piece_refs[0].shape[0]
    row_place, col_place = place_ref[0], place_ref[1]
    core, chip = col_place & 1, col_place // 2
    ham = split(ham_ref[...])
    fetch[0].wait()
    lead = jnp.where(col_place == 0, 1.0, 0.0)
    right_ref[:width, :] = right_ref[:width, :] + lead * upper_ref[...]
    part = mult3(ham, split(right_ref[...]))
    part_ref[...] = part
    fetch[1].wait()
    lead = jnp.where(row_place == 0, 1.0, 0.0)
    left_ref[:width, :] = left_ref[:width, :] + lead * upper_ref[...]
    store = move([(right_ref, right_out), (left_ref, left_out)], sems)
    left = split(left_ref[...])
    coupling_ref[...] = mult3(left, split(part), TURNED)
    for ref, half in ((send_ref, 1 - core), (keep_ref, core)):
        for hop in range(chips):
            start = (half * chips + (chip ^ hop)) * piece
            ref[hop, :piece, :] = part_ref[pl.ds(pl.multiple_of(start, piece), piece), :]
            start = (half * chips + (chip ^ hop)) * strip
            ref[hop, piece:, :] = coupling_ref[pl.ds(pl.multiple_of(start, strip), strip), :]
    near_ref[...] = mult3(ham, left, TURNED)
    for hop, ref in enumerate(piece_refs):
        start = pl.multiple_of((row_place ^ hop) * share, share)
        ref[...] = near_ref[pl.ds(start, share), :]
    wait(store)


def products(place, hamiltonian, half, half_cols, upper, rows, cols):
    rows_dev, cols_dev = hamiltonian.shape
    width = upper.shape[0]
    chips = cols // 2
    share = (rows_dev + width) // cols
    out = pl.pallas_call(
        products_kernel,
        in_specs=[SMEM, VMEM, HBM, HBM, VMEM],
        out_specs=(HBM, HBM) + (VMEM,) * (2 + rows),
        out_shape=(
            array(rows_dev, width),
            array(cols_dev, width),
            array(chips, share, width),
            array(chips, share, width),
        )
        + (array(cols_dev // rows, width),) * rows,
        scratch_shapes=[
            scratch(rows_dev, width),
            scratch(cols_dev, width),
            scratch(rows_dev, width),
            scratch(width, width),
            scratch(cols_dev, width),
            pltpu.SemaphoreType.DMA((2,)),
        ],
        compiler_params=LARGE,
        cost_estimate=estimate(4),
        name="products",
    )(place, hamiltonian, half, half_cols, upper)
    return out[0], out[1], out[2], out[3], out[4:]


def pair_kernel(keep_ref, got_ref, *out_refs):
    for hop, ref in enumerate(out_refs):
        ref[...] = keep_ref[hop] + got_ref[hop]


def pair_add(keep, got):
    return pl.pallas_call(
        pair_kernel,
        in_specs=[VMEM] * 2,
        out_shape=(array(*keep.shape[1:]),) * keep.shape[0],
        compiler_params=LARGE,
        cost_estimate=estimate(0.5),
        name="pair_add",
    )(keep, got)


def tree_sum(terms):
    while len(terms) > 1:
        terms = [terms[i] + terms[i + 1] for i in range(0, len(terms), 2)]
    return terms[0]


def sums_kernel(count, *refs):
    total_refs, piece_refs = refs[:count], refs[count:-2]
    mine_ref, both_ref = refs[-2:]
    piece, share = mine_ref.shape[0], piece_refs[0].shape[0]
    total = tree_sum([ref[...] for ref in total_refs])
    mine_ref[...] = total[:piece]
    both_ref[:share, :] = tree_sum([ref[...] for ref in piece_refs])
    both_ref[share:, :] = total[piece:]


def sum_pieces(totals, pieces, piece):
    share, width = pieces[0].shape
    strip = totals[0].shape[0] - piece
    return pl.pallas_call(
        functools.partial(sums_kernel, len(totals)),
        in_specs=[VMEM] * (len(totals) + len(pieces)),
        out_shape=(array(piece, width), array(share + strip, width)),
        compiler_params=LARGE,
        cost_estimate=estimate(0.5),
        name="sum_pieces",
    )(*totals, *pieces)


def spread_kernel(groups, *refs):
    out_ref = refs[-1]
    start = 0
    for count, first, last in groups:
        total = tree_sum([ref[first:last, :] for ref in refs[:count]])
        refs = refs[count:]
        for c in range(out_ref.shape[0]):
            out_ref[c, start : start + last - first, :] = total
        start += last - first


def sum_gather(cols, *groups):
    terms = [term for group in groups for term in group[0]]
    bounds = [(len(group[0]), group[1], group[2]) for group in groups]
    height = sum(last - first for _, first, last in bounds)
    copies = pl.pallas_call(
        functools.partial(spread_kernel, bounds),
        in_specs=[VMEM] * len(terms),
        out_shape=array(cols, height, terms[0].shape[1]),
        compiler_params=LARGE,
        cost_estimate=estimate(0.5),
        name="sum_copies",
    )(*terms)
    return lax.all_to_all(copies, "col", 0, 0, tiled=True)


def merge_kernel(place_ref, *refs):
    out_ref = refs[-1]
    piece = refs[0].shape[0]
    chip = place_ref[1] // 2
    for hop, ref in enumerate(refs[:-1]):
        out_ref[pl.ds(pl.multiple_of((chip ^ hop) * piece, piece), piece), :] = ref[...]


def merge(place, pieces):
    piece, width = pieces[0].shape
    return pl.pallas_call(
        merge_kernel,
        in_specs=[SMEM] + [VMEM] * len(pieces),
        out_shape=array(len(pieces) * piece, width),
        compiler_params=LARGE,
        cost_estimate=estimate(0.5),
        name="merge_pieces",
    )(place, *pieces)


def update_kernel(
    place_ref, ham_ref, left_ref, mine_ref, other_ref, right_ref, factor_ref,
    parts_ref, *rest_refs
):
    piece_refs, (out_ref, near_ref, sum_ref) = rest_refs[:-3], rest_refs[-3:]
    deep = mine_ref.shape[0]
    share = near_ref.shape[0] // len(piece_refs)
    row_place, core = place_ref[0], place_ref[1] & 1
    for hop, ref in enumerate(piece_refs):
        start = pl.multiple_of((row_place ^ hop) * share, share)
        near_ref[pl.ds(start, share), :] = ref[:share, :]
    strip = parts_ref.shape[1]
    chips = parts_ref.shape[0] // 2
    for c in range(parts_ref.shape[0]):
        start = ((c % 2) * chips + c // 2) * strip
        sum_ref[start : start + strip, :] = parts_ref[c]
    factor = split(factor_ref[...])
    right = split(right_ref[...])
    turn = mult3(split(sum_ref[...]), factor)
    middle = mult3(factor, split(turn), TURNED)
    near = split(mult3(split(near_ref[...]), factor) - mult3(right, split(middle)))
    far = split(mult3(right, factor, ACROSS))
    for place, prod_ref in ((core, mine_ref), (1 - core, other_ref)):
        block = pl.ds(pl.multiple_of(place * deep, deep), deep)
        change = mult3(split(left_ref[block, :]), near, ACROSS)
        change = change + mult3(split(prod_ref[...]), far, ACROSS)
        out_ref[block, :] = ham_ref[block, :] - change


def update(place, hamiltonian, left, mine, other, right, factor, parts, pieces):
    return pl.pallas_call(
        update_kernel,
        in_specs=[SMEM] + [VMEM] * (7 + len(pieces)),
        out_shape=array(*hamiltonian.shape),
        scratch_shapes=[scratch(*right.shape), scratch(*factor.shape)],
        compiler_params=LARGE,
        cost_estimate=estimate(4),
        name="two_sided_update",
    )(place, hamiltonian, left, mine, other, right, factor, parts, *pieces)


def hops(values, axis, size, scale=1):
    got = [values[0]]
    for hop in range(1, len(values)):
        pairs = [(i, i ^ (hop * scale)) for i in range(size)]
        got.append(lax.ppermute(values[hop], axis, pairs))
    return got


def shards(rows, cols, hamiltonian, panel):
    rows_dev, width = panel.shape
    cols_dev = hamiltonian.shape[1]
    row_place = lax.axis_index("row")
    col_place = lax.axis_index("col")
    chips = cols // 2
    strip = width // cols
    piece = rows_dev // cols
    share = cols_dev // rows
    pair = [(i, i ^ 1) for i in range(cols)]
    place = jnp.stack([row_place, col_place]).astype(jnp.int32)

    strips = hops([gram_strips(place, panel, cols)] * rows, "row", rows)

    owners = [c * cols_dev // rows_dev for c in range(cols)]
    owner = col_place * cols_dev // rows_dev
    offset = col_place * cols_dev - owner * rows_dev
    slab = lax.dynamic_slice_in_dim(panel, offset, cols_dev, 0)
    slab = jnp.where(row_place == owner, slab, 0.0)
    strips, slab = lax.optimization_barrier((strips, slab))
    hop, having = rows // 2, [0]
    got = jnp.zeros_like(slab)
    while hop:
        if having != [0]:
            slab = slab + got
        pairs = [
            ((owners[c] ^ d) * cols + c, (owners[c] ^ d ^ hop) * cols + c)
            for c in range(cols)
            for d in having
        ]
        got = lax.ppermute(slab, ("row", "col"), pairs)
        having = having + [d ^ hop for d in having]
        hop //= 2

    gram = sum_gather(cols, (strips, 0, strip))
    first_upper, first_inv = cholesky(gram)
    half, half_cols, gram2_strip = half_stage(place, panel, slab, got, first_inv, cols)
    gram2_strips = hops([gram2_strip] * rows, "row", rows)
    parts = sum_gather(cols, (gram2_strips, 0, strip), (strips, strip, 2 * strip))
    gram2 = parts[:, :strip].reshape(width, width)
    second_upper = near_cholesky(gram2)

    left, right, keep, send, pieces = products(
        place, hamiltonian, half, half_cols, second_upper, rows, cols
    )
    totals = pair_add(keep, lax.ppermute(send, "col", pair))
    pieces = hops(pieces, "row", rows)
    parts, _ = lax.optimization_barrier((parts, totals[0]))
    totals = hops(totals, "col", cols, 2)
    factor, band_block = compact_factor(parts, first_inv, second_upper, first_upper)
    totals, factor = lax.optimization_barrier((totals, factor))
    mine, both = sum_pieces(totals, pieces, piece)
    both = hops([both] * rows, "row", rows)
    mine = merge(place, hops([mine] * chips, "col", cols, 2))
    other = lax.ppermute(mine, "col", pair)
    coupling = sum_gather(cols, (both, share, share + strip))
    updated = update(place, hamiltonian, left, mine, other, right, factor, coupling, both)
    return (updated, band_block)


def solution(mesh):
    in_specs = (P("row", "col"), P("row", None))
    out_specs = (P("row", "col"), P())
    body = functools.partial(shards, mesh.shape["row"], mesh.shape["col"])
    return jax.shard_map(body, mesh=mesh, in_specs=in_specs, out_specs=out_specs, check_vma=False)
```
